32 devices in a mesh: group: 2 (over x), hst: 8 (over z, y), cores: 2 (over core).
Axes of the slice: x: 2, y: 2, z: 4, core: 2. Of those that a mesh axis runs over, the one named last changes fastest.
Arguments:
- observations: bfloat16 [512, 16, 512], P(('group', 'hst', 'cores')), parts along dimension 0, may hold values from -20 to 20
- lengths: int32 [512], P(('group', 'hst', 'cores')), parts along dimension 0, may hold values from 1 to 16, as said below
- actions: int32 [512, 16], P(('group', 'hst', 'cores')), parts along dimension 0, may hold values from 0 to 127
- rewards: float32 [512, 16], P(('group', 'hst', 'cores')), parts along dimension 0, may hold values from -6 to 6
- assign: int32 [512], P(('group', 'hst', 'cores')), parts along dimension 0, may hold values from 0 to 15, as said below
- actor_embed: bfloat16 [1024, 1024], P('group'), parts along dimension 0, may hold values from -0.25 to 0.25
- actor_policy: bfloat16 [2048, 128], P('group'), parts along dimension 0, may hold values from -1 to 1
- master_embed: float32 [1024, 1024], P('group'), parts along dimension 0, may hold values from -0.25 to 0.25
- master_policy: float32 [2048, 128], P('group'), parts along dimension 0, may hold values from -1 to 1
- master_value: float32 [2048], P('group'), parts along dimension 0, may hold values from -0.1875 to 0.1875
- embed_moment: float32 [1024, 1024], P('group'), parts along dimension 0, may hold values from -0.15625 to 0.15625
- policy_moment: float32 [2048, 128], P('group'), parts along dimension 0, may hold values from -0.15625 to 0.15625
- value_moment: float32 [2048], P('group'), parts along dimension 0, may hold values from -0.15625 to 0.15625
- next_obs: bfloat16 [8192, 512], P(('group', 'hst', 'cores')), parts along dimension 0, may hold values from -6 to 6
Outputs:
- next_logits: bfloat16 [8192, 128], P(('group', 'hst', 'cores')), parts along dimension 0
- new_embed: float32 [1024, 1024], P('group'), parts along dimension 0
- new_policy: float32 [2048, 128], P('group'), parts along dimension 0
- new_value: float32 [2048], P('group'), parts along dimension 0
- new_embed_moment: float32 [1024, 1024], P('group'), parts along dimension 0
- new_policy_moment: float32 [2048, 128], P('group'), parts along dimension 0
- new_value_moment: float32 [2048], P('group'), parts along dimension 0
The draws below stay inside these ranges and needn't reach their ends.
There are 2 independent parts, one for each index of `group`. The reference program is written for one: setup_inputs(seed, part) draws one part's arguments, and reference() takes and returns one part's arrays. A program takes and returns all parts, laid end to end along the dimension named above; each array names one. Nothing has to cross between parts.
Inputs may be any that keep to these rules, and one draw needn't show every extreme that they name: `lengths`: valid steps of a trajectory; 16 is reached in every draw. `assign`: within each aligned block of 16 trajectories (one actor device), every learner index is named exactly 1 times.
All inputs are finite; a program needn't handle non-finite values.
Results may differ from the reference program's by a relative error of at most 0.006.
The reference program's roundings to bfloat16 on the way (of `hidden`, `grad_logits` and `grad_preact`) count: a program that leaves them out, or rounds other values in their place, can miss the bound.
Values may be sent and summed in bfloat16 or wider, within the bound.
No kernel may reach another device: no remote copies, remote signals or barrier semaphores. Data moves between devices by JAX's collectives and lax.ppermute only.
A program may use at most 64 MiB of HBM per device.

```python
import jax
import jax.numpy as jnp
from jax import lax

D = 1024
OBS = 512
NACT = 128
SLOT = 16
PER = 1
TRAJ_DEV = 16
NTRAJ = 256
NEXT = 4096
N_HST = 8
N_CORES = 2


def draw_observations(key, part):
    key = jax.random.fold_in(key, 11)
    key_base = jax.random.fold_in(key, 0)
    full_shape = (NTRAJ, SLOT, OBS)
    values = jnp.clip(jax.random.normal(key_base, full_shape, jnp.float32), -6.0, 6.0)
    return values.astype(jnp.bfloat16)


def draw_lengths(key, part):
    key = jax.random.fold_in(key, 12)
    key_top, key_len = jax.random.split(key, 2)
    blocks = NTRAJ // TRAJ_DEV
    ceiling = jax.random.randint(key_top, (blocks, 1), max(SLOT // 4, 1), SLOT + 1)
    drawn = jax.random.randint(key_len, (blocks, TRAJ_DEV), 1, ceiling + 1)
    drawn = drawn.at[0, 0].set(SLOT)
    return drawn.reshape(NTRAJ).astype(jnp.int32)


def draw_assign(key, part):
    key = jax.random.fold_in(key, 13)
    blocks = NTRAJ // TRAJ_DEV
    learners = TRAJ_DEV // PER
    keys_all = jax.random.split(key, blocks)
    orders = jax.vmap(lambda single: jax.random.permutation(single, TRAJ_DEV))(keys_all)
    return (orders % learners).astype(jnp.int32).reshape(NTRAJ)


def with_ends(array, stream_key, least, largest):
    shape = array.shape
    index_at = [jax.random.randint(jax.random.fold_in(stream_key, axis), (), 0, shape[axis]) for axis in range(len(shape))]
    array = array.at[tuple(index_at)].set(least)
    longest = shape.index(max(shape))
    index_at[longest] = (index_at[longest] + 1) % shape[longest]
    return array.at[tuple(index_at)].set(largest)


def block_levels(rng, extent, cuts, least, largest):
    def one(dim, shards_of):
        heights = jax.random.uniform(jax.random.fold_in(jax.random.fold_in(rng, 6), dim), (shards_of,), jnp.float32, least / len(cuts), largest / len(cuts))
        return jnp.repeat(jnp.exp(heights), extent[dim] // shards_of).reshape((-1,) + (1,) * (len(extent) - dim - 1))

    loudness = one(*cuts[0])
    for cut in cuts[1:]:
        loudness = loudness * one(*cut)
    return loudness


def normal_values(stream_key, extent, width, limit, cuts=(), held_as=jnp.bfloat16):
    entries = jax.random.normal(stream_key, extent, jnp.float32) * width
    if len(cuts) > 0:
        entries = block_levels(stream_key, extent, cuts, -0.22, 0.18) * entries
    return jnp.clip(entries, min=-limit, max=limit).astype(held_as)


def setup_inputs(seed: int = 0, part: int = 0) -> dict:
    seeds = jax.random.split(jax.random.key(seed), 15)
    part_splits = jax.random.split(jax.random.fold_in(seeds[14], part), 15)
    return {
        "observations": draw_observations(jax.random.fold_in(jax.random.fold_in(seeds[14], part), 71), part),
        "lengths": draw_lengths(jax.random.fold_in(jax.random.fold_in(seeds[14], part), 71), part),
        "actions": with_ends(jax.random.randint(part_splits[2], (NTRAJ, SLOT), 0, NACT), jax.random.fold_in(part_splits[2], 1), 0, NACT - 1).astype(jnp.int32),
        "rewards": normal_values(part_splits[3], (NTRAJ, SLOT), 1.0, 6.0, ((0, 16),), jnp.float32),
        "assign": draw_assign(jax.random.fold_in(jax.random.fold_in(seeds[14], part), 71), part),
        "actor_embed": normal_values(part_splits[5], (OBS, D), OBS ** -0.5, 0.25),
        "actor_policy": normal_values(part_splits[6], (D, NACT), (D // 32) ** -0.5, 1.0),
        "master_embed": normal_values(part_splits[7], (OBS, D), OBS ** -0.5, 0.25, (), jnp.float32),
        "master_policy": normal_values(part_splits[8], (D, NACT), (D // 32) ** -0.5, 1.0, (), jnp.float32),
        "master_value": normal_values(part_splits[9], (D,), D ** -0.5, 0.1875, (), jnp.float32),
        "embed_moment": normal_values(part_splits[10], (OBS, D), 0.01, 0.15625, (), jnp.float32),
        "policy_moment": normal_values(part_splits[11], (D, NACT), 0.01, 0.15625, (), jnp.float32),
        "value_moment": normal_values(part_splits[12], (D,), 0.01, 0.15625, (), jnp.float32),
        "next_obs": normal_values(part_splits[13], (NEXT, OBS), 1.0, 6.0, ((0, 16),)),
    }


GAMMA = 0.99
ENTROPY_COEF = 0.1
MOMENTUM = 0.9
LEARN_RATE = 0.05


def torso(frames, embed, policy):
    preact = jnp.dot(frames, embed, preferred_element_type=jnp.float32)
    hidden = jnp.maximum(preact, 0.0).astype(jnp.bfloat16)
    logits = jnp.dot(hidden, policy, preferred_element_type=jnp.float32)
    return preact, hidden, logits


def chosen(logprob, actions):
    labels = jnp.arange(logprob.shape[-1]).astype(actions.dtype)
    onehot = labels[None, :] == actions[:, None]
    return onehot, jnp.sum(jnp.where(onehot, logprob, 0.0), axis=-1)


def behaviour(observations, actions, embed, policy):
    traj_count, slot_count, feat_count = observations.shape
    preact, hidden, logits = torso(observations.reshape(traj_count * slot_count, feat_count), embed, policy)
    logprob = jax.nn.log_softmax(logits, axis=-1)
    onehot, taken = chosen(logprob, actions.reshape(-1))
    return taken.reshape(traj_count, slot_count)


def learner_grads(observations, actions, rewards, lengths, behave, weight, embed, policy, value_head):
    traj_count, slot_count, feat_count = observations.shape
    frames = observations.reshape(traj_count * slot_count, feat_count)
    preact, hidden, logits = torso(frames, embed, policy)
    values = jnp.dot(hidden, value_head, preferred_element_type=jnp.float32).reshape(traj_count, slot_count)
    logprob = jax.nn.log_softmax(logits, axis=-1)
    onehot, taken = chosen(logprob, actions.reshape(-1))
    probs = jnp.exp(logprob)
    entropy = -jnp.sum(probs * logprob, axis=-1)
    positions = jnp.arange(slot_count).astype(lengths.dtype)
    inside = (positions[None, :] < lengths[:, None]).astype(jnp.float32)
    beyond = (positions[None, :] + 1 < lengths[:, None]).astype(jnp.float32)
    ratios = jnp.minimum(1.0, jnp.exp(taken.reshape(traj_count, slot_count) - behave))

    def shifted(series):
        return jnp.concatenate([series[:, 1:], jnp.zeros((traj_count, 1), jnp.float32)], axis=1) * beyond

    deltas = inside * ratios * (rewards + GAMMA * shifted(values) - values)

    def backward_step(carry_sum, inputs):
        delta_now, ratio_now, inside_now = inputs
        carry_sum = inside_now * (delta_now + GAMMA * ratio_now * carry_sum)
        return carry_sum, carry_sum

    last_sum, corrections = lax.scan(backward_step, jnp.zeros((traj_count,), jnp.float32),
                                     (deltas.T, ratios.T, inside.T), reverse=True)
    targets = values + corrections.T
    advantage = ratios * (rewards + GAMMA * shifted(targets) - values)
    scale = (weight[:, None] * inside).reshape(-1)
    grad_logits = (scale[:, None] * (-advantage.reshape(-1)[:, None] * (onehot.astype(jnp.float32) - probs)
                                     + ENTROPY_COEF * probs * (logprob + entropy[:, None]))).astype(jnp.bfloat16)
    grad_values = (scale * (values - targets).reshape(-1)).astype(jnp.bfloat16)
    grad_policy = jnp.dot(hidden.T, grad_logits, preferred_element_type=jnp.float32)
    grad_value = jnp.dot(grad_values, hidden, preferred_element_type=jnp.float32)
    grad_hidden = jnp.dot(grad_logits, policy.T, preferred_element_type=jnp.float32) \
        + grad_values.astype(jnp.float32)[:, None] * value_head.astype(jnp.float32)[None, :]
    grad_preact = jnp.where(preact > 0.0, grad_hidden, 0.0).astype(jnp.bfloat16)
    grad_embed = jnp.dot(frames.T, grad_preact, preferred_element_type=jnp.float32)
    return grad_embed, grad_policy, grad_value


def reference(observations, lengths, actions, rewards, assign, actor_embed, actor_policy, master_embed,
              master_policy, master_value, embed_moment, policy_moment, value_moment, next_obs):
    learners = N_HST * N_CORES
    blocks = NTRAJ // TRAJ_DEV
    embed = master_embed.astype(jnp.bfloat16)
    policy = master_policy.astype(jnp.bfloat16)
    value_head = master_value.astype(jnp.bfloat16)
    onehot = (assign[:, None] == jnp.arange(learners).astype(jnp.int32)[None, :]).astype(jnp.float32)
    totals = jnp.sum(onehot * lengths[:, None].astype(jnp.float32), axis=0)
    weight = 1.0 / (learners * jnp.sum(onehot * totals[None, :], axis=1))

    def per_block(carry, inputs):
        block_obs, block_len, block_act, block_rew, block_weight = inputs
        behave = behaviour(block_obs, block_act, actor_embed, actor_policy)
        grads = learner_grads(block_obs, block_act, block_rew, block_len, behave, block_weight,
                              embed, policy, value_head)
        return jax.tree.map(jnp.add, carry, grads), None

    inputs = (observations.reshape(blocks, TRAJ_DEV, SLOT, OBS), lengths.reshape(blocks, TRAJ_DEV),
              actions.reshape(blocks, TRAJ_DEV, SLOT), rewards.reshape(blocks, TRAJ_DEV, SLOT),
              weight.reshape(blocks, TRAJ_DEV))
    start = (jnp.zeros((OBS, D), jnp.float32), jnp.zeros((D, NACT), jnp.float32), jnp.zeros((D,), jnp.float32))
    (grad_embed, grad_policy, grad_value), unused = lax.scan(per_block, start, inputs)
    new_embed_moment = MOMENTUM * embed_moment + grad_embed
    new_policy_moment = MOMENTUM * policy_moment + grad_policy
    new_value_moment = MOMENTUM * value_moment + grad_value
    new_embed = master_embed - LEARN_RATE * new_embed_moment
    new_policy = master_policy - LEARN_RATE * new_policy_moment
    new_value = master_value - LEARN_RATE * new_value_moment
    preact, hidden, logits = torso(next_obs, new_embed.astype(jnp.bfloat16), new_policy.astype(jnp.bfloat16))
    next_logits = logits.astype(jnp.bfloat16)
    return (next_logits, new_embed, new_policy, new_value, new_embed_moment, new_policy_moment, new_value_moment)
```

```python
import functools

import jax
import jax.numpy as jnp
from jax import lax
from jax.experimental import pallas as pl
from jax.experimental.pallas import tpu as pltpu
from jax.sharding import PartitionSpec as P

GAMMA = 0.99
ENTROPY_COEF = 0.1
MOMENTUM = 0.9
LEARN_RATE = 0.05
AXES = ("hst", "cores")
F32 = jnp.float32
BF16 = jnp.bfloat16
VMEM = pl.BlockSpec(memory_space=pltpu.VMEM)
PARAMS = pltpu.CompilerParams(vmem_limit_bytes=56 * 2**20)
BEHAVE, ACTION, REWARD, LENGTH, ASSIGN = range(5)


def iota(shape, dim):
    return lax.broadcasted_iota(jnp.int32, shape, dim)


def mm(a, b):
    return jnp.dot(a, b, preferred_element_type=F32)


def actor_kernel(
    obs, lengths, assign, actions, rewards, actor_embed, actor_policy,
    master_embed, master_policy, master_value, side, embed, head, head_t,
):
    rows = obs.shape[0]
    traj, slots = actions.shape
    spread = (lax.rem(iota((slots, rows), 1), slots) == iota((slots, rows), 0)).astype(F32)
    owner = lax.div(iota((traj, rows), 1), slots) == iota((traj, rows), 0)

    def flat(series):
        wide = jnp.dot(series, spread, precision=lax.Precision.HIGHEST, preferred_element_type=F32)
        return jnp.sum(jnp.where(owner, wide, 0.0), axis=0, keepdims=True)

    def repeat(series):
        return jnp.dot(
            series.astype(F32), owner.astype(F32),
            precision=lax.Precision.HIGHEST, preferred_element_type=F32,
        )

    action = flat(actions[...].astype(F32))
    hidden = jnp.maximum(mm(obs[...], actor_embed[...]), 0.0).astype(BF16)
    logits = mm(hidden, actor_policy[...]).T
    top = jnp.max(logits, axis=0, keepdims=True)
    shifted = logits - top
    norm = jnp.log(jnp.sum(jnp.exp(shifted), axis=0, keepdims=True))
    onehot = iota(logits.shape, 0) == action.astype(jnp.int32)
    side[...] = jnp.zeros_like(side)
    side[BEHAVE : BEHAVE + 1, :] = (
        jnp.sum(jnp.where(onehot, shifted, 0.0), axis=0, keepdims=True) - norm
    )
    side[ACTION : ACTION + 1, :] = action
    side[REWARD : REWARD + 1, :] = flat(rewards[...])
    side[LENGTH : LENGTH + 1, :] = repeat(lengths[...])
    side[ASSIGN : ASSIGN + 1, :] = repeat(assign[...])
    embed[...] = master_embed[...].astype(BF16)
    nact = master_policy.shape[1]
    wide = jnp.concatenate(
        [
            master_policy[...].T,
            master_value[...],
            jnp.zeros((head_t.shape[0] - nact - 1, head_t.shape[1]), F32),
        ],
        axis=0,
    )
    head_t[...] = wide.astype(BF16)
    head[...] = wide.T.astype(BF16)


def actor(slots, obs, lengths, assign, actions, rewards, *weights):
    feats, width = weights[0].shape
    nact = weights[1].shape[1]
    return pl.pallas_call(
        actor_kernel,
        out_shape=(
            jax.ShapeDtypeStruct((8, obs.shape[0]), F32),
            jax.ShapeDtypeStruct((feats, width), BF16),
            jax.ShapeDtypeStruct((width, 2 * nact), BF16),
            jax.ShapeDtypeStruct((2 * nact, width), BF16),
        ),
        in_specs=[VMEM] * 10,
        out_specs=(VMEM,) * 4,
        compiler_params=PARAMS,
        name="actor",
    )(obs, lengths, assign, actions, rewards, *weights)


def weight_kernel(slots, sides, out):
    learners = out.shape[0]
    rows = sides.shape[2]
    total = jnp.zeros((learners, rows), F32)
    first = lax.rem(iota((1, rows), 1), slots) == 0
    for index in range(sides.shape[0]):
        assign = sides[index, ASSIGN : ASSIGN + 1, :].astype(jnp.int32)
        length = jnp.where(first, sides[index, LENGTH : LENGTH + 1, :], 0.0)
        total = total + jnp.where(iota((learners, rows), 0) == assign, length, 0.0)
    summed = jnp.sum(total, axis=1, keepdims=True)
    out[...] = jnp.broadcast_to(1.0 / (learners * summed), out.shape)


def weights_of(slots, learners, sides):
    return pl.pallas_call(
        functools.partial(weight_kernel, slots),
        out_shape=jax.ShapeDtypeStruct((learners, 128), F32),
        in_specs=[VMEM],
        out_specs=VMEM,
        compiler_params=PARAMS,
        name="weights",
    )(sides)


def learner_kernel(slots, nact, frames, sides, weights, embed, head, head_t, grads, hidden, logits_t, grad_t):
    blocks, rows = frames.shape[0], frames.shape[1]
    feats, width = embed.shape
    total = blocks * rows

    def forward(index, carry):
        here = pl.ds(pl.multiple_of(index * rows, rows), rows)
        hid = jnp.maximum(mm(frames[index], embed[...]), 0.0).astype(BF16)
        hidden[here, :] = hid
        logits_t[index] = mm(hid, head[...]).T
        return carry

    lax.fori_loop(0, blocks, forward, 0)

    def vtrace(index, carry):
        side = sides[index]
        logits = logits_t[index, 0:nact, :]
        values = logits_t[index, nact : nact + 1, :]
        behave = side[BEHAVE : BEHAVE + 1, :]
        reward = side[REWARD : REWARD + 1, :]
        length = side[LENGTH : LENGTH + 1, :].astype(jnp.int32)
        assign = side[ASSIGN : ASSIGN + 1, :].astype(jnp.int32)
        action = side[ACTION : ACTION + 1, :].astype(jnp.int32)
        learners = weights.shape[0]
        weight = jnp.sum(
            jnp.where(iota((learners, rows), 0) == assign, weights[:, 0:1], 0.0),
            axis=0, keepdims=True,
        )
        top = jnp.max(logits, axis=0, keepdims=True)
        exps = jnp.exp(logits - top)
        norm = jnp.sum(exps, axis=0, keepdims=True)
        logprob = logits - (top + jnp.log(norm))
        probs = exps * (1.0 / norm)
        onehot = iota(logits.shape, 0) == action
        taken = jnp.sum(jnp.where(onehot, logprob, 0.0), axis=0, keepdims=True)
        entropy = -jnp.sum(probs * logprob, axis=0, keepdims=True)
        step = lax.rem(iota((1, rows), 1), slots)
        inside = (step < length).astype(F32)
        beyond = (step + 1 < length).astype(F32)
        ratios = jnp.minimum(1.0, jnp.exp(taken - behave))

        def later(series, by):
            return pltpu.roll(series, rows - by, 1)

        deltas = inside * ratios * (reward + GAMMA * later(values, 1) * beyond - values)
        decay = GAMMA * ratios * inside
        corrections = deltas
        reach = 1
        while reach < slots:
            within = step + reach < slots
            corrections = corrections + decay * jnp.where(within, later(corrections, reach), 0.0)
            decay = decay * jnp.where(within, later(decay, reach), 0.0)
            reach *= 2
        targets = values + corrections
        advantage = ratios * (reward + GAMMA * later(targets, 1) * beyond - values)
        scale = weight * inside
        grad = scale * (
            -advantage * (onehot.astype(F32) - probs) + ENTROPY_COEF * probs * (logprob + entropy)
        )
        pad = jnp.zeros((head_t.shape[0] - nact - 1, rows), F32)
        grad_t[index] = jnp.concatenate([grad, scale * (values - targets), pad], axis=0)
        return carry

    lax.fori_loop(0, blocks, vtrace, 0)
    grads[...] = jnp.zeros_like(grads)

    def backward(index, carry):
        here = pl.ds(pl.multiple_of(index * rows, rows), rows)
        hid = hidden[here, :]
        wide_t = grad_t[index]
        back = mm(wide_t.T.astype(BF16), head_t[...])
        grad_preact = jnp.where(hid.astype(F32) > 0.0, back, 0.0).astype(BF16)
        grads[0:feats, :] += lax.dot_general(
            frames[index], grad_preact, (((0,), (0,)), ((), ())), preferred_element_type=F32
        )
        tail = grads.shape[0] - feats
        grads[feats:, :] += mm(wide_t[0:tail, :].astype(BF16), hid)
        return carry

    lax.fori_loop(0, blocks, backward, 0)


def learner(slots, nact, frames, sides, weights, embed, head, head_t):
    blocks, rows = frames.shape[0], frames.shape[1]
    feats, width = embed.shape
    wide = head.shape[1]
    return pl.pallas_call(
        functools.partial(learner_kernel, slots, nact),
        out_shape=jax.ShapeDtypeStruct((feats + nact + 16, width), F32),
        in_specs=[VMEM] * 6,
        out_specs=VMEM,
        scratch_shapes=[
            pltpu.VMEM((blocks * rows, width), BF16),
            pltpu.VMEM((blocks, wide, rows), F32),
            pltpu.VMEM((blocks, wide, rows), F32),
        ],
        compiler_params=PARAMS,
        name="learner",
    )(frames, sides, weights, embed, head, head_t)


def update_kernel(
    feats, nact, mine, theirs, master_embed, master_policy, master_value,
    embed_moment, policy_moment, value_moment, next_obs,
    next_logits, new_embed, new_policy, new_value, new_em, new_pm, new_vm,
):
    def step(grad, moment, master, new_moment, new_master):
        held = MOMENTUM * moment[...] + grad
        new_moment[...] = held
        fresh = master[...] - LEARN_RATE * held
        new_master[...] = fresh
        return fresh

    def grad(start, size):
        return mine[start : start + size, :].astype(F32) + theirs[start : start + size, :].astype(F32)

    embed = step(grad(0, feats), embed_moment, master_embed, new_em, new_embed)
    hidden = jnp.maximum(mm(next_obs[...], embed.astype(BF16)), 0.0).astype(BF16)
    policy = step(grad(feats, nact).T, policy_moment, master_policy, new_pm, new_policy)
    step(grad(feats + nact, 16)[0:1, :], value_moment, master_value, new_vm, new_value)
    next_logits[...] = mm(hidden, policy.astype(BF16)).astype(BF16)


def update(mine, theirs, *args):
    embed, policy, value = args[0], args[1], args[2]
    next_obs = args[6]
    feats, nact = embed.shape[0], policy.shape[1]
    shapes = [jax.ShapeDtypeStruct(array.shape, F32) for array in (embed, policy, value)]
    return pl.pallas_call(
        functools.partial(update_kernel, feats, nact),
        out_shape=(jax.ShapeDtypeStruct((next_obs.shape[0], nact), BF16), *shapes, *shapes),
        in_specs=[VMEM] * 9,
        out_specs=(VMEM,) * 7,
        compiler_params=PARAMS,
        name="update",
    )(mine, theirs, *args)


def body(
    n_hst, n_cores, observations, lengths, actions, rewards, assign, actor_embed, actor_policy,
    master_embed, master_policy, master_value, embed_moment, policy_moment, value_moment, next_obs,
):
    traj, slots, feats = observations.shape
    nact = master_policy.shape[1]
    learners = n_hst * n_cores
    rows = traj * slots
    own = observations.reshape(rows, feats)
    value_row = master_value.reshape(1, -1)
    gather = n_hst <= 8
    if gather:
        frames = lax.all_gather(own, "hst")
    else:
        frames = own[None]
    side, embed, head, head_t = actor(
        slots, own, lengths.reshape(1, -1), assign.reshape(1, -1), actions, rewards,
        actor_embed, actor_policy, master_embed, master_policy, value_row,
    )
    if gather:
        sides = lax.all_gather(side, AXES)
        weights = weights_of(slots, learners, sides)
        core = lax.axis_index("cores")
        ours = lax.dynamic_index_in_dim(
            sides.reshape(n_hst, n_cores, *side.shape), core, axis=1, keepdims=False
        )
    else:
        named = (assign[:, None] == jnp.arange(learners)[None, :]).astype(F32)
        totals = lax.psum(jnp.sum(named * lengths[:, None].astype(F32), axis=0), AXES)
        weights = jnp.broadcast_to((1.0 / (learners * totals))[:, None], (learners, 128))
        ours = side[None]
    grads = learner(slots, nact, frames, ours, weights, embed, head, head_t)
    if gather:
        mine = grads.astype(BF16)
        theirs = lax.ppermute(mine, "cores", [(i, i ^ 1) for i in range(n_cores)])
    else:
        mine = lax.psum(grads, AXES)
        theirs = jnp.zeros_like(mine)
    outs = update(
        mine, theirs, master_embed, master_policy, value_row, embed_moment, policy_moment,
        value_moment.reshape(1, -1), next_obs,
    )
    logits, new_embed, new_policy, new_value, new_em, new_pm, new_vm = outs
    return logits, new_embed, new_policy, new_value.reshape(-1), new_em, new_pm, new_vm.reshape(-1)


def solution(mesh):
    split = P(("group", "hst", "cores"))
    whole = P("group")
    return jax.shard_map(
        functools.partial(body, mesh.shape["hst"], mesh.shape["cores"]),
        mesh=mesh,
        in_specs=(split,) * 5 + (whole,) * 8 + (split,),
        out_specs=(split,) + (whole,) * 6,
        check_vma=False,
    )
```

```python
import functools

import jax
import jax.numpy as jnp
from jax import lax
from jax.experimental import pallas as pl
from jax.experimental.pallas import tpu as pltpu
from jax.sharding import PartitionSpec as P

GAMMA = 0.99
ENTROPY_COEF = 0.1
MOMENTUM = 0.9
LEARN_RATE = 0.05
AXES = ("hst", "cores")
F32 = jnp.float32
BF16 = jnp.bfloat16
VMEM = pl.BlockSpec(memory_space=pltpu.VMEM)
MIB = 2**20
BLOCK = 256
PAD = 16
BEHAVE, ACTION, REWARD, LENGTH, ASSIGN = range(5)


def iota(shape, dim):
    return lax.broadcasted_iota(jnp.int32, shape, dim)


def mm(a, b):
    return jnp.dot(a, b, preferred_element_type=F32)


def mm_nt(a, b):
    return lax.dot_general(a, b, (((1,), (1,)), ((), ())), preferred_element_type=F32)


def params(mib):
    return pltpu.CompilerParams(vmem_limit_bytes=mib * MIB)


def actor_kernel(obs, lengths, assign, actions, rewards, actor_embed, actor_policy, side):
    rows = obs.shape[0]
    traj, slots = actions.shape
    spread = (lax.rem(iota((slots, rows), 1), slots) == iota((slots, rows), 0)).astype(F32)
    owner = lax.div(iota((traj, rows), 1), slots) == iota((traj, rows), 0)

    def flat(series):
        wide = jnp.dot(series, spread, precision=lax.Precision.HIGHEST, preferred_element_type=F32)
        return jnp.sum(jnp.where(owner, wide, 0.0), axis=0, keepdims=True)

    def repeat(series):
        return jnp.dot(
            series.astype(F32), owner.astype(F32),
            precision=lax.Precision.HIGHEST, preferred_element_type=F32,
        )

    action = flat(actions[...].astype(F32))
    hidden = jnp.maximum(mm(obs[...], actor_embed[...]), 0.0).astype(BF16)
    logits = mm(hidden, actor_policy[...]).T
    top = jnp.max(logits, axis=0, keepdims=True)
    shifted = logits - top
    norm = jnp.log(jnp.sum(jnp.exp(shifted), axis=0, keepdims=True))
    onehot = iota(logits.shape, 0) == action.astype(jnp.int32)
    side[...] = jnp.zeros_like(side)
    side[BEHAVE : BEHAVE + 1, :] = (
        jnp.sum(jnp.where(onehot, shifted, 0.0), axis=0, keepdims=True) - norm
    )
    side[ACTION : ACTION + 1, :] = action
    side[REWARD : REWARD + 1, :] = flat(rewards[...])
    side[LENGTH : LENGTH + 1, :] = repeat(lengths[...])
    side[ASSIGN : ASSIGN + 1, :] = repeat(assign[...])


def actor(obs, *args):
    return pl.pallas_call(
        actor_kernel,
        out_shape=jax.ShapeDtypeStruct((8, obs.shape[0]), F32),
        in_specs=[VMEM] * 7,
        out_specs=VMEM,
        compiler_params=params(12),
        name="actor",
    )(obs, *args)


def prepare_kernel(master_embed, master_policy, master_value, embed_t, head, head_t):
    embed_t[...] = master_embed[...].T.astype(BF16)
    nact = master_policy.shape[1]
    wide = jnp.concatenate(
        [
            master_policy[...].T,
            master_value[...],
            jnp.zeros((PAD - 1, head_t.shape[1]), F32),
        ],
        axis=0,
    )
    head_t[...] = wide.astype(BF16)
    head[:, 0:nact] = master_policy[...].astype(BF16)
    head[:, nact:] = wide[nact:, :].T.astype(BF16)


def prepare(master_embed, master_policy, master_value):
    feats, width = master_embed.shape
    nact = master_policy.shape[1]
    return pl.pallas_call(
        prepare_kernel,
        out_shape=(
            jax.ShapeDtypeStruct((width, feats), BF16),
            jax.ShapeDtypeStruct((width, nact + PAD), BF16),
            jax.ShapeDtypeStruct((nact + PAD, width), BF16),
        ),
        in_specs=[VMEM] * 3,
        out_specs=(VMEM,) * 3,
        compiler_params=params(12),
        name="prepare",
    )(master_embed, master_policy, master_value)


def learner_weights(slots, sides, out):
    learners, rows = out.shape[0], sides[0].shape[1]
    total = jnp.zeros((learners, rows), F32)
    first = lax.rem(iota((1, rows), 1), slots) == 0
    for side in sides:
        assign = side[ASSIGN : ASSIGN + 1, :].astype(jnp.int32)
        length = jnp.where(first, side[LENGTH : LENGTH + 1, :], 0.0)
        total = total + jnp.where(iota((learners, rows), 0) == assign, length, 0.0)
    summed = jnp.sum(total, axis=1, keepdims=True)
    out[...] = jnp.broadcast_to(1.0 / (learners * summed), out.shape)


def vtrace(slots, nact, side, weights, logits, values):
    rows = logits.shape[1]
    learners = weights.shape[0]
    behave = side[BEHAVE : BEHAVE + 1, :]
    reward = side[REWARD : REWARD + 1, :]
    length = side[LENGTH : LENGTH + 1, :].astype(jnp.int32)
    assign = side[ASSIGN : ASSIGN + 1, :].astype(jnp.int32)
    action = side[ACTION : ACTION + 1, :].astype(jnp.int32)
    weight = jnp.sum(
        jnp.where(iota((learners, rows), 0) == assign, weights[:, 0:1], 0.0), axis=0, keepdims=True
    )
    top = jnp.max(logits, axis=0, keepdims=True)
    exps = jnp.exp(logits - top)
    norm = jnp.sum(exps, axis=0, keepdims=True)
    logprob = logits - (top + jnp.log(norm))
    probs = exps * (1.0 / norm)
    onehot = iota(logits.shape, 0) == action
    taken = jnp.sum(jnp.where(onehot, logprob, 0.0), axis=0, keepdims=True)
    entropy = -jnp.sum(probs * logprob, axis=0, keepdims=True)
    step = lax.rem(iota((1, rows), 1), slots)
    inside = (step < length).astype(F32)
    beyond = (step + 1 < length).astype(F32)
    ratios = jnp.minimum(1.0, jnp.exp(taken - behave))

    def later(series, by):
        return pltpu.roll(series, rows - by, 1)

    deltas = inside * ratios * (reward + GAMMA * later(values, 1) * beyond - values)
    decay = GAMMA * ratios * inside
    corrections = deltas
    reach = 1
    while reach < slots:
        within = step + reach < slots
        corrections = corrections + decay * jnp.where(within, later(corrections, reach), 0.0)
        decay = decay * jnp.where(within, later(decay, reach), 0.0)
        reach *= 2
    targets = values + corrections
    advantage = ratios * (reward + GAMMA * later(targets, 1) * beyond - values)
    scale = weight * inside
    grad = scale * (
        -advantage * (onehot.astype(F32) - probs) + ENTROPY_COEF * probs * (logprob + entropy)
    )
    return grad, scale * (values - targets)


def work(slots, frames, side, weights, embed_t, head, head_t, frames_t, hidden_t, preact_t, add):
    width, feats = embed_t.shape
    nact = head_t.shape[0] - PAD
    tile = 256
    for index, block in enumerate(frames):
        frames_t[:, index * BLOCK : (index + 1) * BLOCK] = block.T
    for start in range(0, width, tile):
        here = slice(start, start + tile)
        hidden_t[here, :] = jnp.maximum(mm(embed_t[here, :], frames_t[...]), 0.0).astype(BF16)
    logits = mm(head_t[...], hidden_t[...])
    grad, grad_values = vtrace(
        slots, nact, side, weights, logits[0:nact, :], logits[nact : nact + 1, :]
    )
    pad = jnp.zeros((PAD - 1, grad.shape[1]), F32)
    grad_t = jnp.concatenate([grad, grad_values, pad], axis=0).astype(BF16)
    for start in range(0, width, tile):
        here = slice(start, start + tile)
        back = mm(head[here, :], grad_t)
        alive = hidden_t[here, :].astype(F32) > 0.0
        preact_t[here, :] = jnp.where(alive, back, 0.0).astype(BF16)
    for index in range(len(frames)):
        lanes = slice(index * BLOCK, (index + 1) * BLOCK)
        add(index, slice(0, feats), mm_nt(frames_t[:, lanes], preact_t[:, lanes]))
        add(index, slice(feats, feats + nact + PAD), mm_nt(grad_t[:, lanes], hidden_t[:, lanes]))


def on_mid():
    line = lax.div(lax.axis_index("hst"), 2)
    return jnp.logical_or(line == 1, line == 2)


def choose(mid, end):
    return jnp.where(on_mid(), mid[...], end[...])


def first_kernel(slots, *refs):
    (own, pair, near, *sides), (embed_t, head, head_t), (out, other, weights), scratch = (
        refs[0:19], refs[19:22], refs[22:25], refs[25:28])
    learner_weights(slots, sides, weights)
    outs = (out, out, other)

    def add(index, rows, value):
        if index == 1:
            outs[index][rows, :] += value
        else:
            outs[index][rows, :] = value

    side = jnp.concatenate([sides[0][...], sides[2][...], sides[4][...]], axis=1)
    work(slots, (own[...], pair[...], near[...]), side, weights, embed_t, head, head_t, *scratch, add)


def second_kernel(slots, *refs):
    (cross, mid, end, side_cross, side_mid, side_end, weights, partial, other) = refs[0:9]
    (embed_t, head, head_t), (out, far), scratch = refs[9:12], refs[12:14], refs[14:17]

    def add(index, rows, value):
        if index == 0:
            out[rows, :] = partial[rows, :] + (other[rows, :] + value)
        else:
            far[rows, :] = value

    side = jnp.concatenate([side_cross[...], choose(side_mid, side_end)], axis=1)
    work(
        slots, (cross[...], mid[...] + end[...]), side, weights, embed_t, head, head_t, *scratch, add
    )


def third_kernel(slots, *refs):
    (mid_a, end_a, mid_b, end_b, smid_a, send_a, smid_b, send_b, weights, far) = refs[0:10]
    (embed_t, head, head_t), (out, last), scratch = refs[10:13], refs[13:15], refs[15:18]

    def add(index, rows, value):
        if index == 0:
            out[rows, :] = far[rows, :] + value
        else:
            last[rows, :] = value

    side = jnp.concatenate([choose(smid_a, send_a), choose(smid_b, send_b)], axis=1)
    work(
        slots, (mid_a[...] + end_a[...], mid_b[...] + end_b[...]), side, weights,
        embed_t, head, head_t, *scratch, add,
    )


def fourth_kernel(slots, *refs):
    (mid, end, side_mid, side_end, weights, half, far, last) = refs[0:8]
    (embed_t, head, head_t), out, scratch = refs[8:11], refs[11], refs[12:15]

    def add(index, rows, value):
        out[rows, :] = (half[rows, :] + (far[rows, :] + (last[rows, :] + value))).astype(BF16)

    work(
        slots, (mid[...] + end[...],), choose(side_mid, side_end), weights,
        embed_t, head, head_t, *scratch, add,
    )


def local_kernel(slots, frames, side, weights, embed_t, head, head_t, out, *scratch):
    def add(index, rows, value):
        if index == 0:
            out[rows, :] = value
        else:
            out[rows, :] += value

    blocks = [frames[index] for index in range(frames.shape[0])]
    work(slots, blocks, side, weights, embed_t, head, head_t, *scratch, add)


def call(kernel, name, slots, blocks, args, mats, outs):
    width, feats = mats[0].shape
    rows = blocks * BLOCK
    return pl.pallas_call(
        functools.partial(kernel, slots),
        out_shape=outs,
        in_specs=[VMEM] * (len(args) + 3),
        out_specs=jax.tree.map(lambda leaf: VMEM, outs),
        scratch_shapes=[
            pltpu.VMEM((feats, rows), BF16),
            pltpu.VMEM((width, rows), BF16),
            pltpu.VMEM((width, rows), BF16),
        ],
        compiler_params=params(32),
        name=name,
    )(*args, *mats)


def update_kernel(
    feats, nact, mine, theirs, master_embed, master_policy, master_value,
    embed_moment, policy_moment, value_moment, next_obs,
    next_logits, new_embed, new_policy, new_value, new_em, new_pm, new_vm,
):
    def step(grad, moment, master, new_moment, new_master):
        held = MOMENTUM * moment[...] + grad
        new_moment[...] = held
        fresh = master[...] - LEARN_RATE * held
        new_master[...] = fresh
        return fresh

    def grad(start, size):
        return mine[start : start + size, :].astype(F32) + theirs[start : start + size, :].astype(F32)

    embed = step(grad(0, feats), embed_moment, master_embed, new_em, new_embed)
    hidden = jnp.maximum(mm(next_obs[...], embed.astype(BF16)), 0.0).astype(BF16)
    policy = step(grad(feats, nact).T, policy_moment, master_policy, new_pm, new_policy)
    step(grad(feats + nact, PAD)[0:1, :], value_moment, master_value, new_vm, new_value)
    next_logits[...] = mm(hidden, policy.astype(BF16)).astype(BF16)


def update(mine, theirs, *args):
    embed, policy, value = args[0], args[1], args[2]
    next_obs = args[6]
    feats, nact = embed.shape[0], policy.shape[1]
    shapes = [jax.ShapeDtypeStruct(array.shape, F32) for array in (embed, policy, value)]
    return pl.pallas_call(
        functools.partial(update_kernel, feats, nact),
        out_shape=(jax.ShapeDtypeStruct((next_obs.shape[0], nact), BF16), *shapes, *shapes),
        in_specs=[VMEM] * 9,
        out_specs=(VMEM,) * 7,
        compiler_params=params(32),
        name="update",
    )(mine, theirs, *args)


def gathered_grads(slots, n_cores, own, side, mats):
    flip = [(place, place ^ 1) for place in range(8)]
    ends = [pair for pair in flip if pair[0] in (0, 1, 6, 7)]
    mids = [pair for pair in flip if pair[0] in (2, 3, 4, 5)]
    near = [(place, place ^ 2) for place in range(8)]
    inner = [(2, 4), (3, 5), (4, 2), (5, 3)]
    outer = [(2, 0), (3, 1), (4, 6), (5, 7)]

    def send(array, pairs):
        return lax.ppermute(array, "hst", pairs)

    pair = send(own, flip)
    close = send(own, near)
    second_mid = send(own, inner)
    sides = [side] + [
        lax.ppermute(side, AXES, [(place, place ^ mask) for place in range(8 * n_cores)])
        for mask in range(1, 8 * n_cores)
    ]
    cross = send(close, flip)
    second_end = send(second_mid, outer)
    third_mid = send(close, inner)
    second_mid_y = send(second_mid, mids)
    second_end_y = send(second_end, ends)
    third_end = send(third_mid, outer)
    third_mid_y = send(third_mid, mids)
    third_end_y = send(third_end, ends)

    width, feats = mats[0].shape
    grads = jax.ShapeDtypeStruct((feats + mats[2].shape[0], width), F32)
    weights = jax.ShapeDtypeStruct((8 * n_cores, 128), F32)
    by = [sides[n_cores * mask] for mask in range(8)]
    partial, other, weights = call(
        first_kernel, "first", slots, 3, (own, pair, close, *sides), mats, (grads, grads, weights)
    )
    half, far = call(
        second_kernel, "second", slots, 2,
        (cross, second_mid, second_end, by[3], by[6], by[4], weights, partial, other), mats,
        (grads, grads),
    )
    far, last = call(
        third_kernel, "third", slots, 2,
        (second_mid_y, second_end_y, third_mid, third_end, by[7], by[5], by[4], by[6], weights, far),
        mats, (grads, grads),
    )
    return call(
        fourth_kernel, "fourth", slots, 1,
        (third_mid_y, third_end_y, by[5], by[7], weights, half, far, last), mats,
        jax.ShapeDtypeStruct(grads.shape, BF16),
    )


def body(
    n_hst, n_cores, observations, lengths, actions, rewards, assign, actor_embed, actor_policy,
    master_embed, master_policy, master_value, embed_moment, policy_moment, value_moment, next_obs,
):
    traj, slots, feats = observations.shape
    learners = n_hst * n_cores
    rows = traj * slots
    own = observations.reshape(rows, feats)
    value_row = master_value.reshape(1, -1)
    side = actor(
        own, lengths.reshape(1, -1), assign.reshape(1, -1), actions, rewards,
        actor_embed, actor_policy,
    )
    mats = prepare(master_embed, master_policy, value_row)
    if n_hst == 8 and n_cores == 2 and rows == BLOCK:
        mine = gathered_grads(slots, n_cores, own, side, mats)
        theirs = lax.ppermute(mine, "cores", [(0, 1), (1, 0)])
    else:
        named = (assign[:, None] == jnp.arange(learners)[None, :]).astype(F32)
        totals = lax.psum(jnp.sum(named * lengths[:, None].astype(F32), axis=0), AXES)
        weights = jnp.broadcast_to((1.0 / (learners * totals))[:, None], (learners, 128))
        grads = call(
            local_kernel, "local", slots, rows // BLOCK,
            (own.reshape(-1, BLOCK, feats), side, weights), mats,
            jax.ShapeDtypeStruct((feats + mats[2].shape[0], mats[0].shape[0]), F32),
        )
        mine = lax.psum(grads, AXES)
        theirs = jnp.zeros_like(mine)
    outs = update(
        mine, theirs, master_embed, master_policy, value_row, embed_moment, policy_moment,
        value_moment.reshape(1, -1), next_obs,
    )
    logits, new_embed, new_policy, new_value, new_em, new_pm, new_vm = outs
    return logits, new_embed, new_policy, new_value.reshape(-1), new_em, new_pm, new_vm.reshape(-1)


def solution(mesh):
    split = P(("group", "hst", "cores"))
    whole = P("group")
    return jax.shard_map(
        functools.partial(body, mesh.shape["hst"], mesh.shape["cores"]),
        mesh=mesh,
        in_specs=(split,) * 5 + (whole,) * 8 + (split,),
        out_specs=(split,) + (whole,) * 6,
        check_vma=False,
    )
```

```python
import functools

import jax
import jax.numpy as jnp
from jax import lax
from jax.experimental import pallas as pl
from jax.experimental.pallas import tpu as pltpu
from jax.sharding import PartitionSpec as P

GAMMA = 0.99
ENTROPY_COEF = 0.1
MOMENTUM = 0.9
LEARN_RATE = 0.05
AXES = ("hst", "cores")
F32 = jnp.float32
BF16 = jnp.bfloat16
VMEM = pl.BlockSpec(memory_space=pltpu.VMEM)
MIB = 2**20
BLOCK = 256
PAD = 16
BEHAVE, ACTION, REWARD, LENGTH, ASSIGN = range(5)


def iota(shape, dim):
    return lax.broadcasted_iota(jnp.int32, shape, dim)


def mm(a, b):
    return jnp.dot(a, b, preferred_element_type=F32)


def mm_nt(a, b):
    return lax.dot_general(a, b, (((1,), (1,)), ((), ())), preferred_element_type=F32)


def params(mib):
    return pltpu.CompilerParams(vmem_limit_bytes=mib * MIB)


def cost(micros):
    return pl.CostEstimate(flops=int(micros * 1.1e9), bytes_accessed=0, transcendentals=0)


def select_kernel(spread, owner):
    traj, rows = owner.shape
    slots = spread.shape[0]
    spread[...] = (lax.rem(iota((slots, rows), 1), slots) == iota((slots, rows), 0)).astype(F32)
    owner[...] = (lax.div(iota((traj, rows), 1), slots) == iota((traj, rows), 0)).astype(F32)


def select(traj, slots):
    rows = traj * slots
    return pl.pallas_call(
        select_kernel,
        out_shape=(jax.ShapeDtypeStruct((slots, rows), F32), jax.ShapeDtypeStruct((traj, rows), F32)),
        out_specs=(VMEM, VMEM),
        cost_estimate=cost(6),
        name="select",
    )()


def prepare_kernel(
    lengths_at, assign_at, actions_at, rewards_at, obs_at, actor_embed_at, actor_policy_at,
    master_embed_at, master_policy_at, master_value_at, spread, owner,
    side, embed_t, head, head_t, *scratch,
):
    sources = (
        lengths_at, assign_at, actions_at, rewards_at, obs_at, actor_embed_at, actor_policy_at,
        master_embed_at, master_policy_at, master_value_at,
    )
    held, sems = scratch[:-1], scratch[-1]
    copies = [
        pltpu.make_async_copy(source, target, sems.at[index])
        for index, (source, target) in enumerate(zip(sources, held))
    ]
    for copy in copies:
        copy.start()
    (lengths, assign, actions, rewards, obs, actor_embed, actor_policy,
     master_embed, master_policy, master_value) = held
    for copy in copies[:7]:
        copy.wait()

    def flat(series):
        wide = jnp.dot(
            series, spread[...], precision=lax.Precision.HIGHEST, preferred_element_type=F32
        )
        return jnp.sum(wide * owner[...], axis=0, keepdims=True)

    def repeat(series):
        return jnp.dot(
            series.astype(F32), owner[...],
            precision=lax.Precision.HIGHEST, preferred_element_type=F32,
        )

    action = flat(actions[...].astype(F32))
    hidden = jnp.maximum(mm(obs[...], actor_embed[...]), 0.0).astype(BF16)
    logits = mm(hidden, actor_policy[...]).T
    top = jnp.max(logits, axis=0, keepdims=True)
    shifted = logits - top
    norm = jnp.log(jnp.sum(jnp.exp(shifted), axis=0, keepdims=True))
    onehot = iota(logits.shape, 0) == action.astype(jnp.int32)
    side[...] = jnp.zeros_like(side)
    side[BEHAVE : BEHAVE + 1, :] = (
        jnp.sum(jnp.where(onehot, shifted, 0.0), axis=0, keepdims=True) - norm
    )
    side[ACTION : ACTION + 1, :] = action
    side[REWARD : REWARD + 1, :] = flat(rewards[...])
    side[LENGTH : LENGTH + 1, :] = repeat(lengths[...])
    side[ASSIGN : ASSIGN + 1, :] = repeat(assign[...])

    for copy in copies[7:]:
        copy.wait()
    embed_t[...] = master_embed[...].T.astype(BF16)
    nact = master_policy.shape[1]
    wide = jnp.concatenate(
        [
            master_policy[...].T,
            master_value[...],
            jnp.zeros((PAD - 1, head_t.shape[1]), F32),
        ],
        axis=0,
    )
    head_t[...] = wide.astype(BF16)
    head[:, 0:nact] = master_policy[...].astype(BF16)
    head[:, nact:] = wide[nact:, :].T.astype(BF16)


def prepare(*args):
    masks = select(*args[2].shape)
    rows = args[4].shape[0]
    feats, width = args[7].shape
    nact = args[8].shape[1]
    return pl.pallas_call(
        prepare_kernel,
        out_shape=(
            jax.ShapeDtypeStruct((8, rows), F32),
            jax.ShapeDtypeStruct((width, feats), BF16),
            jax.ShapeDtypeStruct((width, nact + PAD), BF16),
            jax.ShapeDtypeStruct((nact + PAD, width), BF16),
        ),
        in_specs=[pl.BlockSpec(memory_space=pl.ANY)] * len(args) + [VMEM] * 2,
        out_specs=(VMEM,) * 4,
        scratch_shapes=[pltpu.VMEM(arg.shape, arg.dtype) for arg in args]
        + [pltpu.SemaphoreType.DMA((len(args),))],
        compiler_params=params(16),
        cost_estimate=cost(3),
        name="prepare",
    )(*args, *masks)


def learner_weights(slots, sides, out):
    learners, rows = out.shape[0], sides.shape[1]
    total = jnp.zeros((learners, rows), F32)
    first = lax.rem(iota((1, rows), 1), slots) == 0
    for place in range(0, sides.shape[0], 8):
        assign = sides[place + ASSIGN : place + ASSIGN + 1, :].astype(jnp.int32)
        length = jnp.where(first, sides[place + LENGTH : place + LENGTH + 1, :], 0.0)
        total = total + jnp.where(iota((learners, rows), 0) == assign, length, 0.0)
    summed = jnp.sum(total, axis=1, keepdims=True)
    out[...] = jnp.broadcast_to(1.0 / (learners * summed), out.shape)


def vtrace(slots, nact, side, weights, logits, values):
    rows = logits.shape[1]
    learners = weights.shape[0]
    behave = side[BEHAVE : BEHAVE + 1, :]
    reward = side[REWARD : REWARD + 1, :]
    length = side[LENGTH : LENGTH + 1, :].astype(jnp.int32)
    assign = side[ASSIGN : ASSIGN + 1, :].astype(jnp.int32)
    action = side[ACTION : ACTION + 1, :].astype(jnp.int32)
    weight = jnp.sum(
        jnp.where(iota((learners, rows), 0) == assign, weights[:, 0:1], 0.0), axis=0, keepdims=True
    )
    top = jnp.max(logits, axis=0, keepdims=True)
    exps = jnp.exp(logits - top)
    norm = jnp.sum(exps, axis=0, keepdims=True)
    logprob = logits - (top + jnp.log(norm))
    probs = exps * (1.0 / norm)
    onehot = iota(logits.shape, 0) == action
    taken = jnp.sum(jnp.where(onehot, logprob, 0.0), axis=0, keepdims=True)
    entropy = -jnp.sum(probs * logprob, axis=0, keepdims=True)
    step = lax.rem(iota((1, rows), 1), slots)
    inside = (step < length).astype(F32)
    beyond = (step + 1 < length).astype(F32)
    ratios = jnp.minimum(1.0, jnp.exp(taken - behave))

    def later(series, by):
        return pltpu.roll(series, rows - by, 1)

    deltas = inside * ratios * (reward + GAMMA * later(values, 1) * beyond - values)
    decay = GAMMA * ratios * inside
    corrections = deltas
    reach = 1
    while reach < slots:
        within = step + reach < slots
        corrections = corrections + decay * jnp.where(within, later(corrections, reach), 0.0)
        decay = decay * jnp.where(within, later(decay, reach), 0.0)
        reach *= 2
    targets = values + corrections
    advantage = ratios * (reward + GAMMA * later(targets, 1) * beyond - values)
    scale = weight * inside
    grad = scale * (
        -advantage * (onehot.astype(F32) - probs) + ENTROPY_COEF * probs * (logprob + entropy)
    )
    return grad, scale * (values - targets)


def work(slots, frames, side, weights, embed_t, head, head_t, frames_t, hidden_t, preact_t, add):
    width, feats = embed_t.shape
    nact = head_t.shape[0] - PAD
    tile = 256
    for index, block in enumerate(frames):
        frames_t[:, index * BLOCK : (index + 1) * BLOCK] = block.T
    for start in range(0, width, tile):
        here = slice(start, start + tile)
        hidden_t[here, :] = jnp.maximum(mm(embed_t[here, :], frames_t[...]), 0.0).astype(BF16)
    logits = mm(head_t[...], hidden_t[...])
    grad, grad_values = vtrace(
        slots, nact, side, weights, logits[0:nact, :], logits[nact : nact + 1, :]
    )
    pad = jnp.zeros((PAD - 1, grad.shape[1]), F32)
    grad_t = jnp.concatenate([grad, grad_values, pad], axis=0).astype(BF16)
    for start in range(0, width, tile):
        here = slice(start, start + tile)
        back = mm(head[here, :], grad_t)
        alive = hidden_t[here, :].astype(F32) > 0.0
        preact_t[here, :] = jnp.where(alive, back, 0.0).astype(BF16)
    for index in range(len(frames)):
        lanes = slice(index * BLOCK, (index + 1) * BLOCK)
        add(index, slice(0, feats), mm_nt(frames_t[:, lanes], preact_t[:, lanes]))
        add(index, slice(feats, feats + nact + PAD), mm_nt(grad_t[:, lanes], hidden_t[:, lanes]))


def work(slots, frames, side, weights, embed_t, head, head_t, frames_t, hidden_t, preact_t, add):
    width, feats = embed_t.shape
    nact = head_t.shape[0] - PAD
    tile = 256
    for index, block in enumerate(frames):
        frames_t[:, index * BLOCK : (index + 1) * BLOCK] = block.T
    for start in range(0, width, tile):
        here = slice(start, start + tile)
        hidden_t[here, :] = jnp.maximum(mm(embed_t[here, :], frames_t[...]), 0.0).astype(BF16)
    logits = mm(head_t[...], hidden_t[...])
    grad, grad_values = vtrace(
        slots, nact, side, weights, logits[0:nact, :], logits[nact : nact + 1, :]
    )
    pad = jnp.zeros((PAD - 1, grad.shape[1]), F32)
    grad_t = jnp.concatenate([grad, grad_values, pad], axis=0).astype(BF16)
    for start in range(0, width, tile):
        here = slice(start, start + tile)
        back = mm(head[here, :], grad_t)
        alive = hidden_t[here, :].astype(F32) > 0.0
        preact_t[here, :] = jnp.where(alive, back, 0.0).astype(BF16)
    for index in range(len(frames)):
        lanes = slice(index * BLOCK, (index + 1) * BLOCK)
        add(index, slice(0, feats), mm_nt(frames_t[:, lanes], preact_t[:, lanes]))
        add(index, slice(feats, feats + nact + PAD), mm_nt(grad_t[:, lanes], hidden_t[:, lanes]))


def on_mid():
    line = lax.div(lax.axis_index("hst"), 2)
    return jnp.logical_or(line == 1, line == 2)


def side_of(sides, back, flip):
    line = lax.div(lax.axis_index("hst"), 2)
    there = lax.bitwise_and(line + 4 - back, 3)
    mask = 2 * lax.bitwise_xor(line, there) + flip
    return sides[pl.ds(pl.multiple_of(16 * mask, 8), 8), :]


def first_kernel(slots, *refs):
    (own, own_y, one, *pieces), mats, (out, other, weights, sides), scratch = (
        refs[0:7], refs[7:10], refs[10:14], refs[14:17])
    start = 0
    for piece in pieces:
        sides[start : start + piece.shape[0], :] = piece[...]
        start += piece.shape[0]
    learner_weights(slots, sides, weights)

    def add(index, rows, value):
        if index == 0:
            out[rows, :] = value
        elif index == 1:
            out[rows, :] += value
        else:
            other[rows, :] = value

    side = jnp.concatenate([side_of(sides, *at) for at in ((0, 0), (0, 1), (1, 0))], axis=1)
    work(slots, (own[...], own_y[...], one[...]), side, weights, *mats, *scratch, add)


def second_kernel(slots, *refs):
    (one_y, two, sides, weights, one_sum), mats, (out, other), scratch = (
        refs[0:5], refs[5:8], refs[8:10], refs[10:13])

    def add(index, rows, value):
        if index == 0:
            out[rows, :] = one_sum[rows, :] + value
        else:
            other[rows, :] = value

    side = jnp.concatenate([side_of(sides, 1, 1), side_of(sides, 2, 0)], axis=1)
    work(slots, (one_y[...], two[...]), side, weights, *mats, *scratch, add)


def third_kernel(slots, *refs):
    (two_y, three, sides, weights, own_sum, two_sum), mats, (out, other), scratch = (
        refs[0:6], refs[6:9], refs[9:11], refs[11:14])

    def add(index, rows, value):
        if index == 0:
            out[rows, :] = own_sum[rows, :] + (two_sum[rows, :] + value)
        else:
            other[rows, :] = value

    side = jnp.concatenate([side_of(sides, 2, 1), side_of(sides, 3, 0)], axis=1)
    work(slots, (two_y[...], three[...]), side, weights, *mats, *scratch, add)


def fourth_kernel(slots, *refs):
    (three_y, sides, weights, even_sum, one_sum, three_sum), mats, out, scratch = (
        refs[0:6], refs[6:9], refs[9], refs[10:13])

    def add(index, rows, value):
        out[rows, :] = (
            even_sum[rows, :] + (one_sum[rows, :] + (three_sum[rows, :] + value))
        ).astype(BF16)

    work(slots, (three_y[...],), side_of(sides, 3, 1), weights, *mats, *scratch, add)


def local_kernel(slots, frames, side, weights, embed_t, head, head_t, out, *scratch):
    def add(index, rows, value):
        if index == 0:
            out[rows, :] = value
        else:
            out[rows, :] += value

    blocks = [frames[index] for index in range(frames.shape[0])]
    work(slots, blocks, side, weights, embed_t, head, head_t, *scratch, add)


def call(kernel, name, slots, blocks, args, mats, outs):
    width, feats = mats[0].shape
    rows = blocks * BLOCK
    return pl.pallas_call(
        functools.partial(kernel, slots),
        out_shape=outs,
        in_specs=[VMEM] * (len(args) + 3),
        out_specs=jax.tree.map(lambda leaf: VMEM, outs),
        scratch_shapes=[
            pltpu.VMEM((feats, rows), BF16),
            pltpu.VMEM((width, rows), BF16),
            pltpu.VMEM((width, rows), BF16),
        ],
        compiler_params=params(32),
        cost_estimate=cost(1.2 * blocks + 0.4),
        name=name,
    )(*args, *mats)


def update_kernel(
    feats, nact, mine, theirs, master_embed, master_policy, master_value,
    embed_moment, policy_moment, value_moment, next_obs,
    next_logits, new_embed, new_policy, new_value, new_em, new_pm, new_vm,
):
    def step(grad, moment, master, new_moment, new_master):
        held = MOMENTUM * moment[...] + grad
        new_moment[...] = held
        fresh = master[...] - LEARN_RATE * held
        new_master[...] = fresh
        return fresh

    def grad(start, size):
        return mine[start : start + size, :].astype(F32) + theirs[start : start + size, :].astype(F32)

    embed = step(grad(0, feats), embed_moment, master_embed, new_em, new_embed)
    hidden = jnp.maximum(mm(next_obs[...], embed.astype(BF16)), 0.0).astype(BF16)
    policy = step(grad(feats, nact).T, policy_moment, master_policy, new_pm, new_policy)
    step(grad(feats + nact, PAD)[0:1, :], value_moment, master_value, new_vm, new_value)
    next_logits[...] = mm(hidden, policy.astype(BF16)).astype(BF16)


def update(mine, theirs, *args):
    embed, policy, value = args[0], args[1], args[2]
    next_obs = args[6]
    feats, nact = embed.shape[0], policy.shape[1]
    shapes = [jax.ShapeDtypeStruct(array.shape, F32) for array in (embed, policy, value)]
    return pl.pallas_call(
        functools.partial(update_kernel, feats, nact),
        out_shape=(jax.ShapeDtypeStruct((next_obs.shape[0], nact), BF16), *shapes, *shapes),
        in_specs=[VMEM] * 9,
        out_specs=(VMEM,) * 7,
        compiler_params=params(32),
        cost_estimate=cost(3.4),
        name="update",
    )(mine, theirs, *args)


def gathered_grads(slots, n_cores, own, side, mats):
    across = [(place, place ^ 1) for place in range(8)]
    along = [(place, (place + 2) % 8) for place in range(8)]

    def send(array, pairs):
        return lax.ppermute(array, "hst", pairs)

    one = send(own, along)
    own_y = send(own, across)
    pieces = [side]
    for scale in (1, 4):
        held = pieces[0] if scale == 1 else jnp.concatenate(pieces, axis=0)
        if scale == 4:
            held, one, own_y = lax.optimization_barrier((held, one, own_y))
        pieces = [held] + [
            lax.ppermute(held, AXES, [(at, at ^ (scale * step)) for at in range(8 * n_cores)])
            for step in (1, 2, 3)
        ]
    two = send(one, along)
    one_y = send(one, across)
    three = send(two, along)
    two_y = send(two, across)
    three_y = send(three, across)

    width, feats = mats[0].shape
    grads = jax.ShapeDtypeStruct((feats + mats[2].shape[0], width), F32)
    weights = jax.ShapeDtypeStruct((8 * n_cores, 128), F32)
    sides = jax.ShapeDtypeStruct((64 * n_cores, side.shape[1]), F32)
    own_sum, one_sum, weights, sides = call(
        first_kernel, "first", slots, 3, (own, own_y, one, *pieces), mats,
        (grads, grads, weights, sides),
    )
    one_sum, two_sum = call(
        second_kernel, "second", slots, 2, (one_y, two, sides, weights, one_sum), mats,
        (grads, grads),
    )
    even_sum, three_sum = call(
        third_kernel, "third", slots, 2, (two_y, three, sides, weights, own_sum, two_sum), mats,
        (grads, grads),
    )
    return call(
        fourth_kernel, "fourth", slots, 1,
        (three_y, sides, weights, even_sum, one_sum, three_sum), mats,
        jax.ShapeDtypeStruct(grads.shape, BF16),
    )


def body(
    n_hst, n_cores, observations, lengths, actions, rewards, assign, actor_embed, actor_policy,
    master_embed, master_policy, master_value, embed_moment, policy_moment, value_moment, next_obs,
):
    traj, slots, feats = observations.shape
    learners = n_hst * n_cores
    rows = traj * slots
    own = observations.reshape(rows, feats)
    value_row = master_value.reshape(1, -1)
    side, *mats = prepare(
        lengths.reshape(1, -1), assign.reshape(1, -1), actions, rewards, own,
        actor_embed, actor_policy, master_embed, master_policy, value_row,
    )
    if n_hst == 8 and n_cores == 2 and rows == BLOCK:
        mine = gathered_grads(slots, n_cores, own, side, mats)
        theirs = lax.ppermute(mine, "cores", [(0, 1), (1, 0)])
    else:
        named = (assign[:, None] == jnp.arange(learners)[None, :]).astype(F32)
        totals = lax.psum(jnp.sum(named * lengths[:, None].astype(F32), axis=0), AXES)
        weights = jnp.broadcast_to((1.0 / (learners * totals))[:, None], (learners, 128))
        grads = call(
            local_kernel, "local", slots, rows // BLOCK,
            (own.reshape(-1, BLOCK, feats), side, weights), mats,
            jax.ShapeDtypeStruct((feats + mats[2].shape[0], mats[0].shape[0]), F32),
        )
        mine = lax.psum(grads, AXES)
        theirs = jnp.zeros_like(mine)
    outs = update(
        mine, theirs, master_embed, master_policy, value_row, embed_moment, policy_moment,
        value_moment.reshape(1, -1), next_obs,
    )
    logits, new_embed, new_policy, new_value, new_em, new_pm, new_vm = outs
    return logits, new_embed, new_policy, new_value.reshape(-1), new_em, new_pm, new_vm.reshape(-1)


def solution(mesh):
    split = P(("group", "hst", "cores"))
    whole = P("group")
    return jax.shard_map(
        functools.partial(body, mesh.shape["hst"], mesh.shape["cores"]),
        mesh=mesh,
        in_specs=(split,) * 5 + (whole,) * 8 + (split,),
        out_specs=(split,) + (whole,) * 6,
        check_vma=False,
    )
```

```python
import functools

import jax
import jax.numpy as jnp
from jax import lax
from jax.experimental import pallas as pl
from jax.experimental.pallas import tpu as pltpu
from jax.sharding import PartitionSpec as P

GAMMA = 0.99
ENTROPY_COEF = 0.1
MOMENTUM = 0.9
LEARN_RATE = 0.05
AXES = ("hst", "cores")
F32 = jnp.float32
BF16 = jnp.bfloat16
VMEM = pl.BlockSpec(memory_space=pltpu.VMEM)
MIB = 2**20
BLOCK = 256
PAD = 16
BEHAVE, ACTION, REWARD, LENGTH, ASSIGN = range(5)


def iota(shape, dim):
    return lax.broadcasted_iota(jnp.int32, shape, dim)


def mm(a, b):
    return jnp.dot(a, b, preferred_element_type=F32)


def mm_nt(a, b):
    return lax.dot_general(a, b, (((1,), (1,)), ((), ())), preferred_element_type=F32)


def params(mib):
    return pltpu.CompilerParams(vmem_limit_bytes=mib * MIB)


def cost(micros):
    return pl.CostEstimate(flops=int(micros * 1.1e9), bytes_accessed=0, transcendentals=0)


def select_kernel(spread, owner):
    traj, rows = owner.shape
    slots = spread.shape[0]
    spread[...] = (lax.rem(iota((slots, rows), 1), slots) == iota((slots, rows), 0)).astype(F32)
    owner[...] = (lax.div(iota((traj, rows), 1), slots) == iota((traj, rows), 0)).astype(F32)


def select(traj, slots):
    rows = traj * slots
    return pl.pallas_call(
        select_kernel,
        out_shape=(jax.ShapeDtypeStruct((slots, rows), F32), jax.ShapeDtypeStruct((traj, rows), F32)),
        out_specs=(VMEM, VMEM),
        cost_estimate=cost(40),
        name="select",
    )()


def prepare_kernel(
    lengths_at, assign_at, actions_at, rewards_at, obs_at, actor_embed_at, actor_policy_at,
    master_embed_at, master_policy_at, master_value_at, spread, owner,
    side, embed_t, head, head_t, *scratch,
):
    sources = (
        lengths_at, assign_at, actions_at, rewards_at, obs_at, actor_embed_at, actor_policy_at,
        master_embed_at, master_policy_at, master_value_at,
    )
    held, sems = scratch[:-1], scratch[-1]
    copies = [
        pltpu.make_async_copy(source, target, sems.at[index])
        for index, (source, target) in enumerate(zip(sources, held))
    ]
    for copy in copies:
        copy.start()
    (lengths, assign, actions, rewards, obs, actor_embed, actor_policy,
     master_embed, master_policy, master_value) = held
    for copy in copies[:7]:
        copy.wait()

    def flat(series):
        wide = jnp.dot(
            series, spread[...], precision=lax.Precision.HIGHEST, preferred_element_type=F32
        )
        return jnp.sum(wide * owner[...], axis=0, keepdims=True)

    def repeat(series):
        return jnp.dot(
            series.astype(F32), owner[...],
            precision=lax.Precision.HIGHEST, preferred_element_type=F32,
        )

    action = flat(actions[...].astype(F32))
    hidden = jnp.maximum(mm(obs[...], actor_embed[...]), 0.0).astype(BF16)
    logits = mm(hidden, actor_policy[...]).T
    top = jnp.max(logits, axis=0, keepdims=True)
    shifted = logits - top
    norm = jnp.log(jnp.sum(jnp.exp(shifted), axis=0, keepdims=True))
    onehot = iota(logits.shape, 0) == action.astype(jnp.int32)
    side[...] = jnp.zeros_like(side)
    side[BEHAVE : BEHAVE + 1, :] = (
        jnp.sum(jnp.where(onehot, shifted, 0.0), axis=0, keepdims=True) - norm
    )
    side[ACTION : ACTION + 1, :] = action
    side[REWARD : REWARD + 1, :] = flat(rewards[...])
    side[LENGTH : LENGTH + 1, :] = repeat(lengths[...])
    side[ASSIGN : ASSIGN + 1, :] = repeat(assign[...])

    for copy in copies[7:]:
        copy.wait()
    embed_t[...] = master_embed[...].T.astype(BF16)
    nact = master_policy.shape[1]
    wide = jnp.concatenate(
        [
            master_policy[...].T,
            master_value[...],
            jnp.zeros((PAD - 1, head_t.shape[1]), F32),
        ],
        axis=0,
    )
    head_t[...] = wide.astype(BF16)
    head[:, 0:nact] = master_policy[...].astype(BF16)
    head[:, nact:] = wide[nact:, :].T.astype(BF16)


def prepare(*args):
    masks = select(*args[2].shape)
    rows = args[4].shape[0]
    feats, width = args[7].shape
    nact = args[8].shape[1]
    return pl.pallas_call(
        prepare_kernel,
        out_shape=(
            jax.ShapeDtypeStruct((8, rows), F32),
            jax.ShapeDtypeStruct((width, feats), BF16),
            jax.ShapeDtypeStruct((width, nact + PAD), BF16),
            jax.ShapeDtypeStruct((nact + PAD, width), BF16),
        ),
        in_specs=[pl.BlockSpec(memory_space=pl.ANY)] * len(args) + [VMEM] * 2,
        out_specs=(VMEM,) * 4,
        scratch_shapes=[pltpu.VMEM(arg.shape, arg.dtype) for arg in args]
        + [pltpu.SemaphoreType.DMA((len(args),))],
        compiler_params=params(16),
        cost_estimate=cost(3),
        name="prepare",
    )(*args, *masks)


def learner_weights(slots, sides, out):
    learners, rows = out.shape[0], sides.shape[1]
    total = jnp.zeros((learners, rows), F32)
    first = lax.rem(iota((1, rows), 1), slots) == 0
    for place in range(0, sides.shape[0], 8):
        assign = sides[place + ASSIGN : place + ASSIGN + 1, :].astype(jnp.int32)
        length = jnp.where(first, sides[place + LENGTH : place + LENGTH + 1, :], 0.0)
        total = total + jnp.where(iota((learners, rows), 0) == assign, length, 0.0)
    summed = jnp.sum(total, axis=1, keepdims=True)
    out[...] = jnp.broadcast_to(1.0 / (learners * summed), out.shape)


def vtrace(slots, nact, side, weights, logits, values):
    rows = logits.shape[1]
    learners = weights.shape[0]
    behave = side[BEHAVE : BEHAVE + 1, :]
    reward = side[REWARD : REWARD + 1, :]
    length = side[LENGTH : LENGTH + 1, :].astype(jnp.int32)
    assign = side[ASSIGN : ASSIGN + 1, :].astype(jnp.int32)
    action = side[ACTION : ACTION + 1, :].astype(jnp.int32)
    weight = jnp.sum(
        jnp.where(iota((learners, rows), 0) == assign, weights[:, 0:1], 0.0), axis=0, keepdims=True
    )
    top = jnp.max(logits, axis=0, keepdims=True)
    exps = jnp.exp(logits - top)
    norm = jnp.sum(exps, axis=0, keepdims=True)
    logprob = logits - (top + jnp.log(norm))
    probs = exps * (1.0 / norm)
    onehot = iota(logits.shape, 0) == action
    taken = jnp.sum(jnp.where(onehot, logprob, 0.0), axis=0, keepdims=True)
    entropy = -jnp.sum(probs * logprob, axis=0, keepdims=True)
    step = lax.rem(iota((1, rows), 1), slots)
    inside = (step < length).astype(F32)
    beyond = (step + 1 < length).astype(F32)
    ratios = jnp.minimum(1.0, jnp.exp(taken - behave))

    def later(series, by):
        return pltpu.roll(series, rows - by, 1)

    deltas = inside * ratios * (reward + GAMMA * later(values, 1) * beyond - values)
    decay = GAMMA * ratios * inside
    corrections = deltas
    reach = 1
    while reach < slots:
        within = step + reach < slots
        corrections = corrections + decay * jnp.where(within, later(corrections, reach), 0.0)
        decay = decay * jnp.where(within, later(decay, reach), 0.0)
        reach *= 2
    targets = values + corrections
    advantage = ratios * (reward + GAMMA * later(targets, 1) * beyond - values)
    scale = weight * inside
    grad = scale * (
        -advantage * (onehot.astype(F32) - probs) + ENTROPY_COEF * probs * (logprob + entropy)
    )
    return grad, scale * (values - targets)


def forward(frames, embed_t, head_t, frames_t, hidden_t):
    width = embed_t.shape[0]
    tile = 256
    for index, block in enumerate(frames):
        frames_t[:, index * BLOCK : (index + 1) * BLOCK] = block.T
    for start in range(0, width, tile):
        here = slice(start, start + tile)
        hidden_t[here, :] = jnp.maximum(mm(embed_t[here, :], frames_t[...]), 0.0).astype(BF16)
    return mm(head_t[...], hidden_t[...])


def backward(slots, logits, side, weights, head, frames_t, hidden_t, preact_t, add):
    width, feats = head.shape[0], frames_t.shape[0]
    nact = logits.shape[0] - PAD
    tile = 256
    grad, grad_values = vtrace(
        slots, nact, side, weights, logits[0:nact, :], logits[nact : nact + 1, :]
    )
    pad = jnp.zeros((PAD - 1, grad.shape[1]), F32)
    grad_t = jnp.concatenate([grad, grad_values, pad], axis=0).astype(BF16)
    for start in range(0, width, tile):
        here = slice(start, start + tile)
        back = mm(head[here, :], grad_t)
        alive = hidden_t[here, :].astype(F32) > 0.0
        preact_t[here, :] = jnp.where(alive, back, 0.0).astype(BF16)
    for index in range(frames_t.shape[1] // BLOCK):
        lanes = slice(index * BLOCK, (index + 1) * BLOCK)
        add(index, slice(0, feats), mm_nt(frames_t[:, lanes], preact_t[:, lanes]))
        add(index, slice(feats, feats + nact + PAD), mm_nt(grad_t[:, lanes], hidden_t[:, lanes]))


def work(slots, frames, side, weights, embed_t, head, head_t, frames_t, hidden_t, preact_t, add):
    logits = forward(frames, embed_t, head_t, frames_t, hidden_t)
    backward(slots, logits, side, weights, head, frames_t, hidden_t, preact_t, add)


def side_of(sides, back, flip):
    line = lax.div(lax.axis_index("hst"), 2)
    there = lax.bitwise_and(line + 4 - back, 3)
    mask = 2 * lax.bitwise_xor(line, there) + flip
    return sides[pl.ds(pl.multiple_of(16 * mask, 8), 8), :]


def ahead_kernel(own, own_y, one, embed_t, head_t, frames_t, hidden_t, logits):
    logits[...] = forward((own[...], own_y[...], one[...]), embed_t, head_t, frames_t, hidden_t)


def ahead(frames, embed_t, head_t):
    width, feats = embed_t.shape
    rows = len(frames) * BLOCK
    return pl.pallas_call(
        ahead_kernel,
        out_shape=(
            jax.ShapeDtypeStruct((feats, rows), BF16),
            jax.ShapeDtypeStruct((width, rows), BF16),
            jax.ShapeDtypeStruct((head_t.shape[0], rows), F32),
        ),
        in_specs=[VMEM] * 5,
        out_specs=(VMEM,) * 3,
        compiler_params=params(20),
        cost_estimate=cost(1.6),
        name="ahead",
    )(*frames, embed_t, head_t)


def first_kernel(slots, *refs):
    (frames_t, hidden_t, logits, *pieces), mats, (out, other, weights, sides), scratch = (
        refs[0:7], refs[7:10], refs[10:14], refs[14:17])
    start = 0
    for piece in pieces:
        sides[start : start + piece.shape[0], :] = piece[...]
        start += piece.shape[0]
    learner_weights(slots, sides, weights)

    def add(index, rows, value):
        if index == 0:
            out[rows, :] = value
        elif index == 1:
            out[rows, :] += value
        else:
            other[rows, :] = value

    side = jnp.concatenate([side_of(sides, *at) for at in ((0, 0), (0, 1), (1, 0))], axis=1)
    backward(slots, logits[...], side, weights, mats[1], frames_t, hidden_t, scratch[2], add)


def second_kernel(slots, *refs):
    (one_y, two, sides, weights, one_sum), mats, (out, other), scratch = (
        refs[0:5], refs[5:8], refs[8:10], refs[10:13])

    def add(index, rows, value):
        if index == 0:
            out[rows, :] = one_sum[rows, :] + value
        else:
            other[rows, :] = value

    side = jnp.concatenate([side_of(sides, 1, 1), side_of(sides, 2, 0)], axis=1)
    work(slots, (one_y[...], two[...]), side, weights, *mats, *scratch, add)


def third_kernel(slots, *refs):
    (two_y, three, sides, weights, own_sum, two_sum), mats, (out, other), scratch = (
        refs[0:6], refs[6:9], refs[9:11], refs[11:14])

    def add(index, rows, value):
        if index == 0:
            out[rows, :] = own_sum[rows, :] + (two_sum[rows, :] + value)
        else:
            other[rows, :] = value

    side = jnp.concatenate([side_of(sides, 2, 1), side_of(sides, 3, 0)], axis=1)
    work(slots, (two_y[...], three[...]), side, weights, *mats, *scratch, add)


def fourth_kernel(slots, *refs):
    (three_y, sides, weights, even_sum, one_sum, three_sum), mats, out, scratch = (
        refs[0:6], refs[6:9], refs[9], refs[10:13])

    def add(index, rows, value):
        out[rows, :] = (
            even_sum[rows, :] + (one_sum[rows, :] + (three_sum[rows, :] + value))
        ).astype(BF16)

    work(slots, (three_y[...],), side_of(sides, 3, 1), weights, *mats, *scratch, add)


def local_kernel(slots, frames, side, weights, embed_t, head, head_t, out, *scratch):
    def add(index, rows, value):
        if index == 0:
            out[rows, :] = value
        else:
            out[rows, :] += value

    blocks = [frames[index] for index in range(frames.shape[0])]
    work(slots, blocks, side, weights, embed_t, head, head_t, *scratch, add)


def call(kernel, name, slots, blocks, args, mats, outs):
    width, feats = mats[0].shape
    rows = blocks * BLOCK
    return pl.pallas_call(
        functools.partial(kernel, slots),
        out_shape=outs,
        in_specs=[VMEM] * (len(args) + 3),
        out_specs=jax.tree.map(lambda leaf: VMEM, outs),
        scratch_shapes=[
            pltpu.VMEM((feats, rows), BF16),
            pltpu.VMEM((width, rows), BF16),
            pltpu.VMEM((width, rows), BF16),
        ],
        compiler_params=params(32),
        cost_estimate=cost(1.2 * blocks + 0.4),
        name=name,
    )(*args, *mats)


def update_kernel(
    feats, nact, mine, theirs, master_embed, master_policy, master_value,
    embed_moment, policy_moment, value_moment, next_obs,
    next_logits, new_embed, new_policy, new_value, new_em, new_pm, new_vm,
):
    def step(grad, moment, master, new_moment, new_master):
        held = MOMENTUM * moment[...] + grad
        new_moment[...] = held
        fresh = master[...] - LEARN_RATE * held
        new_master[...] = fresh
        return fresh

    def grad(start, size):
        return mine[start : start + size, :].astype(F32) + theirs[start : start + size, :].astype(F32)

    embed = step(grad(0, feats), embed_moment, master_embed, new_em, new_embed)
    hidden = jnp.maximum(mm(next_obs[...], embed.astype(BF16)), 0.0).astype(BF16)
    policy = step(grad(feats, nact).T, policy_moment, master_policy, new_pm, new_policy)
    step(grad(feats + nact, PAD)[0:1, :], value_moment, master_value, new_vm, new_value)
    next_logits[...] = mm(hidden, policy.astype(BF16)).astype(BF16)


def update(mine, theirs, *args):
    embed, policy, value = args[0], args[1], args[2]
    next_obs = args[6]
    feats, nact = embed.shape[0], policy.shape[1]
    shapes = [jax.ShapeDtypeStruct(array.shape, F32) for array in (embed, policy, value)]
    return pl.pallas_call(
        functools.partial(update_kernel, feats, nact),
        out_shape=(jax.ShapeDtypeStruct((next_obs.shape[0], nact), BF16), *shapes, *shapes),
        in_specs=[VMEM] * 9,
        out_specs=(VMEM,) * 7,
        compiler_params=params(32),
        cost_estimate=cost(3.4),
        name="update",
    )(mine, theirs, *args)


def gathered_grads(slots, n_cores, own, side, mats):
    across = [(place, place ^ 1) for place in range(8)]
    along = [(place, (place + 2) % 8) for place in range(8)]

    def send(array, pairs):
        return lax.ppermute(array, "hst", pairs)

    one = send(own, along)
    own_y = send(own, across)
    pieces = [side]
    for scale in (1, 4):
        held = pieces[0] if scale == 1 else jnp.concatenate(pieces, axis=0)
        if scale == 4:
            held, one, own_y = lax.optimization_barrier((held, one, own_y))
        pieces = [held] + [
            lax.ppermute(held, AXES, [(at, at ^ (scale * step)) for at in range(8 * n_cores)])
            for step in (1, 2, 3)
        ]
    two = send(one, along)
    one_y = send(one, across)
    three = send(two, along)
    two_y = send(two, across)
    three_y = send(three, across)
    done = ahead((own, own_y, one), mats[0], mats[2])
    pieces, two = lax.optimization_barrier((pieces, two))

    width, feats = mats[0].shape
    grads = jax.ShapeDtypeStruct((feats + mats[2].shape[0], width), F32)
    weights = jax.ShapeDtypeStruct((8 * n_cores, 128), F32)
    sides = jax.ShapeDtypeStruct((64 * n_cores, side.shape[1]), F32)
    own_sum, one_sum, weights, sides = call(
        first_kernel, "first", slots, 3, (*done, *pieces), mats,
        (grads, grads, weights, sides),
    )
    one_sum, two_sum = call(
        second_kernel, "second", slots, 2, (one_y, two, sides, weights, one_sum), mats,
        (grads, grads),
    )
    even_sum, three_sum = call(
        third_kernel, "third", slots, 2, (two_y, three, sides, weights, own_sum, two_sum), mats,
        (grads, grads),
    )
    return call(
        fourth_kernel, "fourth", slots, 1,
        (three_y, sides, weights, even_sum, one_sum, three_sum), mats,
        jax.ShapeDtypeStruct(grads.shape, BF16),
    )


def body(
    n_hst, n_cores, observations, lengths, actions, rewards, assign, actor_embed, actor_policy,
    master_embed, master_policy, master_value, embed_moment, policy_moment, value_moment, next_obs,
):
    traj, slots, feats = observations.shape
    learners = n_hst * n_cores
    rows = traj * slots
    own = observations.reshape(rows, feats)
    value_row = master_value.reshape(1, -1)
    side, *mats = prepare(
        lengths.reshape(1, -1), assign.reshape(1, -1), actions, rewards, own,
        actor_embed, actor_policy, master_embed, master_policy, value_row,
    )
    if n_hst == 8 and n_cores == 2 and rows == BLOCK:
        mine = gathered_grads(slots, n_cores, own, side, mats)
        theirs = lax.ppermute(mine, "cores", [(0, 1), (1, 0)])
    else:
        named = (assign[:, None] == jnp.arange(learners)[None, :]).astype(F32)
        totals = lax.psum(jnp.sum(named * lengths[:, None].astype(F32), axis=0), AXES)
        weights = jnp.broadcast_to((1.0 / (learners * totals))[:, None], (learners, 128))
        grads = call(
            local_kernel, "local", slots, rows // BLOCK,
            (own.reshape(-1, BLOCK, feats), side, weights), mats,
            jax.ShapeDtypeStruct((feats + mats[2].shape[0], mats[0].shape[0]), F32),
        )
        mine = lax.psum(grads, AXES)
        theirs = jnp.zeros_like(mine)
    outs = update(
        mine, theirs, master_embed, master_policy, value_row, embed_moment, policy_moment,
        value_moment.reshape(1, -1), next_obs,
    )
    logits, new_embed, new_policy, new_value, new_em, new_pm, new_vm = outs
    return logits, new_embed, new_policy, new_value.reshape(-1), new_em, new_pm, new_vm.reshape(-1)


def solution(mesh):
    split = P(("group", "hst", "cores"))
    whole = P("group")
    return jax.shard_map(
        functools.partial(body, mesh.shape["hst"], mesh.shape["cores"]),
        mesh=mesh,
        in_specs=(split,) * 5 + (whole,) * 8 + (split,),
        out_specs=(split,) + (whole,) * 6,
        check_vma=False,
    )
```

```python
import functools

import jax
import jax.numpy as jnp
from jax import lax
from jax.experimental import pallas as pl
from jax.experimental.pallas import tpu as pltpu
from jax.sharding import PartitionSpec as P

GAMMA = 0.99
ENTROPY_COEF = 0.1
MOMENTUM = 0.9
LEARN_RATE = 0.05
AXES = ("hst", "cores")
F32 = jnp.float32
BF16 = jnp.bfloat16
VMEM = pl.BlockSpec(memory_space=pltpu.VMEM)
MIB = 2**20
BLOCK = 256
HALF = 128
PAD = 16
BEHAVE, ACTION, REWARD, LENGTH, ASSIGN, LENGTH_2, ASSIGN_2 = range(7)


def iota(shape, dim):
    return lax.broadcasted_iota(jnp.int32, shape, dim)


def mm(a, b):
    return jnp.dot(a, b, preferred_element_type=F32)


def mm_nt(a, b):
    return lax.dot_general(a, b, (((1,), (1,)), ((), ())), preferred_element_type=F32)


def params(mib):
    return pltpu.CompilerParams(vmem_limit_bytes=mib * MIB)


def cost(micros):
    return pl.CostEstimate(flops=int(micros * 1.1e9), bytes_accessed=0, transcendentals=0)


def select_kernel(spread, owner):
    traj, rows = owner.shape
    slots = spread.shape[0]
    spread[...] = (lax.rem(iota((slots, rows), 1), slots) == iota((slots, rows), 0)).astype(F32)
    owner[...] = (lax.div(iota((traj, rows), 1), slots) == iota((traj, rows), 0)).astype(F32)


def select(traj, slots):
    rows = traj * slots
    return pl.pallas_call(
        select_kernel,
        out_shape=(jax.ShapeDtypeStruct((slots, rows), F32), jax.ShapeDtypeStruct((traj, rows), F32)),
        out_specs=(VMEM, VMEM),
        compiler_params=params(4),
        cost_estimate=cost(40),
        name="select",
    )()


def side_kernel(
    lengths, assign, lengths_2, assign_2, actions, rewards, actor_embed, actor_policy,
    spread, owner, *refs,
):
    halves, side = refs[:-1], refs[-1]

    def flat(series):
        wide = jnp.dot(
            series, spread[...], precision=lax.Precision.HIGHEST, preferred_element_type=F32
        )
        return jnp.sum(wide * owner[...], axis=0, keepdims=True)

    def repeat(series):
        return jnp.dot(
            series.astype(F32), owner[...],
            precision=lax.Precision.HIGHEST, preferred_element_type=F32,
        )

    action = flat(actions[...].astype(F32))
    obs = jnp.concatenate([half[...] for half in halves], axis=0)
    hidden = jnp.maximum(mm(obs, actor_embed[...]), 0.0).astype(BF16)
    logits = mm(hidden, actor_policy[...]).T
    top = jnp.max(logits, axis=0, keepdims=True)
    shifted = logits - top
    norm = jnp.log(jnp.sum(jnp.exp(shifted), axis=0, keepdims=True))
    onehot = iota(logits.shape, 0) == action.astype(jnp.int32)
    side[...] = jnp.zeros_like(side)
    side[BEHAVE : BEHAVE + 1, :] = (
        jnp.sum(jnp.where(onehot, shifted, 0.0), axis=0, keepdims=True) - norm
    )
    side[ACTION : ACTION + 1, :] = action
    side[REWARD : REWARD + 1, :] = flat(rewards[...])
    side[LENGTH : LENGTH + 1, :] = repeat(lengths[...])
    side[ASSIGN : ASSIGN + 1, :] = repeat(assign[...])
    side[LENGTH_2 : LENGTH_2 + 1, :] = repeat(lengths_2[...])
    side[ASSIGN_2 : ASSIGN_2 + 1, :] = repeat(assign_2[...])


def side_data(spread, owner, halves, *args):
    count = len(args) + 2 + len(halves)
    return pl.pallas_call(
        side_kernel,
        out_shape=jax.ShapeDtypeStruct((8, spread.shape[1]), F32),
        in_specs=[VMEM] * count,
        out_specs=VMEM,
        compiler_params=params(12),
        cost_estimate=cost(1.3),
        name="side",
    )(*args, spread, owner, *halves)


def convert_kernel(master_embed, master_policy, master_value, embed_t, head, head_t):
    embed_t[...] = master_embed[...].T.astype(BF16)
    nact = master_policy.shape[1]
    wide = jnp.concatenate(
        [
            master_policy[...].T,
            master_value[...],
            jnp.zeros((PAD - 1, head_t.shape[1]), F32),
        ],
        axis=0,
    )
    head_t[...] = wide.astype(BF16)
    head[:, 0:nact] = master_policy[...].astype(BF16)
    head[:, nact:] = wide[nact:, :].T.astype(BF16)


def convert(master_embed, master_policy, master_value):
    feats, width = master_embed.shape
    nact = master_policy.shape[1]
    return pl.pallas_call(
        convert_kernel,
        out_shape=(
            jax.ShapeDtypeStruct((width, feats), BF16),
            jax.ShapeDtypeStruct((width, nact + PAD), BF16),
            jax.ShapeDtypeStruct((nact + PAD, width), BF16),
        ),
        in_specs=[VMEM] * 3,
        out_specs=(VMEM,) * 3,
        compiler_params=params(12),
        cost_estimate=cost(0.6),
        name="convert",
    )(master_embed, master_policy, master_value)


def learner_weights(slots, sides, out):
    learners, rows = out.shape[0], sides.shape[1]
    total = jnp.zeros((learners, rows), F32)
    first = lax.rem(iota((1, rows), 1), slots) == 0
    for place in range(0, sides.shape[0], 8):
        for length_at, assign_at in ((LENGTH, ASSIGN), (LENGTH_2, ASSIGN_2)):
            assign = sides[place + assign_at : place + assign_at + 1, :].astype(jnp.int32)
            length = jnp.where(first, sides[place + length_at : place + length_at + 1, :], 0.0)
            total = total + jnp.where(iota((learners, rows), 0) == assign, length, 0.0)
    summed = jnp.sum(total, axis=1, keepdims=True)
    out[...] = jnp.broadcast_to(1.0 / (learners * summed), out.shape)


def vtrace(slots, nact, side, weights, logits, values):
    rows = logits.shape[1]
    learners = weights.shape[0]
    behave = side[BEHAVE : BEHAVE + 1, :]
    reward = side[REWARD : REWARD + 1, :]
    length = side[LENGTH : LENGTH + 1, :].astype(jnp.int32)
    assign = side[ASSIGN : ASSIGN + 1, :].astype(jnp.int32)
    action = side[ACTION : ACTION + 1, :].astype(jnp.int32)
    weight = jnp.sum(
        jnp.where(iota((learners, rows), 0) == assign, weights[:, 0:1], 0.0), axis=0, keepdims=True
    )
    top = jnp.max(logits, axis=0, keepdims=True)
    exps = jnp.exp(logits - top)
    norm = jnp.sum(exps, axis=0, keepdims=True)
    logprob = logits - (top + jnp.log(norm))
    probs = exps * (1.0 / norm)
    onehot = iota(logits.shape, 0) == action
    taken = jnp.sum(jnp.where(onehot, logprob, 0.0), axis=0, keepdims=True)
    entropy = -jnp.sum(probs * logprob, axis=0, keepdims=True)
    step = lax.rem(iota((1, rows), 1), slots)
    inside = (step < length).astype(F32)
    beyond = (step + 1 < length).astype(F32)
    ratios = jnp.minimum(1.0, jnp.exp(taken - behave))

    def later(series, by):
        return pltpu.roll(series, rows - by, 1)

    deltas = inside * ratios * (reward + GAMMA * later(values, 1) * beyond - values)
    decay = GAMMA * ratios * inside
    corrections = deltas
    reach = 1
    while reach < slots:
        within = step + reach < slots
        corrections = corrections + decay * jnp.where(within, later(corrections, reach), 0.0)
        decay = decay * jnp.where(within, later(decay, reach), 0.0)
        reach *= 2
    targets = values + corrections
    advantage = ratios * (reward + GAMMA * later(targets, 1) * beyond - values)
    scale = weight * inside
    grad = scale * (
        -advantage * (onehot.astype(F32) - probs) + ENTROPY_COEF * probs * (logprob + entropy)
    )
    return grad, scale * (values - targets)


def forward(frames, embed_t, head_t, frames_t, hidden_t):
    width = embed_t.shape[0]
    tile = 256
    for index, half in enumerate(frames):
        frames_t[:, index * HALF : (index + 1) * HALF] = half[...].T
    for start in range(0, width, tile):
        here = slice(start, start + tile)
        hidden_t[here, :] = jnp.maximum(mm(embed_t[here, :], frames_t[...]), 0.0).astype(BF16)
    return mm(head_t[...], hidden_t[...])


def backward(slots, logits, side, weights, head, frames_t, hidden_t, preact_t, add):
    width, feats = head.shape[0], frames_t.shape[0]
    nact = logits.shape[0] - PAD
    tile = 256
    grad, grad_values = vtrace(
        slots, nact, side, weights, logits[0:nact, :], logits[nact : nact + 1, :]
    )
    pad = jnp.zeros((PAD - 1, grad.shape[1]), F32)
    grad_t = jnp.concatenate([grad, grad_values, pad], axis=0).astype(BF16)
    for start in range(0, width, tile):
        here = slice(start, start + tile)
        back = mm(head[here, :], grad_t)
        alive = hidden_t[here, :].astype(F32) > 0.0
        preact_t[here, :] = jnp.where(alive, back, 0.0).astype(BF16)
    for index in range(frames_t.shape[1] // BLOCK):
        lanes = slice(index * BLOCK, (index + 1) * BLOCK)
        add(index, slice(0, feats), mm_nt(frames_t[:, lanes], preact_t[:, lanes]))
        add(index, slice(feats, feats + nact + PAD), mm_nt(grad_t[:, lanes], hidden_t[:, lanes]))


def work(slots, frames, side, weights, embed_t, head, head_t, frames_t, hidden_t, preact_t, add):
    logits = forward(frames, embed_t, head_t, frames_t, hidden_t)
    backward(slots, logits, side, weights, head, frames_t, hidden_t, preact_t, add)


def ring_place(hst):
    line, across = lax.div(hst, 2), lax.rem(hst, 2)
    return jnp.where(across == 0, line, 7 - line)


def side_of(sides, step):
    hst = lax.axis_index("hst")
    way = jnp.where(lax.axis_index("cores") == 0, 7, 1)
    there = lax.bitwise_and(ring_place(hst) + way * step, 7)
    chip = jnp.where(there < 4, 2 * there, 2 * (7 - there) + 1)
    mask = lax.bitwise_xor(hst, chip)
    return sides[pl.ds(pl.multiple_of(8 * mask, 8), 8), :]


def ahead_kernel(*refs):
    (*frames, embed_t, head_t, frames_t, hidden_t, logits) = refs
    logits[...] = forward(frames, embed_t, head_t, frames_t, hidden_t)


def ahead(frames, embed_t, head_t):
    width, feats = embed_t.shape
    rows = len(frames) * HALF
    return pl.pallas_call(
        ahead_kernel,
        out_shape=(
            jax.ShapeDtypeStruct((feats, rows), BF16),
            jax.ShapeDtypeStruct((width, rows), BF16),
            jax.ShapeDtypeStruct((head_t.shape[0], rows), F32),
        ),
        in_specs=[VMEM] * (len(frames) + 2),
        out_specs=(VMEM,) * 3,
        compiler_params=params(20),
        cost_estimate=cost(1.6),
        name="ahead",
    )(*frames, embed_t, head_t)


def first_kernel(slots, *refs):
    (frames_t, hidden_t, logits, *pieces), mats, outs, (weights, sides), scratch = (
        refs[0:7], refs[7:10], refs[10:13], refs[13:15], refs[15:18])
    start = 0
    for piece in pieces:
        sides[start : start + piece.shape[0], :] = piece[...]
        start += piece.shape[0]
    learner_weights(slots, sides, weights)

    def add(index, rows, value):
        outs[index][rows, :] = value

    side = jnp.concatenate([side_of(sides, step) for step in (0, 1, 2)], axis=1)
    backward(slots, logits[...], side, weights, mats[1], frames_t, hidden_t, scratch[2], add)


def second_kernel(slots, *refs):
    frames, (sides, weights, sum_0), mats, (sum_04, sum_3), scratch = (
        refs[0:4], refs[4:7], refs[7:10], refs[10:12], refs[12:15])

    def add(index, rows, value):
        if index == 0:
            sum_3[rows, :] = value
        else:
            sum_04[rows, :] = sum_0[rows, :] + value

    side = jnp.concatenate([side_of(sides, 3), side_of(sides, 4)], axis=1)
    work(slots, frames, side, weights, *mats, *scratch, add)


def third_kernel(slots, *refs):
    frames, (sides, weights, sum_04, sum_1, sum_2), mats, (even, sum_15), scratch = (
        refs[0:4], refs[4:9], refs[9:12], refs[12:14], refs[14:17])

    def add(index, rows, value):
        if index == 0:
            sum_15[rows, :] = sum_1[rows, :] + value
        else:
            even[rows, :] = sum_04[rows, :] + (sum_2[rows, :] + value)

    side = jnp.concatenate([side_of(sides, 5), side_of(sides, 6)], axis=1)
    work(slots, frames, side, weights, *mats, *scratch, add)


def fourth_kernel(slots, *refs):
    frames, (sides, weights, even, sum_15, sum_3), mats, out, scratch = (
        refs[0:2], refs[2:7], refs[7:10], refs[10], refs[11:14])

    def add(index, rows, value):
        out[rows, :] = (
            even[rows, :] + (sum_15[rows, :] + (sum_3[rows, :] + value))
        ).astype(BF16)

    work(slots, frames, side_of(sides, 7), weights, *mats, *scratch, add)


def local_kernel(slots, frames, side, weights, embed_t, head, head_t, out, *scratch):
    def add(index, rows, value):
        if index == 0:
            out[rows, :] = value
        else:
            out[rows, :] += value

    halves = [frames.at[index] for index in range(frames.shape[0])]
    work(slots, halves, side, weights, embed_t, head, head_t, *scratch, add)


def call(kernel, name, slots, blocks, args, mats, outs):
    width, feats = mats[0].shape
    rows = blocks * BLOCK
    return pl.pallas_call(
        functools.partial(kernel, slots),
        out_shape=outs,
        in_specs=[VMEM] * (len(args) + 3),
        out_specs=jax.tree.map(lambda leaf: VMEM, outs),
        scratch_shapes=[
            pltpu.VMEM((feats, rows), BF16),
            pltpu.VMEM((width, rows), BF16),
            pltpu.VMEM((width, rows), BF16),
        ],
        compiler_params=params(32),
        cost_estimate=cost(1.2 * blocks + 0.4),
        name=name,
    )(*args, *mats)


def update_kernel(
    feats, nact, mine, theirs, master_embed, master_policy, master_value,
    embed_moment, policy_moment, value_moment, next_obs,
    next_logits, new_embed, new_policy, new_value, new_em, new_pm, new_vm,
):
    def step(grad, moment, master, new_moment, new_master):
        held = MOMENTUM * moment[...] + grad
        new_moment[...] = held
        fresh = master[...] - LEARN_RATE * held
        new_master[...] = fresh
        return fresh

    def grad(start, size):
        return mine[start : start + size, :].astype(F32) + theirs[start : start + size, :].astype(F32)

    embed = step(grad(0, feats), embed_moment, master_embed, new_em, new_embed)
    hidden = jnp.maximum(mm(next_obs[...], embed.astype(BF16)), 0.0).astype(BF16)
    policy = step(grad(feats, nact).T, policy_moment, master_policy, new_pm, new_policy)
    step(grad(feats + nact, PAD)[0:1, :], value_moment, master_value, new_vm, new_value)
    next_logits[...] = mm(hidden, policy.astype(BF16)).astype(BF16)


def update(mine, theirs, *args):
    embed, policy, value = args[0], args[1], args[2]
    next_obs = args[6]
    feats, nact = embed.shape[0], policy.shape[1]
    shapes = [jax.ShapeDtypeStruct(array.shape, F32) for array in (embed, policy, value)]
    return pl.pallas_call(
        functools.partial(update_kernel, feats, nact),
        out_shape=(jax.ShapeDtypeStruct((next_obs.shape[0], nact), BF16), *shapes, *shapes),
        in_specs=[VMEM] * 9,
        out_specs=(VMEM,) * 7,
        compiler_params=params(32),
        cost_estimate=cost(3.4),
        name="update",
    )(mine, theirs, *args)


def gathered_grads(slots, halves, side, mats):
    cycle = [0, 2, 4, 6, 7, 5, 3, 1]
    ring = [
        (2 * cycle[place] + core, 2 * cycle[(place + way) % 8] + core)
        for place in range(8)
        for core, way in ((0, 1), (1, -1))
    ]

    def send(blocks):
        return [lax.ppermute(half, AXES, ring) for half in blocks]

    blocks = [halves]
    for step in range(7):
        blocks.append(send(blocks[-1]))
    pieces = [side]
    for mask in (1, 2, 4):
        held = pieces[0] if mask == 1 else jnp.concatenate(pieces, axis=0)
        pieces.append(lax.ppermute(held, "hst", [(at, at ^ mask) for at in range(8)]))

    width, feats = mats[0].shape
    grads = jax.ShapeDtypeStruct((feats + mats[2].shape[0], width), F32)
    weights = jax.ShapeDtypeStruct((16, 128), F32)
    sides = jax.ShapeDtypeStruct((64, side.shape[1]), F32)
    done = ahead(blocks[0] + blocks[1] + blocks[2], mats[0], mats[2])
    sum_0, sum_1, sum_2, weights, sides = call(
        first_kernel, "first", slots, 3, (*done, *pieces), mats,
        (grads, grads, grads, weights, sides),
    )
    sum_04, sum_3 = call(
        second_kernel, "second", slots, 2, (*blocks[3], *blocks[4], sides, weights, sum_0), mats,
        (grads, grads),
    )
    even, sum_15 = call(
        third_kernel, "third", slots, 2,
        (*blocks[5], *blocks[6], sides, weights, sum_04, sum_1, sum_2), mats, (grads, grads),
    )
    return call(
        fourth_kernel, "fourth", slots, 1, (*blocks[7], sides, weights, even, sum_15, sum_3), mats,
        jax.ShapeDtypeStruct(grads.shape, BF16),
    )


def body(
    n_hst, n_cores, observations, lengths, actions, rewards, assign, actor_embed, actor_policy,
    master_embed, master_policy, master_value, embed_moment, policy_moment, value_moment, next_obs,
):
    traj, slots, feats = observations.shape
    learners = n_hst * n_cores
    rows = traj * slots
    own = observations.reshape(rows, feats)
    value_row = master_value.reshape(1, -1)
    spread, owner = select(traj, slots)
    flip = [(core, core ^ 1) for core in range(n_cores)]
    there = [lax.ppermute(array, "cores", flip) for array in (lengths, assign)]
    gather = n_hst == 8 and n_cores == 2 and rows == BLOCK
    halves = [own[start : start + HALF] for start in range(0, rows, HALF)]
    side = side_data(
        spread, owner, halves, *[array.reshape(1, -1) for array in (lengths, assign, *there)],
        actions, rewards, actor_embed, actor_policy,
    )
    mats = convert(master_embed, master_policy, value_row)
    if gather:
        mine = gathered_grads(slots, halves, side, mats)
        theirs = lax.ppermute(mine, "cores", flip)
    else:
        named = (assign[:, None] == jnp.arange(learners)[None, :]).astype(F32)
        totals = lax.psum(jnp.sum(named * lengths[:, None].astype(F32), axis=0), AXES)
        weights = jnp.broadcast_to((1.0 / (learners * totals))[:, None], (learners, 128))
        grads = call(
            local_kernel, "local", slots, rows // BLOCK,
            (own.reshape(-1, HALF, feats), side, weights), mats,
            jax.ShapeDtypeStruct((feats + mats[2].shape[0], mats[0].shape[0]), F32),
        )
        mine = lax.psum(grads, AXES)
        theirs = jnp.zeros_like(mine)
    outs = update(
        mine, theirs, master_embed, master_policy, value_row, embed_moment, policy_moment,
        value_moment.reshape(1, -1), next_obs,
    )
    logits, new_embed, new_policy, new_value, new_em, new_pm, new_vm = outs
    return logits, new_embed, new_policy, new_value.reshape(-1), new_em, new_pm, new_vm.reshape(-1)


def solution(mesh):
    split = P(("group", "hst", "cores"))
    whole = P("group")
    return jax.shard_map(
        functools.partial(body, mesh.shape["hst"], mesh.shape["cores"]),
        mesh=mesh,
        in_specs=(split,) * 5 + (whole,) * 8 + (split,),
        out_specs=(split,) + (whole,) * 6,
        check_vma=False,
    )
```

```python
import functools

import jax
import jax.numpy as jnp
from jax import lax
from jax.experimental import pallas as pl
from jax.experimental.pallas import tpu as pltpu
from jax.sharding import PartitionSpec as P

GAMMA = 0.99
ENTROPY_COEF = 0.1
MOMENTUM = 0.9
LEARN_RATE = 0.05
AXES = ("hst", "cores")
F32 = jnp.float32
BF16 = jnp.bfloat16
VMEM = pl.BlockSpec(memory_space=pltpu.VMEM)
MIB = 2**20
BLOCK = 256
PAD = 16
BEHAVE, ACTION, REWARD, LENGTH, ASSIGN, LENGTH_2, ASSIGN_2 = range(7)


def iota(shape, dim):
    return lax.broadcasted_iota(jnp.int32, shape, dim)


def mm(a, b):
    return jnp.dot(a, b, preferred_element_type=F32)


def mm_nt(a, b):
    return lax.dot_general(a, b, (((1,), (1,)), ((), ())), preferred_element_type=F32)


def params(mib):
    return pltpu.CompilerParams(vmem_limit_bytes=mib * MIB)


def cost(micros):
    return pl.CostEstimate(flops=int(micros * 1.1e9), bytes_accessed=0, transcendentals=0)


def select_kernel(spread, owner):
    traj, rows = owner.shape
    slots = spread.shape[0]
    spread[...] = (lax.rem(iota((slots, rows), 1), slots) == iota((slots, rows), 0)).astype(F32)
    owner[...] = (lax.div(iota((traj, rows), 1), slots) == iota((traj, rows), 0)).astype(F32)


def select(traj, slots):
    rows = traj * slots
    return pl.pallas_call(
        select_kernel,
        out_shape=(jax.ShapeDtypeStruct((slots, rows), F32), jax.ShapeDtypeStruct((traj, rows), F32)),
        out_specs=(VMEM, VMEM),
        compiler_params=params(4),
        cost_estimate=cost(40),
        name="select",
    )()


def side_kernel(
    lengths, assign, lengths_2, assign_2, actions, rewards, actor_embed, actor_policy,
    spread, owner, obs, side,
):

    def flat(series):
        wide = jnp.dot(
            series, spread[...], precision=lax.Precision.HIGHEST, preferred_element_type=F32
        )
        return jnp.sum(wide * owner[...], axis=0, keepdims=True)

    def repeat(series):
        return jnp.dot(
            series.astype(F32), owner[...],
            precision=lax.Precision.HIGHEST, preferred_element_type=F32,
        )

    action = flat(actions[...].astype(F32))
    hidden = jnp.maximum(mm(obs[...], actor_embed[...]), 0.0).astype(BF16)
    logits = mm(hidden, actor_policy[...]).T
    top = jnp.max(logits, axis=0, keepdims=True)
    shifted = logits - top
    norm = jnp.log(jnp.sum(jnp.exp(shifted), axis=0, keepdims=True))
    onehot = iota(logits.shape, 0) == action.astype(jnp.int32)
    side[...] = jnp.zeros_like(side)
    side[BEHAVE : BEHAVE + 1, :] = (
        jnp.sum(jnp.where(onehot, shifted, 0.0), axis=0, keepdims=True) - norm
    )
    side[ACTION : ACTION + 1, :] = action
    side[REWARD : REWARD + 1, :] = flat(rewards[...])
    side[LENGTH : LENGTH + 1, :] = repeat(lengths[...])
    side[ASSIGN : ASSIGN + 1, :] = repeat(assign[...])
    side[LENGTH_2 : LENGTH_2 + 1, :] = repeat(lengths_2[...])
    side[ASSIGN_2 : ASSIGN_2 + 1, :] = repeat(assign_2[...])


def side_data(spread, owner, obs, *args):
    count = len(args) + 3
    return pl.pallas_call(
        side_kernel,
        out_shape=jax.ShapeDtypeStruct((8, spread.shape[1]), F32),
        in_specs=[VMEM] * count,
        out_specs=VMEM,
        compiler_params=params(12),
        cost_estimate=cost(1.3),
        name="side",
    )(*args, spread, owner, obs)


def convert_kernel(master_embed, master_policy, master_value, embed_t, head, head_t):
    embed_t[...] = master_embed[...].T.astype(BF16)
    nact = master_policy.shape[1]
    wide = jnp.concatenate(
        [
            master_policy[...].T,
            master_value[...],
            jnp.zeros((PAD - 1, head_t.shape[1]), F32),
        ],
        axis=0,
    )
    head_t[...] = wide.astype(BF16)
    head[:, 0:nact] = master_policy[...].astype(BF16)
    head[:, nact:] = wide[nact:, :].T.astype(BF16)


def convert(master_embed, master_policy, master_value):
    feats, width = master_embed.shape
    nact = master_policy.shape[1]
    return pl.pallas_call(
        convert_kernel,
        out_shape=(
            jax.ShapeDtypeStruct((width, feats), BF16),
            jax.ShapeDtypeStruct((width, nact + PAD), BF16),
            jax.ShapeDtypeStruct((nact + PAD, width), BF16),
        ),
        in_specs=[VMEM] * 3,
        out_specs=(VMEM,) * 3,
        compiler_params=params(12),
        cost_estimate=cost(0.6),
        name="convert",
    )(master_embed, master_policy, master_value)


def learner_weights(slots, sides, out):
    learners, rows = out.shape[0], sides.shape[1]
    total = jnp.zeros((learners, rows), F32)
    first = lax.rem(iota((1, rows), 1), slots) == 0
    for place in range(0, sides.shape[0], 8):
        for length_at, assign_at in ((LENGTH, ASSIGN), (LENGTH_2, ASSIGN_2)):
            assign = sides[place + assign_at : place + assign_at + 1, :].astype(jnp.int32)
            length = jnp.where(first, sides[place + length_at : place + length_at + 1, :], 0.0)
            total = total + jnp.where(iota((learners, rows), 0) == assign, length, 0.0)
    summed = jnp.sum(total, axis=1, keepdims=True)
    out[...] = jnp.broadcast_to(1.0 / (learners * summed), out.shape)


def vtrace(slots, nact, side, weights, logits, values):
    rows = logits.shape[1]
    learners = weights.shape[0]
    behave = side[BEHAVE : BEHAVE + 1, :]
    reward = side[REWARD : REWARD + 1, :]
    length = side[LENGTH : LENGTH + 1, :].astype(jnp.int32)
    assign = side[ASSIGN : ASSIGN + 1, :].astype(jnp.int32)
    action = side[ACTION : ACTION + 1, :].astype(jnp.int32)
    weight = jnp.sum(
        jnp.where(iota((learners, rows), 0) == assign, weights[:, 0:1], 0.0), axis=0, keepdims=True
    )
    top = jnp.max(logits, axis=0, keepdims=True)
    exps = jnp.exp(logits - top)
    norm = jnp.sum(exps, axis=0, keepdims=True)
    logprob = logits - (top + jnp.log(norm))
    probs = exps * (1.0 / norm)
    onehot = iota(logits.shape, 0) == action
    taken = jnp.sum(jnp.where(onehot, logprob, 0.0), axis=0, keepdims=True)
    entropy = -jnp.sum(probs * logprob, axis=0, keepdims=True)
    step = lax.rem(iota((1, rows), 1), slots)
    inside = (step < length).astype(F32)
    beyond = (step + 1 < length).astype(F32)
    ratios = jnp.minimum(1.0, jnp.exp(taken - behave))

    def later(series, by):
        return pltpu.roll(series, rows - by, 1)

    deltas = inside * ratios * (reward + GAMMA * later(values, 1) * beyond - values)
    decay = GAMMA * ratios * inside
    corrections = deltas
    reach = 1
    while reach < slots:
        within = step + reach < slots
        corrections = corrections + decay * jnp.where(within, later(corrections, reach), 0.0)
        decay = decay * jnp.where(within, later(decay, reach), 0.0)
        reach *= 2
    targets = values + corrections
    advantage = ratios * (reward + GAMMA * later(targets, 1) * beyond - values)
    scale = weight * inside
    grad = scale * (
        -advantage * (onehot.astype(F32) - probs) + ENTROPY_COEF * probs * (logprob + entropy)
    )
    return grad, scale * (values - targets)


def forward(frames, embed_t, head_t, frames_t, hidden_t):
    width = embed_t.shape[0]
    tile = 256
    for index, block in enumerate(frames):
        frames_t[:, index * BLOCK : (index + 1) * BLOCK] = block[...].T
    for start in range(0, width, tile):
        here = slice(start, start + tile)
        hidden_t[here, :] = jnp.maximum(mm(embed_t[here, :], frames_t[...]), 0.0).astype(BF16)
    return mm(head_t[...], hidden_t[...])


def backward(slots, logits, side, weights, head, frames_t, hidden_t, preact_t, add):
    width, feats = head.shape[0], frames_t.shape[0]
    nact = logits.shape[0] - PAD
    tile = 256
    grad, grad_values = vtrace(
        slots, nact, side, weights, logits[0:nact, :], logits[nact : nact + 1, :]
    )
    pad = jnp.zeros((PAD - 1, grad.shape[1]), F32)
    grad_t = jnp.concatenate([grad, grad_values, pad], axis=0).astype(BF16)
    for start in range(0, width, tile):
        here = slice(start, start + tile)
        back = mm(head[here, :], grad_t)
        alive = hidden_t[here, :].astype(F32) > 0.0
        preact_t[here, :] = jnp.where(alive, back, 0.0).astype(BF16)
    for index in range(frames_t.shape[1] // BLOCK):
        lanes = slice(index * BLOCK, (index + 1) * BLOCK)
        add(index, slice(0, feats), mm_nt(frames_t[:, lanes], preact_t[:, lanes]))
        add(index, slice(feats, feats + nact + PAD), mm_nt(grad_t[:, lanes], hidden_t[:, lanes]))


def work(slots, frames, side, weights, embed_t, head, head_t, frames_t, hidden_t, preact_t, add):
    logits = forward(frames, embed_t, head_t, frames_t, hidden_t)
    backward(slots, logits, side, weights, head, frames_t, hidden_t, preact_t, add)


def side_of(sides, back, flip):
    line = lax.div(lax.axis_index("hst"), 2)
    there = lax.bitwise_xor(line, lax.bitwise_and(line + 4 - back, 3))
    return sides[pl.ds(pl.multiple_of(8 * (4 * flip + there), 8), 8), :]


def ahead_kernel(*refs):
    (*frames, embed_t, head_t, frames_t, hidden_t, logits) = refs
    logits[...] = forward(frames, embed_t, head_t, frames_t, hidden_t)


def ahead(frames, embed_t, head_t):
    width, feats = embed_t.shape
    rows = len(frames) * BLOCK
    return pl.pallas_call(
        ahead_kernel,
        out_shape=(
            jax.ShapeDtypeStruct((feats, rows), BF16),
            jax.ShapeDtypeStruct((width, rows), BF16),
            jax.ShapeDtypeStruct((head_t.shape[0], rows), F32),
        ),
        in_specs=[VMEM] * (len(frames) + 2),
        out_specs=(VMEM,) * 3,
        compiler_params=params(20),
        cost_estimate=cost(0.1),
        name="ahead",
    )(*frames, embed_t, head_t)


def first_kernel(slots, *refs):
    (frames_t, hidden_t, logits, *pieces), mats, (sum_0, sum_1, weights, sides), scratch = (
        refs[0:5], refs[5:8], refs[8:12], refs[12:15])
    start = 0
    for piece in pieces:
        sides[start : start + piece.shape[0], :] = piece[...]
        start += piece.shape[0]
    learner_weights(slots, sides, weights)

    def add(index, rows, value):
        if index == 0:
            sum_0[rows, :] = value
        elif index == 1:
            sum_0[rows, :] += value
        else:
            sum_1[rows, :] = value

    side = jnp.concatenate([side_of(sides, *at) for at in ((0, 0), (0, 1), (1, 0))], axis=1)
    backward(slots, logits[...], side, weights, mats[1], frames_t, hidden_t, scratch[2], add)


def second_kernel(slots, *refs):
    frames, (sides, weights, sum_1), mats, (sum_1y, sum_2), scratch = (
        refs[0:2], refs[2:5], refs[5:8], refs[8:10], refs[10:13])

    def add(index, rows, value):
        if index == 0:
            sum_1y[rows, :] = sum_1[rows, :] + value
        else:
            sum_2[rows, :] = value

    side = jnp.concatenate([side_of(sides, 1, 1), side_of(sides, 2, 0)], axis=1)
    work(slots, frames, side, weights, *mats, *scratch, add)


def third_kernel(slots, *refs):
    frames, (sides, weights, sum_0, sum_2), mats, (even, sum_3), scratch = (
        refs[0:2], refs[2:6], refs[6:9], refs[9:11], refs[11:14])

    def add(index, rows, value):
        if index == 0:
            even[rows, :] = sum_0[rows, :] + (sum_2[rows, :] + value)
        else:
            sum_3[rows, :] = value

    side = jnp.concatenate([side_of(sides, 2, 1), side_of(sides, 3, 0)], axis=1)
    work(slots, frames, side, weights, *mats, *scratch, add)


def fourth_kernel(slots, *refs):
    frames, (sides, weights, even, sum_1y, sum_3), mats, out, scratch = (
        refs[0:1], refs[1:6], refs[6:9], refs[9], refs[10:13])

    def add(index, rows, value):
        out[rows, :] = (
            even[rows, :] + (sum_1y[rows, :] + (sum_3[rows, :] + value))
        ).astype(BF16)

    work(slots, frames, side_of(sides, 3, 1), weights, *mats, *scratch, add)


def local_kernel(slots, frames, side, weights, embed_t, head, head_t, out, *scratch):
    def add(index, rows, value):
        if index == 0:
            out[rows, :] = value
        else:
            out[rows, :] += value

    blocks = [frames.at[index] for index in range(frames.shape[0])]
    work(slots, blocks, side, weights, embed_t, head, head_t, *scratch, add)


def call(kernel, name, slots, blocks, args, mats, outs):
    width, feats = mats[0].shape
    rows = blocks * BLOCK
    return pl.pallas_call(
        functools.partial(kernel, slots),
        out_shape=outs,
        in_specs=[VMEM] * (len(args) + 3),
        out_specs=jax.tree.map(lambda leaf: VMEM, outs),
        scratch_shapes=[
            pltpu.VMEM((feats, rows), BF16),
            pltpu.VMEM((width, rows), BF16),
            pltpu.VMEM((width, rows), BF16),
        ],
        compiler_params=params(32),
        cost_estimate=cost(1.2 * blocks + 0.4),
        name=name,
    )(*args, *mats)


def update_kernel(
    feats, nact, mine, theirs, master_embed, master_policy, master_value,
    embed_moment, policy_moment, value_moment, next_obs,
    next_logits, new_embed, new_policy, new_value, new_em, new_pm, new_vm,
):
    def step(grad, moment, master, new_moment, new_master):
        held = MOMENTUM * moment[...] + grad
        new_moment[...] = held
        fresh = master[...] - LEARN_RATE * held
        new_master[...] = fresh
        return fresh

    def grad(start, size):
        return mine[start : start + size, :].astype(F32) + theirs[start : start + size, :].astype(F32)

    embed = step(grad(0, feats), embed_moment, master_embed, new_em, new_embed)
    hidden = jnp.maximum(mm(next_obs[...], embed.astype(BF16)), 0.0).astype(BF16)
    policy = step(grad(feats, nact).T, policy_moment, master_policy, new_pm, new_policy)
    step(grad(feats + nact, PAD)[0:1, :], value_moment, master_value, new_vm, new_value)
    next_logits[...] = mm(hidden, policy.astype(BF16)).astype(BF16)


def update(mine, theirs, *args):
    embed, policy, value = args[0], args[1], args[2]
    next_obs = args[6]
    feats, nact = embed.shape[0], policy.shape[1]
    shapes = [jax.ShapeDtypeStruct(array.shape, F32) for array in (embed, policy, value)]
    return pl.pallas_call(
        functools.partial(update_kernel, feats, nact),
        out_shape=(jax.ShapeDtypeStruct((next_obs.shape[0], nact), BF16), *shapes, *shapes),
        in_specs=[VMEM] * 9,
        out_specs=(VMEM,) * 7,
        compiler_params=params(32),
        cost_estimate=cost(3.4),
        name="update",
    )(mine, theirs, *args)


def gathered_grads(slots, own, side, mats):
    def exchange(array, mask):
        return lax.ppermute(array, "hst", [(at, at ^ mask) for at in range(8)])

    def shift(array, by):
        return lax.ppermute(array, "hst", [(at, (at + 2 * by) % 8) for at in range(8)])

    one = shift(own, 1)
    own_y = exchange(own, 1)
    pieces = [side] + [exchange(side, 2 * mask) for mask in (1, 2, 3)]
    line = jnp.concatenate(pieces, axis=0)
    line, one, again = lax.optimization_barrier((line, one, own))
    line_y = exchange(line, 1)
    three = shift(again, -1)
    one_y = exchange(one, 1)
    two = shift(one, 1)
    three_y = exchange(three, 1)
    two_y = exchange(two, 1)

    width, feats = mats[0].shape
    grads = jax.ShapeDtypeStruct((feats + mats[2].shape[0], width), F32)
    weights = jax.ShapeDtypeStruct((16, 128), F32)
    sides = jax.ShapeDtypeStruct((64, side.shape[1]), F32)
    done = ahead((own, own_y, one), mats[0], mats[2])
    sum_0, sum_1, weights, sides = call(
        first_kernel, "first", slots, 3, (*done, line, line_y), mats,
        (grads, grads, weights, sides),
    )
    sum_1y, sum_2 = call(
        second_kernel, "second", slots, 2, (one_y, two, sides, weights, sum_1), mats,
        (grads, grads),
    )
    even, sum_3 = call(
        third_kernel, "third", slots, 2, (two_y, three, sides, weights, sum_0, sum_2), mats,
        (grads, grads),
    )
    return call(
        fourth_kernel, "fourth", slots, 1, (three_y, sides, weights, even, sum_1y, sum_3), mats,
        jax.ShapeDtypeStruct(grads.shape, BF16),
    )


def body(
    n_hst, n_cores, observations, lengths, actions, rewards, assign, actor_embed, actor_policy,
    master_embed, master_policy, master_value, embed_moment, policy_moment, value_moment, next_obs,
):
    traj, slots, feats = observations.shape
    learners = n_hst * n_cores
    rows = traj * slots
    own = observations.reshape(rows, feats)
    value_row = master_value.reshape(1, -1)
    spread, owner = select(traj, slots)
    flip = [(core, core ^ 1) for core in range(n_cores)]
    there = [lax.ppermute(array, "cores", flip) for array in (lengths, assign)]
    gather = n_hst == 8 and n_cores == 2 and rows == BLOCK
    side = side_data(
        spread, owner, own, *[array.reshape(1, -1) for array in (lengths, assign, *there)],
        actions, rewards, actor_embed, actor_policy,
    )
    mats = convert(master_embed, master_policy, value_row)
    side, mats = lax.optimization_barrier((side, mats))
    if gather:
        mine = gathered_grads(slots, own, side, mats)
        theirs = lax.ppermute(mine, "cores", flip)
    else:
        named = (assign[:, None] == jnp.arange(learners)[None, :]).astype(F32)
        totals = lax.psum(jnp.sum(named * lengths[:, None].astype(F32), axis=0), AXES)
        weights = jnp.broadcast_to((1.0 / (learners * totals))[:, None], (learners, 128))
        grads = call(
            local_kernel, "local", slots, rows // BLOCK,
            (own.reshape(-1, BLOCK, feats), side, weights), mats,
            jax.ShapeDtypeStruct((feats + mats[2].shape[0], mats[0].shape[0]), F32),
        )
        mine = lax.psum(grads, AXES)
        theirs = jnp.zeros_like(mine)
    outs = update(
        mine, theirs, master_embed, master_policy, value_row, embed_moment, policy_moment,
        value_moment.reshape(1, -1), next_obs,
    )
    logits, new_embed, new_policy, new_value, new_em, new_pm, new_vm = outs
    return logits, new_embed, new_policy, new_value.reshape(-1), new_em, new_pm, new_vm.reshape(-1)


def solution(mesh):
    split = P(("group", "hst", "cores"))
    whole = P("group")
    return jax.shard_map(
        functools.partial(body, mesh.shape["hst"], mesh.shape["cores"]),
        mesh=mesh,
        in_specs=(split,) * 5 + (whole,) * 8 + (split,),
        out_specs=(split,) + (whole,) * 6,
        check_vma=False,
    )
```

```python
import functools

import jax
import jax.numpy as jnp
from jax import lax
from jax.experimental import pallas as pl
from jax.experimental.pallas import tpu as pltpu
from jax.sharding import PartitionSpec as P

GAMMA = 0.99
ENTROPY_COEF = 0.1
MOMENTUM = 0.9
LEARN_RATE = 0.05
AXES = ("hst", "cores")
F32 = jnp.float32
BF16 = jnp.bfloat16
VMEM = pl.BlockSpec(memory_space=pltpu.VMEM)
MIB = 2**20
BLOCK = 256
PAD = 16
CHUNKS = 4
BEHAVE, ACTION, REWARD, LENGTH, ASSIGN, LENGTH_2, ASSIGN_2 = range(7)


def iota(shape, dim):
    return lax.broadcasted_iota(jnp.int32, shape, dim)


def mm(a, b):
    return jnp.dot(a, b, preferred_element_type=F32)


def mm_nt(a, b):
    return lax.dot_general(a, b, (((1,), (1,)), ((), ())), preferred_element_type=F32)


def params(mib):
    return pltpu.CompilerParams(vmem_limit_bytes=mib * MIB)


def cost(micros):
    return pl.CostEstimate(flops=int(micros * 1.1e9), bytes_accessed=0, transcendentals=0)


def select_kernel(spread, owner):
    traj, rows = owner.shape
    slots = spread.shape[0]
    spread[...] = (lax.rem(iota((slots, rows), 1), slots) == iota((slots, rows), 0)).astype(F32)
    owner[...] = (lax.div(iota((traj, rows), 1), slots) == iota((traj, rows), 0)).astype(F32)


def select(traj, slots):
    rows = traj * slots
    return pl.pallas_call(
        select_kernel,
        out_shape=(jax.ShapeDtypeStruct((slots, rows), F32), jax.ShapeDtypeStruct((traj, rows), F32)),
        out_specs=(VMEM, VMEM),
        compiler_params=params(4),
        cost_estimate=cost(40),
        name="select",
    )()


def side_kernel(
    lengths, assign, lengths_2, assign_2, actions, rewards, actor_embed, actor_policy,
    spread, owner, obs, side,
):

    def flat(series):
        wide = jnp.dot(
            series, spread[...], precision=lax.Precision.HIGHEST, preferred_element_type=F32
        )
        return jnp.sum(wide * owner[...], axis=0, keepdims=True)

    def repeat(series):
        return jnp.dot(
            series.astype(F32), owner[...],
            precision=lax.Precision.HIGHEST, preferred_element_type=F32,
        )

    action = flat(actions[...].astype(F32))
    hidden = jnp.maximum(mm(obs[...], actor_embed[...]), 0.0).astype(BF16)
    logits = mm(hidden, actor_policy[...]).T
    top = jnp.max(logits, axis=0, keepdims=True)
    shifted = logits - top
    norm = jnp.log(jnp.sum(jnp.exp(shifted), axis=0, keepdims=True))
    onehot = iota(logits.shape, 0) == action.astype(jnp.int32)
    side[...] = jnp.zeros_like(side)
    side[BEHAVE : BEHAVE + 1, :] = (
        jnp.sum(jnp.where(onehot, shifted, 0.0), axis=0, keepdims=True) - norm
    )
    side[ACTION : ACTION + 1, :] = action
    side[REWARD : REWARD + 1, :] = flat(rewards[...])
    side[LENGTH : LENGTH + 1, :] = repeat(lengths[...])
    side[ASSIGN : ASSIGN + 1, :] = repeat(assign[...])
    side[LENGTH_2 : LENGTH_2 + 1, :] = repeat(lengths_2[...])
    side[ASSIGN_2 : ASSIGN_2 + 1, :] = repeat(assign_2[...])


def side_data(spread, owner, obs, *args):
    count = len(args) + 3
    return pl.pallas_call(
        side_kernel,
        out_shape=jax.ShapeDtypeStruct((8, spread.shape[1]), F32),
        in_specs=[VMEM] * count,
        out_specs=VMEM,
        compiler_params=params(12),
        cost_estimate=cost(1.3),
        name="side",
    )(*args, spread, owner, obs)


def convert_kernel(master_embed, master_policy, master_value, embed_t, head, head_t):
    embed_t[...] = master_embed[...].T.astype(BF16)
    nact = master_policy.shape[1]
    wide = jnp.concatenate(
        [
            master_policy[...].T,
            master_value[...],
            jnp.zeros((PAD - 1, head_t.shape[1]), F32),
        ],
        axis=0,
    )
    head_t[...] = wide.astype(BF16)
    head[:, 0:nact] = master_policy[...].astype(BF16)
    head[:, nact:] = wide[nact:, :].T.astype(BF16)


def convert(master_embed, master_policy, master_value):
    feats, width = master_embed.shape
    nact = master_policy.shape[1]
    return pl.pallas_call(
        convert_kernel,
        out_shape=(
            jax.ShapeDtypeStruct((width, feats), BF16),
            jax.ShapeDtypeStruct((width, nact + PAD), BF16),
            jax.ShapeDtypeStruct((nact + PAD, width), BF16),
        ),
        in_specs=[VMEM] * 3,
        out_specs=(VMEM,) * 3,
        compiler_params=params(12),
        cost_estimate=cost(0.6),
        name="convert",
    )(master_embed, master_policy, master_value)


def learner_weights(slots, sides, out):
    learners, rows = out.shape[0], sides.shape[1]
    total = jnp.zeros((learners, rows), F32)
    first = lax.rem(iota((1, rows), 1), slots) == 0
    for place in range(0, sides.shape[0], 8):
        for length_at, assign_at in ((LENGTH, ASSIGN), (LENGTH_2, ASSIGN_2)):
            assign = sides[place + assign_at : place + assign_at + 1, :].astype(jnp.int32)
            length = jnp.where(first, sides[place + length_at : place + length_at + 1, :], 0.0)
            total = total + jnp.where(iota((learners, rows), 0) == assign, length, 0.0)
    summed = jnp.sum(total, axis=1, keepdims=True)
    out[...] = jnp.broadcast_to(1.0 / (learners * summed), out.shape)


def vtrace(slots, nact, side, weights, logits, values):
    rows = logits.shape[1]
    learners = weights.shape[0]
    behave = side[BEHAVE : BEHAVE + 1, :]
    reward = side[REWARD : REWARD + 1, :]
    length = side[LENGTH : LENGTH + 1, :].astype(jnp.int32)
    assign = side[ASSIGN : ASSIGN + 1, :].astype(jnp.int32)
    action = side[ACTION : ACTION + 1, :].astype(jnp.int32)
    weight = jnp.sum(
        jnp.where(iota((learners, rows), 0) == assign, weights[:, 0:1], 0.0), axis=0, keepdims=True
    )
    top = jnp.max(logits, axis=0, keepdims=True)
    exps = jnp.exp(logits - top)
    norm = jnp.sum(exps, axis=0, keepdims=True)
    logprob = logits - (top + jnp.log(norm))
    probs = exps * (1.0 / norm)
    onehot = iota(logits.shape, 0) == action
    taken = jnp.sum(jnp.where(onehot, logprob, 0.0), axis=0, keepdims=True)
    entropy = -jnp.sum(probs * logprob, axis=0, keepdims=True)
    step = lax.rem(iota((1, rows), 1), slots)
    inside = (step < length).astype(F32)
    beyond = (step + 1 < length).astype(F32)
    ratios = jnp.minimum(1.0, jnp.exp(taken - behave))

    def later(series, by):
        return pltpu.roll(series, rows - by, 1)

    deltas = inside * ratios * (reward + GAMMA * later(values, 1) * beyond - values)
    decay = GAMMA * ratios * inside
    corrections = deltas
    reach = 1
    while reach < slots:
        within = step + reach < slots
        corrections = corrections + decay * jnp.where(within, later(corrections, reach), 0.0)
        decay = decay * jnp.where(within, later(decay, reach), 0.0)
        reach *= 2
    targets = values + corrections
    advantage = ratios * (reward + GAMMA * later(targets, 1) * beyond - values)
    scale = weight * inside
    grad = scale * (
        -advantage * (onehot.astype(F32) - probs) + ENTROPY_COEF * probs * (logprob + entropy)
    )
    return grad, scale * (values - targets)


def forward(frames, embed_t, head_t, frames_t, hidden_t):
    width = embed_t.shape[0]
    tile = 256
    for index, block in enumerate(frames):
        frames_t[:, index * BLOCK : (index + 1) * BLOCK] = block[...].T
    for start in range(0, width, tile):
        here = slice(start, start + tile)
        hidden_t[here, :] = jnp.maximum(mm(embed_t[here, :], frames_t[...]), 0.0).astype(BF16)
    return mm(head_t[...], hidden_t[...])


def backward(slots, logits, side, weights, head, frames_t, hidden_t, preact_t, add):
    width, feats = head.shape[0], frames_t.shape[0]
    nact = logits.shape[0] - PAD
    tile = 256
    grad, grad_values = vtrace(
        slots, nact, side, weights, logits[0:nact, :], logits[nact : nact + 1, :]
    )
    pad = jnp.zeros((PAD - 1, grad.shape[1]), F32)
    grad_t = jnp.concatenate([grad, grad_values, pad], axis=0).astype(BF16)
    for start in range(0, width, tile):
        here = slice(start, start + tile)
        back = mm(head[here, :], grad_t)
        alive = hidden_t[here, :].astype(F32) > 0.0
        preact_t[here, :] = jnp.where(alive, back, 0.0).astype(BF16)
    for index in range(frames_t.shape[1] // BLOCK):
        lanes = slice(index * BLOCK, (index + 1) * BLOCK)
        add(index, slice(0, feats), mm_nt(frames_t[:, lanes], preact_t[:, lanes]))
        add(index, slice(feats, feats + nact + PAD), mm_nt(grad_t[:, lanes], hidden_t[:, lanes]))


def work(slots, frames, side, weights, embed_t, head, head_t, frames_t, hidden_t, preact_t, add):
    logits = forward(frames, embed_t, head_t, frames_t, hidden_t)
    backward(slots, logits, side, weights, head, frames_t, hidden_t, preact_t, add)


def side_of(sides, back, flip):
    line = lax.div(lax.axis_index("hst"), 2)
    there = lax.bitwise_xor(line, lax.bitwise_and(line + 4 - back, 3))
    return sides[pl.ds(pl.multiple_of(8 * (4 * flip + there), 8), 8), :]


def ahead_kernel(*refs):
    (*frames, embed_t, head_t, frames_t, hidden_t, logits) = refs
    logits[...] = forward(frames, embed_t, head_t, frames_t, hidden_t)


def ahead(frames, embed_t, head_t):
    width, feats = embed_t.shape
    rows = len(frames) * BLOCK
    return pl.pallas_call(
        ahead_kernel,
        out_shape=(
            jax.ShapeDtypeStruct((feats, rows), BF16),
            jax.ShapeDtypeStruct((width, rows), BF16),
            jax.ShapeDtypeStruct((head_t.shape[0], rows), F32),
        ),
        in_specs=[VMEM] * (len(frames) + 2),
        out_specs=(VMEM,) * 3,
        compiler_params=params(20),
        cost_estimate=cost(0.2),
        name="ahead",
    )(*frames, embed_t, head_t)


def first_kernel(slots, *refs):
    (frames_t, hidden_t, logits, *pieces), mats, (sum_0, sum_1, weights, sides), scratch = (
        refs[0:5], refs[5:8], refs[8:12], refs[12:15])
    start = 0
    for piece in pieces:
        sides[start : start + piece.shape[0], :] = piece[...]
        start += piece.shape[0]
    learner_weights(slots, sides, weights)

    def add(index, rows, value):
        if index == 0:
            sum_0[rows, :] = value
        elif index == 1:
            sum_0[rows, :] += value
        else:
            sum_1[rows, :] = value

    side = jnp.concatenate([side_of(sides, *at) for at in ((0, 0), (0, 1), (1, 0))], axis=1)
    backward(slots, logits[...], side, weights, mats[1], frames_t, hidden_t, scratch[2], add)


def second_kernel(slots, *refs):
    frames, (sides, weights, sum_1), mats, (sum_1y, sum_3), scratch = (
        refs[0:2], refs[2:5], refs[5:8], refs[8:10], refs[10:13])

    def add(index, rows, value):
        if index == 0:
            sum_1y[rows, :] = sum_1[rows, :] + value
        else:
            sum_3[rows, :] = value

    side = jnp.concatenate([side_of(sides, 1, 1), side_of(sides, 3, 0)], axis=1)
    work(slots, frames, side, weights, *mats, *scratch, add)


def third_kernel(slots, *refs):
    frames, (sides, weights, sum_1y, sum_3), mats, (odd, sum_2), scratch = (
        refs[0:2], refs[2:6], refs[6:9], refs[9:11], refs[11:14])

    def add(index, rows, value):
        if index == 0:
            odd[rows, :] = sum_1y[rows, :] + (sum_3[rows, :] + value)
        else:
            sum_2[rows, :] = value

    side = jnp.concatenate([side_of(sides, 3, 1), side_of(sides, 2, 0)], axis=1)
    work(slots, frames, side, weights, *mats, *scratch, add)


def fourth_kernel(slots, *refs):
    frames, (sides, weights, odd, sum_0, sum_2), mats, out, scratch = (
        refs[0:1], refs[1:6], refs[6:9], refs[9], refs[10:13])

    def add(index, rows, value):
        out[rows, :] = (
            odd[rows, :] + (sum_0[rows, :] + (sum_2[rows, :] + value))
        ).astype(BF16)

    work(slots, frames, side_of(sides, 2, 1), weights, *mats, *scratch, add)


def local_kernel(slots, frames, side, weights, embed_t, head, head_t, out, *scratch):
    def add(index, rows, value):
        if index == 0:
            out[rows, :] = value
        else:
            out[rows, :] += value

    blocks = [frames.at[index] for index in range(frames.shape[0])]
    work(slots, blocks, side, weights, embed_t, head, head_t, *scratch, add)


def call(kernel, name, slots, blocks, args, mats, outs):
    width, feats = mats[0].shape
    rows = blocks * BLOCK
    return pl.pallas_call(
        functools.partial(kernel, slots),
        out_shape=outs,
        in_specs=[VMEM] * (len(args) + 3),
        out_specs=jax.tree.map(lambda leaf: VMEM, outs),
        scratch_shapes=[
            pltpu.VMEM((feats, rows), BF16),
            pltpu.VMEM((width, rows), BF16),
            pltpu.VMEM((width, rows), BF16),
        ],
        compiler_params=params(32),
        cost_estimate=cost(1.2 * blocks + 0.4),
        name=name,
    )(*args, *mats)


def update_kernel(
    feats, nact, mine, theirs, master_embed, master_policy, master_value,
    embed_moment, policy_moment, value_moment, next_obs,
    next_logits, new_embed_at, new_policy_at, new_value, new_em_at, new_pm_at, new_vm,
    new_embed, new_policy, new_em, new_pm, sems,
):
    copies = []

    def store(source, target, rows):
        copy = pltpu.make_async_copy(source.at[rows, :], target.at[rows, :], sems.at[len(copies)])
        copy.start()
        copies.append(copy)

    def grad(start, size):
        return mine[start : start + size, :].astype(F32) + theirs[start : start + size, :].astype(F32)

    def step(grad, moment, master):
        held = MOMENTUM * moment + grad
        return held, master - LEARN_RATE * held

    def chunks(height):
        return [pl.ds(start, height // CHUNKS) for start in range(0, height, height // CHUNKS)]

    preact = None
    for rows in chunks(feats):
        held, fresh = step(grad(rows.start, rows.size), embed_moment[rows, :], master_embed[rows, :])
        new_em[rows, :] = held
        new_embed[rows, :] = fresh
        store(new_em, new_em_at, rows)
        store(new_embed, new_embed_at, rows)
        part = mm(next_obs[:, rows], fresh.astype(BF16))
        preact = part if preact is None else preact + part
    policy_grad = grad(feats, nact).T
    held, fresh = step(policy_grad, policy_moment[...], master_policy[...])
    new_pm[...] = held
    new_policy[...] = fresh
    every = pl.ds(0, new_pm.shape[0])
    store(new_pm, new_pm_at, every)
    store(new_policy, new_policy_at, every)
    new_vm[...], new_value[...] = step(
        grad(feats + nact, PAD)[0:1, :], value_moment[...], master_value[...]
    )
    hidden = jnp.maximum(preact, 0.0).astype(BF16)
    next_logits[...] = mm(hidden, fresh.astype(BF16)).astype(BF16)
    for copy in copies:
        copy.wait()


def update(mine, theirs, *args):
    embed, policy, value = args[0], args[1], args[2]
    next_obs = args[6]
    feats, nact = embed.shape[0], policy.shape[1]
    shapes = [jax.ShapeDtypeStruct(array.shape, F32) for array in (embed, policy, value)]
    anywhere = pl.BlockSpec(memory_space=pl.ANY)
    specs = (anywhere, anywhere, VMEM)
    held = [pltpu.VMEM(array.shape, F32) for array in (embed, policy)]
    return pl.pallas_call(
        functools.partial(update_kernel, feats, nact),
        out_shape=(jax.ShapeDtypeStruct((next_obs.shape[0], nact), BF16), *shapes, *shapes),
        in_specs=[VMEM] * 9,
        out_specs=(VMEM, *specs, *specs),
        scratch_shapes=[*held, *held, pltpu.SemaphoreType.DMA((2 * CHUNKS + 2,))],
        compiler_params=params(24),
        cost_estimate=cost(3.4),
        name="update",
    )(mine, theirs, *args)


def gathered_grads(slots, own, side, mats):
    def exchange(array, mask, name):
        with jax.named_scope(name):
            return lax.ppermute(array, "hst", [(at, at ^ mask) for at in range(8)])

    def shift(array, by, name):
        with jax.named_scope(name):
            return lax.ppermute(array, "hst", [(at, (at + 2 * by) % 8) for at in range(8)])

    one = shift(own, 1, "one")
    own_y = exchange(own, 1, "own_y")
    pieces = [side] + [exchange(side, 2 * mask, "side_z") for mask in (1, 2, 3)]
    line = jnp.concatenate(pieces, axis=0)
    line, _ = lax.optimization_barrier((line, side))
    one, _ = lax.optimization_barrier((one, pieces[1]))
    again, _ = lax.optimization_barrier((own, pieces[1]))
    line_y = exchange(line, 1, "side_y")
    three = shift(again, -1, "three")
    one_y = exchange(one, 1, "one_y")
    two = shift(one, 1, "two")
    three_y = exchange(three, 1, "three_y")

    width, feats = mats[0].shape
    grads = jax.ShapeDtypeStruct((feats + mats[2].shape[0], width), F32)
    weights = jax.ShapeDtypeStruct((16, 128), F32)
    sides = jax.ShapeDtypeStruct((64, side.shape[1]), F32)
    done = ahead((own, own_y, one), mats[0], mats[2])
    sum_0, sum_1, weights, sides = call(
        first_kernel, "first", slots, 3, (*done, line, line_y), mats,
        (grads, grads, weights, sides),
    )
    sum_1y, sum_3 = call(
        second_kernel, "second", slots, 2, (one_y, three, sides, weights, sum_1), mats,
        (grads, grads),
    )
    two, sum_3 = lax.optimization_barrier((two, sum_3))
    two_y = exchange(two, 1, "two_y")
    odd, sum_2 = call(
        third_kernel, "third", slots, 2, (three_y, two, sides, weights, sum_1y, sum_3), mats,
        (grads, grads),
    )
    return call(
        fourth_kernel, "fourth", slots, 1, (two_y, sides, weights, odd, sum_0, sum_2), mats,
        jax.ShapeDtypeStruct(grads.shape, BF16),
    )


def body(
    n_hst, n_cores, observations, lengths, actions, rewards, assign, actor_embed, actor_policy,
    master_embed, master_policy, master_value, embed_moment, policy_moment, value_moment, next_obs,
):
    traj, slots, feats = observations.shape
    learners = n_hst * n_cores
    rows = traj * slots
    own = observations.reshape(rows, feats)
    value_row = master_value.reshape(1, -1)
    spread, owner = select(traj, slots)
    flip = [(core, core ^ 1) for core in range(n_cores)]
    there = [lax.ppermute(array, "cores", flip) for array in (lengths, assign)]
    gather = n_hst == 8 and n_cores == 2 and rows == BLOCK
    side = side_data(
        spread, owner, own, *[array.reshape(1, -1) for array in (lengths, assign, *there)],
        actions, rewards, actor_embed, actor_policy,
    )
    mats = convert(master_embed, master_policy, value_row)
    side, mats = lax.optimization_barrier((side, mats))
    if gather:
        mine = gathered_grads(slots, own, side, mats)
        theirs = lax.ppermute(mine, "cores", flip)
    else:
        named = (assign[:, None] == jnp.arange(learners)[None, :]).astype(F32)
        totals = lax.psum(jnp.sum(named * lengths[:, None].astype(F32), axis=0), AXES)
        weights = jnp.broadcast_to((1.0 / (learners * totals))[:, None], (learners, 128))
        grads = call(
            local_kernel, "local", slots, rows // BLOCK,
            (own.reshape(-1, BLOCK, feats), side, weights), mats,
            jax.ShapeDtypeStruct((feats + mats[2].shape[0], mats[0].shape[0]), F32),
        )
        mine = lax.psum(grads, AXES)
        theirs = jnp.zeros_like(mine)
    outs = update(
        mine, theirs, master_embed, master_policy, value_row, embed_moment, policy_moment,
        value_moment.reshape(1, -1), next_obs,
    )
    logits, new_embed, new_policy, new_value, new_em, new_pm, new_vm = outs
    return logits, new_embed, new_policy, new_value.reshape(-1), new_em, new_pm, new_vm.reshape(-1)


def solution(mesh):
    split = P(("group", "hst", "cores"))
    whole = P("group")
    return jax.shard_map(
        functools.partial(body, mesh.shape["hst"], mesh.shape["cores"]),
        mesh=mesh,
        in_specs=(split,) * 5 + (whole,) * 8 + (split,),
        out_specs=(split,) + (whole,) * 6,
        check_vma=False,
    )
```

```python
import functools

import jax
import jax.numpy as jnp
from jax import lax
from jax.experimental import pallas as pl
from jax.experimental.pallas import tpu as pltpu
from jax.sharding import PartitionSpec as P

GAMMA = 0.99
ENTROPY_COEF = 0.1
MOMENTUM = 0.9
LEARN_RATE = 0.05
AXES = ("hst", "cores")
F32 = jnp.float32
BF16 = jnp.bfloat16
VMEM = pl.BlockSpec(memory_space=pltpu.VMEM)
MIB = 2**20
BLOCK = 256
PAD = 16
CHUNKS = 4
BEHAVE, ACTION, REWARD, LENGTH, ASSIGN, LENGTH_2, ASSIGN_2 = range(7)


def iota(shape, dim):
    return lax.broadcasted_iota(jnp.int32, shape, dim)


def mm(a, b):
    return jnp.dot(a, b, preferred_element_type=F32)


def mm_nt(a, b):
    return lax.dot_general(a, b, (((1,), (1,)), ((), ())), preferred_element_type=F32)


def params(mib):
    return pltpu.CompilerParams(vmem_limit_bytes=mib * MIB)


def cost(micros):
    return pl.CostEstimate(flops=int(micros * 1.1e9), bytes_accessed=0, transcendentals=0)


def select_kernel(spread, owner):
    traj, rows = owner.shape
    slots = spread.shape[0]
    spread[...] = (lax.rem(iota((slots, rows), 1), slots) == iota((slots, rows), 0)).astype(F32)
    owner[...] = (lax.div(iota((traj, rows), 1), slots) == iota((traj, rows), 0)).astype(F32)


def select(traj, slots):
    rows = traj * slots
    return pl.pallas_call(
        select_kernel,
        out_shape=(jax.ShapeDtypeStruct((slots, rows), F32), jax.ShapeDtypeStruct((traj, rows), F32)),
        out_specs=(VMEM, VMEM),
        compiler_params=params(4),
        cost_estimate=cost(40),
        name="select",
    )()


def side_kernel(
    lengths, assign, lengths_2, assign_2, actions, rewards, actor_embed, actor_policy,
    spread, owner, obs, side,
):

    def flat(series):
        wide = jnp.dot(
            series, spread[...], precision=lax.Precision.HIGHEST, preferred_element_type=F32
        )
        return jnp.sum(wide * owner[...], axis=0, keepdims=True)

    def repeat(series):
        return jnp.dot(
            series.astype(F32), owner[...],
            precision=lax.Precision.HIGHEST, preferred_element_type=F32,
        )

    action = flat(actions[...].astype(F32))
    hidden = jnp.maximum(mm(obs[...], actor_embed[...]), 0.0).astype(BF16)
    logits = mm(hidden, actor_policy[...]).T
    top = jnp.max(logits, axis=0, keepdims=True)
    shifted = logits - top
    norm = jnp.log(jnp.sum(jnp.exp(shifted), axis=0, keepdims=True))
    onehot = iota(logits.shape, 0) == action.astype(jnp.int32)
    side[...] = jnp.zeros_like(side)
    side[BEHAVE : BEHAVE + 1, :] = (
        jnp.sum(jnp.where(onehot, shifted, 0.0), axis=0, keepdims=True) - norm
    )
    side[ACTION : ACTION + 1, :] = action
    side[REWARD : REWARD + 1, :] = flat(rewards[...])
    side[LENGTH : LENGTH + 1, :] = repeat(lengths[...])
    side[ASSIGN : ASSIGN + 1, :] = repeat(assign[...])
    side[LENGTH_2 : LENGTH_2 + 1, :] = repeat(lengths_2[...])
    side[ASSIGN_2 : ASSIGN_2 + 1, :] = repeat(assign_2[...])


def side_data(spread, owner, obs, *args):
    count = len(args) + 3
    return pl.pallas_call(
        side_kernel,
        out_shape=jax.ShapeDtypeStruct((8, spread.shape[1]), F32),
        in_specs=[VMEM] * count,
        out_specs=VMEM,
        compiler_params=params(12),
        cost_estimate=cost(1.3),
        name="side",
    )(*args, spread, owner, obs)


def convert_kernel(master_embed, master_policy, master_value, embed_t, head, head_t):
    embed_t[...] = master_embed[...].T.astype(BF16)
    nact = master_policy.shape[1]
    wide = jnp.concatenate(
        [
            master_policy[...].T,
            master_value[...],
            jnp.zeros((PAD - 1, head_t.shape[1]), F32),
        ],
        axis=0,
    )
    head_t[...] = wide.astype(BF16)
    head[:, 0:nact] = master_policy[...].astype(BF16)
    head[:, nact:] = wide[nact:, :].T.astype(BF16)


def convert(master_embed, master_policy, master_value):
    feats, width = master_embed.shape
    nact = master_policy.shape[1]
    return pl.pallas_call(
        convert_kernel,
        out_shape=(
            jax.ShapeDtypeStruct((width, feats), BF16),
            jax.ShapeDtypeStruct((width, nact + PAD), BF16),
            jax.ShapeDtypeStruct((nact + PAD, width), BF16),
        ),
        in_specs=[VMEM] * 3,
        out_specs=(VMEM,) * 3,
        compiler_params=params(12),
        cost_estimate=cost(0.6),
        name="convert",
    )(master_embed, master_policy, master_value)


def learner_weights(slots, sides, out):
    learners, rows = out.shape[0], sides.shape[1]
    total = jnp.zeros((learners, rows), F32)
    first = lax.rem(iota((1, rows), 1), slots) == 0
    for place in range(0, sides.shape[0], 8):
        for length_at, assign_at in ((LENGTH, ASSIGN), (LENGTH_2, ASSIGN_2)):
            assign = sides[place + assign_at : place + assign_at + 1, :].astype(jnp.int32)
            length = jnp.where(first, sides[place + length_at : place + length_at + 1, :], 0.0)
            total = total + jnp.where(iota((learners, rows), 0) == assign, length, 0.0)
    summed = jnp.sum(total, axis=1, keepdims=True)
    out[...] = jnp.broadcast_to(1.0 / (learners * summed), out.shape)


def vtrace(slots, nact, side, weights, logits, values):
    rows = logits.shape[1]
    learners = weights.shape[0]
    behave = side[BEHAVE : BEHAVE + 1, :]
    reward = side[REWARD : REWARD + 1, :]
    length = side[LENGTH : LENGTH + 1, :].astype(jnp.int32)
    assign = side[ASSIGN : ASSIGN + 1, :].astype(jnp.int32)
    action = side[ACTION : ACTION + 1, :].astype(jnp.int32)
    weight = jnp.sum(
        jnp.where(iota((learners, rows), 0) == assign, weights[:, 0:1], 0.0), axis=0, keepdims=True
    )
    top = jnp.max(logits, axis=0, keepdims=True)
    exps = jnp.exp(logits - top)
    norm = jnp.sum(exps, axis=0, keepdims=True)
    logprob = logits - (top + jnp.log(norm))
    probs = exps * (1.0 / norm)
    onehot = iota(logits.shape, 0) == action
    taken = jnp.sum(jnp.where(onehot, logprob, 0.0), axis=0, keepdims=True)
    entropy = -jnp.sum(probs * logprob, axis=0, keepdims=True)
    step = lax.rem(iota((1, rows), 1), slots)
    inside = (step < length).astype(F32)
    beyond = (step + 1 < length).astype(F32)
    ratios = jnp.minimum(1.0, jnp.exp(taken - behave))

    def later(series, by):
        return pltpu.roll(series, rows - by, 1)

    deltas = inside * ratios * (reward + GAMMA * later(values, 1) * beyond - values)
    decay = GAMMA * ratios * inside
    corrections = deltas
    reach = 1
    while reach < slots:
        within = step + reach < slots
        corrections = corrections + decay * jnp.where(within, later(corrections, reach), 0.0)
        decay = decay * jnp.where(within, later(decay, reach), 0.0)
        reach *= 2
    targets = values + corrections
    advantage = ratios * (reward + GAMMA * later(targets, 1) * beyond - values)
    scale = weight * inside
    grad = scale * (
        -advantage * (onehot.astype(F32) - probs) + ENTROPY_COEF * probs * (logprob + entropy)
    )
    return grad, scale * (values - targets)


def forward(frames, embed_t, head_t, frames_t, hidden_t):
    width = embed_t.shape[0]
    tile = 256
    for index, block in enumerate(frames):
        frames_t[:, index * BLOCK : (index + 1) * BLOCK] = block[...].T
    for start in range(0, width, tile):
        here = slice(start, start + tile)
        hidden_t[here, :] = jnp.maximum(mm(embed_t[here, :], frames_t[...]), 0.0).astype(BF16)
    return mm(head_t[...], hidden_t[...])


def backward(slots, logits, side, weights, head, frames_t, hidden_t, preact_t, add):
    width, feats = head.shape[0], frames_t.shape[0]
    nact = logits.shape[0] - PAD
    tile = 256
    grad, grad_values = vtrace(
        slots, nact, side, weights, logits[0:nact, :], logits[nact : nact + 1, :]
    )
    pad = jnp.zeros((PAD - 1, grad.shape[1]), F32)
    grad_t = jnp.concatenate([grad, grad_values, pad], axis=0).astype(BF16)
    for start in range(0, width, tile):
        here = slice(start, start + tile)
        back = mm(head[here, :], grad_t)
        alive = hidden_t[here, :].astype(F32) > 0.0
        preact_t[here, :] = jnp.where(alive, back, 0.0).astype(BF16)
    for index in range(frames_t.shape[1] // BLOCK):
        lanes = slice(index * BLOCK, (index + 1) * BLOCK)
        add(index, slice(0, feats), mm_nt(frames_t[:, lanes], preact_t[:, lanes]))
        add(index, slice(feats, feats + nact + PAD), mm_nt(grad_t[:, lanes], hidden_t[:, lanes]))


def work(slots, frames, side, weights, embed_t, head, head_t, frames_t, hidden_t, preact_t, add):
    logits = forward(frames, embed_t, head_t, frames_t, hidden_t)
    backward(slots, logits, side, weights, head, frames_t, hidden_t, preact_t, add)


def side_of(sides, back, flip):
    line = lax.div(lax.axis_index("hst"), 2)
    there = lax.bitwise_xor(line, lax.bitwise_and(line + 4 - back, 3))
    return sides[pl.ds(pl.multiple_of(8 * (2 * there + flip), 8), 8), :]


def ahead_kernel(*refs):
    (*frames, embed_t, head_t, frames_t, hidden_t, logits) = refs
    logits[...] = forward(frames, embed_t, head_t, frames_t, hidden_t)


def ahead(frames, embed_t, head_t):
    width, feats = embed_t.shape
    rows = len(frames) * BLOCK
    return pl.pallas_call(
        ahead_kernel,
        out_shape=(
            jax.ShapeDtypeStruct((feats, rows), BF16),
            jax.ShapeDtypeStruct((width, rows), BF16),
            jax.ShapeDtypeStruct((head_t.shape[0], rows), F32),
        ),
        in_specs=[VMEM] * (len(frames) + 2),
        out_specs=(VMEM,) * 3,
        compiler_params=params(20),
        cost_estimate=cost(1.6),
        name="ahead",
    )(*frames, embed_t, head_t)


def first_kernel(slots, *refs):
    (frames_t, hidden_t, logits, *pieces), mats, (sum_0, sum_1, weights, sides), scratch = (
        refs[0:7], refs[7:10], refs[10:14], refs[14:17])
    start = 0
    for piece in pieces:
        sides[start : start + piece.shape[0], :] = piece[...]
        start += piece.shape[0]
    learner_weights(slots, sides, weights)

    def add(index, rows, value):
        if index == 0:
            sum_0[rows, :] = value
        elif index == 1:
            sum_0[rows, :] += value
        else:
            sum_1[rows, :] = value

    side = jnp.concatenate([side_of(sides, *at) for at in ((0, 0), (0, 1), (1, 0))], axis=1)
    backward(slots, logits[...], side, weights, mats[1], frames_t, hidden_t, scratch[2], add)


def second_kernel(slots, *refs):
    frames, (sides, weights, sum_1), mats, (sum_1y, sum_3), scratch = (
        refs[0:2], refs[2:5], refs[5:8], refs[8:10], refs[10:13])

    def add(index, rows, value):
        if index == 0:
            sum_1y[rows, :] = sum_1[rows, :] + value
        else:
            sum_3[rows, :] = value

    side = jnp.concatenate([side_of(sides, 1, 1), side_of(sides, 3, 0)], axis=1)
    work(slots, frames, side, weights, *mats, *scratch, add)


def third_kernel(slots, *refs):
    frames, (sides, weights, sum_1y, sum_3), mats, (odd, sum_2), scratch = (
        refs[0:2], refs[2:6], refs[6:9], refs[9:11], refs[11:14])

    def add(index, rows, value):
        if index == 0:
            odd[rows, :] = sum_1y[rows, :] + (sum_3[rows, :] + value)
        else:
            sum_2[rows, :] = value

    side = jnp.concatenate([side_of(sides, 3, 1), side_of(sides, 2, 0)], axis=1)
    work(slots, frames, side, weights, *mats, *scratch, add)


def fourth_kernel(slots, *refs):
    frames, (sides, weights, odd, sum_0, sum_2), mats, out, scratch = (
        refs[0:1], refs[1:6], refs[6:9], refs[9], refs[10:13])

    def add(index, rows, value):
        out[rows, :] = (
            odd[rows, :] + (sum_0[rows, :] + (sum_2[rows, :] + value))
        ).astype(BF16)

    work(slots, frames, side_of(sides, 2, 1), weights, *mats, *scratch, add)


def local_kernel(slots, frames, side, weights, embed_t, head, head_t, out, *scratch):
    def add(index, rows, value):
        if index == 0:
            out[rows, :] = value
        else:
            out[rows, :] += value

    blocks = [frames.at[index] for index in range(frames.shape[0])]
    work(slots, blocks, side, weights, embed_t, head, head_t, *scratch, add)


def call(kernel, name, slots, blocks, args, mats, outs):
    width, feats = mats[0].shape
    rows = blocks * BLOCK
    return pl.pallas_call(
        functools.partial(kernel, slots),
        out_shape=outs,
        in_specs=[VMEM] * (len(args) + 3),
        out_specs=jax.tree.map(lambda leaf: VMEM, outs),
        scratch_shapes=[
            pltpu.VMEM((feats, rows), BF16),
            pltpu.VMEM((width, rows), BF16),
            pltpu.VMEM((width, rows), BF16),
        ],
        compiler_params=params(32),
        cost_estimate=cost(1.2 * blocks + 0.4),
        name=name,
    )(*args, *mats)


def update_kernel(
    feats, nact, mine, theirs, master_embed, master_policy, master_value,
    embed_moment, policy_moment, value_moment, next_obs,
    next_logits, new_embed_at, new_policy_at, new_value, new_em_at, new_pm_at, new_vm,
    new_embed, new_policy, new_em, new_pm, rounded, sems,
):
    copies = []

    def store(source, target, rows):
        copy = pltpu.make_async_copy(source.at[rows, :], target.at[rows, :], sems.at[len(copies)])
        copy.start()
        copies.append(copy)

    def grad(start, size):
        return mine[start : start + size, :].astype(F32) + theirs[start : start + size, :].astype(F32)

    def step(grad, moment, master):
        held = MOMENTUM * moment + grad
        return held, master - LEARN_RATE * held

    def chunks(height):
        return [pl.ds(start, height // CHUNKS) for start in range(0, height, height // CHUNKS)]

    for rows in chunks(feats):
        held, fresh = step(grad(rows.start, rows.size), embed_moment[rows, :], master_embed[rows, :])
        new_em[rows, :] = held
        new_embed[rows, :] = fresh
        rounded[rows, :] = fresh.astype(BF16)
        store(new_em, new_em_at, rows)
        store(new_embed, new_embed_at, rows)
    policy_grad = grad(feats, nact).T
    held, fresh = step(policy_grad, policy_moment[...], master_policy[...])
    new_pm[...] = held
    new_policy[...] = fresh
    every = pl.ds(0, new_pm.shape[0])
    store(new_pm, new_pm_at, every)
    store(new_policy, new_policy_at, every)
    new_vm[...], new_value[...] = step(
        grad(feats + nact, PAD)[0:1, :], value_moment[...], master_value[...]
    )
    hidden = jnp.maximum(mm(next_obs[...], rounded[...]), 0.0).astype(BF16)
    next_logits[...] = mm(hidden, fresh.astype(BF16)).astype(BF16)
    for copy in copies:
        copy.wait()


def update(mine, theirs, *args):
    embed, policy, value = args[0], args[1], args[2]
    next_obs = args[6]
    feats, nact = embed.shape[0], policy.shape[1]
    shapes = [jax.ShapeDtypeStruct(array.shape, F32) for array in (embed, policy, value)]
    anywhere = pl.BlockSpec(memory_space=pl.ANY)
    specs = (anywhere, anywhere, VMEM)
    held = [pltpu.VMEM(array.shape, F32) for array in (embed, policy)]
    return pl.pallas_call(
        functools.partial(update_kernel, feats, nact),
        out_shape=(jax.ShapeDtypeStruct((next_obs.shape[0], nact), BF16), *shapes, *shapes),
        in_specs=[VMEM] * 9,
        out_specs=(VMEM, *specs, *specs),
        scratch_shapes=[*held, *held, pltpu.VMEM(embed.shape, BF16), pltpu.SemaphoreType.DMA((2 * CHUNKS + 2,))],
        compiler_params=params(24),
        cost_estimate=cost(3.4),
        name="update",
    )(mine, theirs, *args)


def gathered_grads(slots, own, side, mats):
    def exchange(array, mask, name):
        with jax.named_scope(name):
            return lax.ppermute(array, "hst", [(at, at ^ mask) for at in range(8)])

    def shift(array, by, name):
        with jax.named_scope(name):
            return lax.ppermute(array, "hst", [(at, (at + 2 * by) % 8) for at in range(8)])

    one = shift(own, 1, "one")
    own_y = exchange(own, 1, "own_y")
    pair = jnp.concatenate([side, exchange(side, 1, "side_y")], axis=0)
    pair, _, _ = lax.optimization_barrier((pair, one, own_y))
    pieces = [pair] + [exchange(pair, 2 * mask, "side_z") for mask in (1, 2, 3)]
    again, _ = lax.optimization_barrier((own, side))
    three = shift(again, -1, "three")
    one_y = exchange(one, 1, "one_y")
    two = shift(one, 1, "two")
    three_y = exchange(three, 1, "three_y")
    pieces, one_y = lax.optimization_barrier((pieces, one_y))
    width, feats = mats[0].shape
    grads = jax.ShapeDtypeStruct((feats + mats[2].shape[0], width), F32)
    weights = jax.ShapeDtypeStruct((16, 128), F32)
    sides = jax.ShapeDtypeStruct((64, side.shape[1]), F32)
    done = ahead((own, own_y, one), mats[0], mats[2])
    sum_0, sum_1, weights, sides = call(
        first_kernel, "first", slots, 3, (*done, *pieces), mats,
        (grads, grads, weights, sides),
    )
    sum_1y, sum_3 = call(
        second_kernel, "second", slots, 2, (one_y, three, sides, weights, sum_1), mats,
        (grads, grads),
    )
    two, sum_3 = lax.optimization_barrier((two, sum_3))
    two_y = exchange(two, 1, "two_y")
    odd, sum_2 = call(
        third_kernel, "third", slots, 2, (three_y, two, sides, weights, sum_1y, sum_3), mats,
        (grads, grads),
    )
    return call(
        fourth_kernel, "fourth", slots, 1, (two_y, sides, weights, odd, sum_0, sum_2), mats,
        jax.ShapeDtypeStruct(grads.shape, BF16),
    )


def body(
    n_hst, n_cores, observations, lengths, actions, rewards, assign, actor_embed, actor_policy,
    master_embed, master_policy, master_value, embed_moment, policy_moment, value_moment, next_obs,
):
    traj, slots, feats = observations.shape
    learners = n_hst * n_cores
    rows = traj * slots
    own = observations.reshape(rows, feats)
    value_row = master_value.reshape(1, -1)
    spread, owner = select(traj, slots)
    flip = [(core, core ^ 1) for core in range(n_cores)]
    there = [lax.ppermute(array, "cores", flip) for array in (lengths, assign)]
    gather = n_hst == 8 and n_cores == 2 and rows == BLOCK
    side = side_data(
        spread, owner, own, *[array.reshape(1, -1) for array in (lengths, assign, *there)],
        actions, rewards, actor_embed, actor_policy,
    )
    mats = convert(master_embed, master_policy, value_row)
    side, mats = lax.optimization_barrier((side, mats))
    if gather:
        mine = gathered_grads(slots, own, side, mats)
        theirs = lax.ppermute(mine, "cores", flip)
    else:
        named = (assign[:, None] == jnp.arange(learners)[None, :]).astype(F32)
        totals = lax.psum(jnp.sum(named * lengths[:, None].astype(F32), axis=0), AXES)
        weights = jnp.broadcast_to((1.0 / (learners * totals))[:, None], (learners, 128))
        grads = call(
            local_kernel, "local", slots, rows // BLOCK,
            (own.reshape(-1, BLOCK, feats), side, weights), mats,
            jax.ShapeDtypeStruct((feats + mats[2].shape[0], mats[0].shape[0]), F32),
        )
        mine = lax.psum(grads, AXES)
        theirs = jnp.zeros_like(mine)
    outs = update(
        mine, theirs, master_embed, master_policy, value_row, embed_moment, policy_moment,
        value_moment.reshape(1, -1), next_obs,
    )
    logits, new_embed, new_policy, new_value, new_em, new_pm, new_vm = outs
    return logits, new_embed, new_policy, new_value.reshape(-1), new_em, new_pm, new_vm.reshape(-1)


def solution(mesh):
    split = P(("group", "hst", "cores"))
    whole = P("group")
    return jax.shard_map(
        functools.partial(body, mesh.shape["hst"], mesh.shape["cores"]),
        mesh=mesh,
        in_specs=(split,) * 5 + (whole,) * 8 + (split,),
        out_specs=(split,) + (whole,) * 6,
        check_vma=False,
    )
```

```python
import functools

import jax
import jax.numpy as jnp
from jax import lax
from jax.experimental import pallas as pl
from jax.experimental.pallas import tpu as pltpu
from jax.sharding import PartitionSpec as P

GAMMA = 0.99
ENTROPY_COEF = 0.1
MOMENTUM = 0.9
LEARN_RATE = 0.05
AXES = ("hst", "cores")
F32 = jnp.float32
BF16 = jnp.bfloat16
VMEM = pl.BlockSpec(memory_space=pltpu.VMEM)
MIB = 2**20
BLOCK = 256
PAD = 16
BEHAVE, ACTION, REWARD, LENGTH, ASSIGN, LENGTH_2, ASSIGN_2 = range(7)


def iota(shape, dim):
    return lax.broadcasted_iota(jnp.int32, shape, dim)


def mm(a, b):
    return jnp.dot(a, b, preferred_element_type=F32)


def mm_nt(a, b):
    return lax.dot_general(a, b, (((1,), (1,)), ((), ())), preferred_element_type=F32)


def params(mib):
    return pltpu.CompilerParams(vmem_limit_bytes=mib * MIB)


def cost(micros):
    return pl.CostEstimate(flops=int(micros * 1.1e9), bytes_accessed=0, transcendentals=0)


def select_kernel(spread, owner):
    traj, rows = owner.shape
    slots = spread.shape[0]
    spread[...] = (lax.rem(iota((slots, rows), 1), slots) == iota((slots, rows), 0)).astype(F32)
    owner[...] = (lax.div(iota((traj, rows), 1), slots) == iota((traj, rows), 0)).astype(F32)


def select(traj, slots):
    rows = traj * slots
    return pl.pallas_call(
        select_kernel,
        out_shape=(jax.ShapeDtypeStruct((slots, rows), F32), jax.ShapeDtypeStruct((traj, rows), F32)),
        out_specs=(VMEM, VMEM),
        compiler_params=params(4),
        cost_estimate=cost(40),
        name="select",
    )()


def side_kernel(
    lengths, assign, lengths_2, assign_2, actions, rewards, actor_embed, actor_policy,
    spread, owner, obs, side,
):

    def flat(series):
        wide = jnp.dot(
            series, spread[...], precision=lax.Precision.HIGHEST, preferred_element_type=F32
        )
        return jnp.sum(wide * owner[...], axis=0, keepdims=True)

    def repeat(series):
        return jnp.dot(
            series.astype(F32), owner[...],
            precision=lax.Precision.HIGHEST, preferred_element_type=F32,
        )

    action = flat(actions[...].astype(F32))
    hidden = jnp.maximum(mm(obs[...], actor_embed[...]), 0.0).astype(BF16)
    logits = mm(hidden, actor_policy[...]).T
    top = jnp.max(logits, axis=0, keepdims=True)
    shifted = logits - top
    norm = jnp.log(jnp.sum(jnp.exp(shifted), axis=0, keepdims=True))
    onehot = iota(logits.shape, 0) == action.astype(jnp.int32)
    side[...] = jnp.zeros_like(side)
    side[BEHAVE : BEHAVE + 1, :] = (
        jnp.sum(jnp.where(onehot, shifted, 0.0), axis=0, keepdims=True) - norm
    )
    side[ACTION : ACTION + 1, :] = action
    side[REWARD : REWARD + 1, :] = flat(rewards[...])
    side[LENGTH : LENGTH + 1, :] = repeat(lengths[...])
    side[ASSIGN : ASSIGN + 1, :] = repeat(assign[...])
    side[LENGTH_2 : LENGTH_2 + 1, :] = repeat(lengths_2[...])
    side[ASSIGN_2 : ASSIGN_2 + 1, :] = repeat(assign_2[...])


def side_data(spread, owner, obs, *args):
    count = len(args) + 3
    return pl.pallas_call(
        side_kernel,
        out_shape=jax.ShapeDtypeStruct((8, spread.shape[1]), F32),
        in_specs=[VMEM] * count,
        out_specs=VMEM,
        compiler_params=params(12),
        cost_estimate=cost(1.3),
        name="side",
    )(*args, spread, owner, obs)


def convert_kernel(master_embed, master_policy, master_value, embed_t, head, head_t):
    embed_t[...] = master_embed[...].T.astype(BF16)
    nact = master_policy.shape[1]
    wide = jnp.concatenate(
        [
            master_policy[...].T,
            master_value[...],
            jnp.zeros((PAD - 1, head_t.shape[1]), F32),
        ],
        axis=0,
    )
    head_t[...] = wide.astype(BF16)
    head[:, 0:nact] = master_policy[...].astype(BF16)
    head[:, nact:] = wide[nact:, :].T.astype(BF16)


def convert(master_embed, master_policy, master_value):
    feats, width = master_embed.shape
    nact = master_policy.shape[1]
    return pl.pallas_call(
        convert_kernel,
        out_shape=(
            jax.ShapeDtypeStruct((width, feats), BF16),
            jax.ShapeDtypeStruct((width, nact + PAD), BF16),
            jax.ShapeDtypeStruct((nact + PAD, width), BF16),
        ),
        in_specs=[VMEM] * 3,
        out_specs=(VMEM,) * 3,
        compiler_params=params(12),
        cost_estimate=cost(0.6),
        name="convert",
    )(master_embed, master_policy, master_value)


def learner_weights(slots, sides, out):
    learners, rows = out.shape[0], sides.shape[1]
    total = jnp.zeros((learners, rows), F32)
    first = lax.rem(iota((1, rows), 1), slots) == 0
    for place in range(0, sides.shape[0], 8):
        for length_at, assign_at in ((LENGTH, ASSIGN), (LENGTH_2, ASSIGN_2)):
            assign = sides[place + assign_at : place + assign_at + 1, :].astype(jnp.int32)
            length = jnp.where(first, sides[place + length_at : place + length_at + 1, :], 0.0)
            total = total + jnp.where(iota((learners, rows), 0) == assign, length, 0.0)
    summed = jnp.sum(total, axis=1, keepdims=True)
    out[...] = jnp.broadcast_to(1.0 / (learners * summed), out.shape)


def vtrace(slots, nact, side, weights, logits, values):
    rows = logits.shape[1]
    learners = weights.shape[0]
    behave = side[BEHAVE : BEHAVE + 1, :]
    reward = side[REWARD : REWARD + 1, :]
    length = side[LENGTH : LENGTH + 1, :].astype(jnp.int32)
    assign = side[ASSIGN : ASSIGN + 1, :].astype(jnp.int32)
    action = side[ACTION : ACTION + 1, :].astype(jnp.int32)
    weight = jnp.sum(
        jnp.where(iota((learners, rows), 0) == assign, weights[:, 0:1], 0.0), axis=0, keepdims=True
    )
    top = jnp.max(logits, axis=0, keepdims=True)
    exps = jnp.exp(logits - top)
    norm = jnp.sum(exps, axis=0, keepdims=True)
    logprob = logits - (top + jnp.log(norm))
    probs = exps * (1.0 / norm)
    onehot = iota(logits.shape, 0) == action
    taken = jnp.sum(jnp.where(onehot, logprob, 0.0), axis=0, keepdims=True)
    entropy = -jnp.sum(probs * logprob, axis=0, keepdims=True)
    step = lax.rem(iota((1, rows), 1), slots)
    inside = (step < length).astype(F32)
    beyond = (step + 1 < length).astype(F32)
    ratios = jnp.minimum(1.0, jnp.exp(taken - behave))

    def later(series, by):
        return pltpu.roll(series, rows - by, 1)

    deltas = inside * ratios * (reward + GAMMA * later(values, 1) * beyond - values)
    decay = GAMMA * ratios * inside
    corrections = deltas
    reach = 1
    while reach < slots:
        within = step + reach < slots
        corrections = corrections + decay * jnp.where(within, later(corrections, reach), 0.0)
        decay = decay * jnp.where(within, later(decay, reach), 0.0)
        reach *= 2
    targets = values + corrections
    advantage = ratios * (reward + GAMMA * later(targets, 1) * beyond - values)
    scale = weight * inside
    grad = scale * (
        -advantage * (onehot.astype(F32) - probs) + ENTROPY_COEF * probs * (logprob + entropy)
    )
    return grad, scale * (values - targets)


def forward(frames, embed_t, head_t, frames_t, hidden_t):
    width = embed_t.shape[0]
    tile = 256
    for index, block in enumerate(frames):
        frames_t[:, index * BLOCK : (index + 1) * BLOCK] = block[...].T
    for start in range(0, width, tile):
        here = slice(start, start + tile)
        hidden_t[here, :] = jnp.maximum(mm(embed_t[here, :], frames_t[...]), 0.0).astype(BF16)
    return mm(head_t[...], hidden_t[...])


def backward(slots, logits, side, weights, head, frames_t, hidden_t, preact_t, add):
    width, feats = head.shape[0], frames_t.shape[0]
    nact = logits.shape[0] - PAD
    tile = 256
    grad, grad_values = vtrace(
        slots, nact, side, weights, logits[0:nact, :], logits[nact : nact + 1, :]
    )
    pad = jnp.zeros((PAD - 1, grad.shape[1]), F32)
    grad_t = jnp.concatenate([grad, grad_values, pad], axis=0).astype(BF16)
    for start in range(0, width, tile):
        here = slice(start, start + tile)
        back = mm(head[here, :], grad_t)
        alive = hidden_t[here, :].astype(F32) > 0.0
        preact_t[here, :] = jnp.where(alive, back, 0.0).astype(BF16)
    for index in range(frames_t.shape[1] // BLOCK):
        lanes = slice(index * BLOCK, (index + 1) * BLOCK)
        add(index, slice(0, feats), mm_nt(frames_t[:, lanes], preact_t[:, lanes]))
        add(index, slice(feats, feats + nact + PAD), mm_nt(grad_t[:, lanes], hidden_t[:, lanes]))


def work(slots, frames, side, weights, embed_t, head, head_t, frames_t, hidden_t, preact_t, add):
    logits = forward(frames, embed_t, head_t, frames_t, hidden_t)
    backward(slots, logits, side, weights, head, frames_t, hidden_t, preact_t, add)


def side_of(sides, mask):
    return sides[8 * mask : 8 * mask + 8, :]


def ahead_kernel(*refs):
    (*frames, embed_t, head_t, frames_t, hidden_t, logits) = refs
    logits[...] = forward(frames, embed_t, head_t, frames_t, hidden_t)


def ahead(frames, embed_t, head_t):
    width, feats = embed_t.shape
    rows = len(frames) * BLOCK
    return pl.pallas_call(
        ahead_kernel,
        out_shape=(
            jax.ShapeDtypeStruct((feats, rows), BF16),
            jax.ShapeDtypeStruct((width, rows), BF16),
            jax.ShapeDtypeStruct((head_t.shape[0], rows), F32),
        ),
        in_specs=[VMEM] * (len(frames) + 2),
        out_specs=(VMEM,) * 3,
        compiler_params=params(20),
        cost_estimate=cost(1.6),
        name="ahead",
    )(*frames, embed_t, head_t)


def first_kernel(slots, *refs):
    (frames_t, hidden_t, logits, *pieces), mats, (sum_01, sum_2, weights, sides), scratch = (
        refs[0:7], refs[7:10], refs[10:14], refs[14:17])
    start = 0
    for piece in pieces:
        sides[start : start + piece.shape[0], :] = piece[...]
        start += piece.shape[0]
    learner_weights(slots, sides, weights)

    def add(index, rows, value):
        if index == 0:
            sum_01[rows, :] = value
        elif index == 1:
            sum_01[rows, :] += value
        else:
            sum_2[rows, :] = value

    side = jnp.concatenate([side_of(sides, mask) for mask in (0, 1, 2)], axis=1)
    backward(slots, logits[...], side, weights, mats[1], frames_t, hidden_t, scratch[2], add)


def second_kernel(slots, *refs):
    frames, (sides, weights, sum_01, sum_2), mats, (sum_0123, sum_4), scratch = (
        refs[0:2], refs[2:6], refs[6:9], refs[9:11], refs[11:14])

    def add(index, rows, value):
        if index == 0:
            sum_0123[rows, :] = sum_01[rows, :] + (sum_2[rows, :] + value)
        else:
            sum_4[rows, :] = value

    side = jnp.concatenate([side_of(sides, 3), side_of(sides, 4)], axis=1)
    work(slots, frames, side, weights, *mats, *scratch, add)


def third_kernel(slots, *refs):
    frames, (sides, weights, sum_4), mats, (sum_45, sum_6), scratch = (
        refs[0:2], refs[2:5], refs[5:8], refs[8:10], refs[10:13])

    def add(index, rows, value):
        if index == 0:
            sum_45[rows, :] = sum_4[rows, :] + value
        else:
            sum_6[rows, :] = value

    side = jnp.concatenate([side_of(sides, 5), side_of(sides, 6)], axis=1)
    work(slots, frames, side, weights, *mats, *scratch, add)


def fourth_kernel(slots, *refs):
    frames, (sides, weights, sum_0123, sum_45, sum_6), mats, out, scratch = (
        refs[0:1], refs[1:6], refs[6:9], refs[9], refs[10:13])

    def add(index, rows, value):
        out[rows, :] = (
            sum_0123[rows, :] + (sum_45[rows, :] + (sum_6[rows, :] + value))
        ).astype(BF16)

    work(slots, frames, side_of(sides, 7), weights, *mats, *scratch, add)


def local_kernel(slots, frames, side, weights, embed_t, head, head_t, out, *scratch):
    def add(index, rows, value):
        if index == 0:
            out[rows, :] = value
        else:
            out[rows, :] += value

    blocks = [frames.at[index] for index in range(frames.shape[0])]
    work(slots, blocks, side, weights, embed_t, head, head_t, *scratch, add)


def call(kernel, name, slots, blocks, args, mats, outs):
    width, feats = mats[0].shape
    rows = blocks * BLOCK
    return pl.pallas_call(
        functools.partial(kernel, slots),
        out_shape=outs,
        in_specs=[VMEM] * (len(args) + 3),
        out_specs=jax.tree.map(lambda leaf: VMEM, outs),
        scratch_shapes=[
            pltpu.VMEM((feats, rows), BF16),
            pltpu.VMEM((width, rows), BF16),
            pltpu.VMEM((width, rows), BF16),
        ],
        compiler_params=params(32),
        cost_estimate=cost(1.2 * blocks + 0.4),
        name=name,
    )(*args, *mats)


def update_kernel(
    feats, nact, mine, theirs, master_embed, master_policy, master_value,
    embed_moment, policy_moment, value_moment, next_obs,
    next_logits, new_embed, new_policy, new_value, new_em, new_pm, new_vm,
):
    def step(grad, moment, master, new_moment, new_master):
        held = MOMENTUM * moment[...] + grad
        new_moment[...] = held
        fresh = master[...] - LEARN_RATE * held
        new_master[...] = fresh
        return fresh

    def grad(start, size):
        return mine[start : start + size, :].astype(F32) + theirs[start : start + size, :].astype(F32)

    embed = step(grad(0, feats), embed_moment, master_embed, new_em, new_embed)
    hidden = jnp.maximum(mm(next_obs[...], embed.astype(BF16)), 0.0).astype(BF16)
    policy = step(grad(feats, nact).T, policy_moment, master_policy, new_pm, new_policy)
    step(grad(feats + nact, PAD)[0:1, :], value_moment, master_value, new_vm, new_value)
    next_logits[...] = mm(hidden, policy.astype(BF16)).astype(BF16)


def update(mine, theirs, *args):
    embed, policy, value = args[0], args[1], args[2]
    next_obs = args[6]
    feats, nact = embed.shape[0], policy.shape[1]
    shapes = [jax.ShapeDtypeStruct(array.shape, F32) for array in (embed, policy, value)]
    return pl.pallas_call(
        functools.partial(update_kernel, feats, nact),
        out_shape=(jax.ShapeDtypeStruct((next_obs.shape[0], nact), BF16), *shapes, *shapes),
        in_specs=[VMEM] * 9,
        out_specs=(VMEM,) * 7,
        compiler_params=params(32),
        cost_estimate=cost(3.4),
        name="update",
    )(mine, theirs, *args)


def gathered_grads(slots, own, side, mats):
    def exchange(array, mask, name):
        with jax.named_scope(name):
            return lax.ppermute(array, "hst", [(at, at ^ mask) for at in range(8)])

    b2 = exchange(own, 2, "b2")
    b1 = exchange(own, 1, "b1")
    pair = jnp.concatenate([side, exchange(side, 1, "side_y")], axis=0)
    pair, _, _ = lax.optimization_barrier((pair, b2, b1))
    pieces = [pair] + [exchange(pair, 2 * mask, "side_z") for mask in (1, 2, 3)]
    b4 = exchange(own, 4, "b4")
    b3 = exchange(b2, 1, "b3")
    b5 = exchange(b4, 1, "b5")
    b6 = exchange(b4, 2, "b6")
    pieces, b3 = lax.optimization_barrier((pieces, b3))
    width, feats = mats[0].shape
    grads = jax.ShapeDtypeStruct((feats + mats[2].shape[0], width), F32)
    weights = jax.ShapeDtypeStruct((16, 128), F32)
    sides = jax.ShapeDtypeStruct((64, side.shape[1]), F32)
    done = ahead((own, b1, b2), mats[0], mats[2])
    sum_01, sum_2, weights, sides = call(
        first_kernel, "first", slots, 3, (*done, *pieces), mats, (grads, grads, weights, sides),
    )
    sum_0123, sum_4 = call(
        second_kernel, "second", slots, 2, (b3, b4, sides, weights, sum_01, sum_2), mats,
        (grads, grads),
    )
    b6, sum_4 = lax.optimization_barrier((b6, sum_4))
    b7 = exchange(b6, 1, "b7")
    sum_45, sum_6 = call(
        third_kernel, "third", slots, 2, (b5, b6, sides, weights, sum_4), mats, (grads, grads),
    )
    return call(
        fourth_kernel, "fourth", slots, 1, (b7, sides, weights, sum_0123, sum_45, sum_6), mats,
        jax.ShapeDtypeStruct(grads.shape, BF16),
    )


def body(
    n_hst, n_cores, observations, lengths, actions, rewards, assign, actor_embed, actor_policy,
    master_embed, master_policy, master_value, embed_moment, policy_moment, value_moment, next_obs,
):
    traj, slots, feats = observations.shape
    learners = n_hst * n_cores
    rows = traj * slots
    own = observations.reshape(rows, feats)
    value_row = master_value.reshape(1, -1)
    spread, owner = select(traj, slots)
    flip = [(core, core ^ 1) for core in range(n_cores)]
    there = [lax.ppermute(array, "cores", flip) for array in (lengths, assign)]
    gather = n_hst == 8 and n_cores == 2 and rows == BLOCK
    side = side_data(
        spread, owner, own, *[array.reshape(1, -1) for array in (lengths, assign, *there)],
        actions, rewards, actor_embed, actor_policy,
    )
    mats = convert(master_embed, master_policy, value_row)
    side, mats = lax.optimization_barrier((side, mats))
    if gather:
        mine = gathered_grads(slots, own, side, mats)
        theirs = lax.ppermute(mine, "cores", flip)
    else:
        named = (assign[:, None] == jnp.arange(learners)[None, :]).astype(F32)
        totals = lax.psum(jnp.sum(named * lengths[:, None].astype(F32), axis=0), AXES)
        weights = jnp.broadcast_to((1.0 / (learners * totals))[:, None], (learners, 128))
        grads = call(
            local_kernel, "local", slots, rows // BLOCK,
            (own.reshape(-1, BLOCK, feats), side, weights), mats,
            jax.ShapeDtypeStruct((feats + mats[2].shape[0], mats[0].shape[0]), F32),
        )
        mine = lax.psum(grads, AXES)
        theirs = jnp.zeros_like(mine)
    outs = update(
        mine, theirs, master_embed, master_policy, value_row, embed_moment, policy_moment,
        value_moment.reshape(1, -1), next_obs,
    )
    logits, new_embed, new_policy, new_value, new_em, new_pm, new_vm = outs
    return logits, new_embed, new_policy, new_value.reshape(-1), new_em, new_pm, new_vm.reshape(-1)


def solution(mesh):
    split = P(("group", "hst", "cores"))
    whole = P("group")
    return jax.shard_map(
        functools.partial(body, mesh.shape["hst"], mesh.shape["cores"]),
        mesh=mesh,
        in_specs=(split,) * 5 + (whole,) * 8 + (split,),
        out_specs=(split,) + (whole,) * 6,
        check_vma=False,
    )
```

```python
import functools

import jax
import jax.numpy as jnp
from jax import lax
from jax.experimental import pallas as pl
from jax.experimental.pallas import tpu as pltpu
from jax.sharding import PartitionSpec as P

GAMMA = 0.99
ENTROPY_COEF = 0.1
MOMENTUM = 0.9
LEARN_RATE = 0.05
AXES = ("hst", "cores")
F32 = jnp.float32
BF16 = jnp.bfloat16
VMEM = pl.BlockSpec(memory_space=pltpu.VMEM)
MIB = 2**20
BLOCK = 256
PAD = 16
BEHAVE, ACTION, REWARD, LENGTH, ASSIGN, LENGTH_2, ASSIGN_2 = range(7)


def iota(shape, dim):
    return lax.broadcasted_iota(jnp.int32, shape, dim)


def mm(a, b):
    return jnp.dot(a, b, preferred_element_type=F32)


def mm_nt(a, b):
    return lax.dot_general(a, b, (((1,), (1,)), ((), ())), preferred_element_type=F32)


def params(mib):
    return pltpu.CompilerParams(vmem_limit_bytes=mib * MIB)


def cost(micros):
    return pl.CostEstimate(flops=int(micros * 1.1e9), bytes_accessed=0, transcendentals=0)


def select_kernel(spread, owner):
    traj, rows = owner.shape
    slots = spread.shape[0]
    spread[...] = (lax.rem(iota((slots, rows), 1), slots) == iota((slots, rows), 0)).astype(F32)
    owner[...] = (lax.div(iota((traj, rows), 1), slots) == iota((traj, rows), 0)).astype(F32)


def select(traj, slots):
    rows = traj * slots
    return pl.pallas_call(
        select_kernel,
        out_shape=(jax.ShapeDtypeStruct((slots, rows), F32), jax.ShapeDtypeStruct((traj, rows), F32)),
        out_specs=(VMEM, VMEM),
        compiler_params=params(4),
        cost_estimate=cost(40),
        name="select",
    )()


def side_kernel(
    lengths, assign, lengths_2, assign_2, actions, rewards, actor_embed, actor_policy,
    spread, owner, obs, side,
):

    def flat(series):
        wide = jnp.dot(
            series, spread[...], precision=lax.Precision.HIGHEST, preferred_element_type=F32
        )
        return jnp.sum(wide * owner[...], axis=0, keepdims=True)

    def repeat(series):
        return jnp.dot(
            series.astype(F32), owner[...],
            precision=lax.Precision.HIGHEST, preferred_element_type=F32,
        )

    action = flat(actions[...].astype(F32))
    hidden = jnp.maximum(mm(obs[...], actor_embed[...]), 0.0).astype(BF16)
    logits = mm(hidden, actor_policy[...]).T
    top = jnp.max(logits, axis=0, keepdims=True)
    shifted = logits - top
    norm = jnp.log(jnp.sum(jnp.exp(shifted), axis=0, keepdims=True))
    onehot = iota(logits.shape, 0) == action.astype(jnp.int32)
    side[...] = jnp.zeros_like(side)
    side[BEHAVE : BEHAVE + 1, :] = (
        jnp.sum(jnp.where(onehot, shifted, 0.0), axis=0, keepdims=True) - norm
    )
    side[ACTION : ACTION + 1, :] = action
    side[REWARD : REWARD + 1, :] = flat(rewards[...])
    side[LENGTH : LENGTH + 1, :] = repeat(lengths[...])
    side[ASSIGN : ASSIGN + 1, :] = repeat(assign[...])
    side[LENGTH_2 : LENGTH_2 + 1, :] = repeat(lengths_2[...])
    side[ASSIGN_2 : ASSIGN_2 + 1, :] = repeat(assign_2[...])


def side_data(spread, owner, obs, *args):
    count = len(args) + 3
    return pl.pallas_call(
        side_kernel,
        out_shape=jax.ShapeDtypeStruct((8, spread.shape[1]), F32),
        in_specs=[VMEM] * count,
        out_specs=VMEM,
        compiler_params=params(12),
        cost_estimate=cost(1.3),
        name="side",
    )(*args, spread, owner, obs)


def convert_kernel(master_embed, master_policy, master_value, embed_t, head, head_t):
    embed_t[...] = master_embed[...].T.astype(BF16)
    nact = master_policy.shape[1]
    wide = jnp.concatenate(
        [
            master_policy[...].T,
            master_value[...],
            jnp.zeros((PAD - 1, head_t.shape[1]), F32),
        ],
        axis=0,
    )
    head_t[...] = wide.astype(BF16)
    head[:, 0:nact] = master_policy[...].astype(BF16)
    head[:, nact:] = wide[nact:, :].T.astype(BF16)


def convert(master_embed, master_policy, master_value):
    feats, width = master_embed.shape
    nact = master_policy.shape[1]
    return pl.pallas_call(
        convert_kernel,
        out_shape=(
            jax.ShapeDtypeStruct((width, feats), BF16),
            jax.ShapeDtypeStruct((width, nact + PAD), BF16),
            jax.ShapeDtypeStruct((nact + PAD, width), BF16),
        ),
        in_specs=[VMEM] * 3,
        out_specs=(VMEM,) * 3,
        compiler_params=params(12),
        cost_estimate=cost(0.6),
        name="convert",
    )(master_embed, master_policy, master_value)


def learner_weights(slots, sides, out):
    learners, rows = out.shape[0], sides.shape[1]
    total = jnp.zeros((learners, rows), F32)
    first = lax.rem(iota((1, rows), 1), slots) == 0
    for place in range(0, sides.shape[0], 8):
        for length_at, assign_at in ((LENGTH, ASSIGN), (LENGTH_2, ASSIGN_2)):
            assign = sides[place + assign_at : place + assign_at + 1, :].astype(jnp.int32)
            length = jnp.where(first, sides[place + length_at : place + length_at + 1, :], 0.0)
            total = total + jnp.where(iota((learners, rows), 0) == assign, length, 0.0)
    summed = jnp.sum(total, axis=1, keepdims=True)
    out[...] = jnp.broadcast_to(1.0 / (learners * summed), out.shape)


def vtrace(slots, nact, side, weights, logits, values):
    rows = logits.shape[1]
    learners = weights.shape[0]
    behave = side[BEHAVE : BEHAVE + 1, :]
    reward = side[REWARD : REWARD + 1, :]
    length = side[LENGTH : LENGTH + 1, :].astype(jnp.int32)
    assign = side[ASSIGN : ASSIGN + 1, :].astype(jnp.int32)
    action = side[ACTION : ACTION + 1, :].astype(jnp.int32)
    weight = jnp.sum(
        jnp.where(iota((learners, rows), 0) == assign, weights[:, 0:1], 0.0), axis=0, keepdims=True
    )
    top = jnp.max(logits, axis=0, keepdims=True)
    exps = jnp.exp(logits - top)
    norm = jnp.sum(exps, axis=0, keepdims=True)
    logprob = logits - (top + jnp.log(norm))
    probs = exps * (1.0 / norm)
    onehot = iota(logits.shape, 0) == action
    taken = jnp.sum(jnp.where(onehot, logprob, 0.0), axis=0, keepdims=True)
    entropy = -jnp.sum(probs * logprob, axis=0, keepdims=True)
    step = lax.rem(iota((1, rows), 1), slots)
    inside = (step < length).astype(F32)
    beyond = (step + 1 < length).astype(F32)
    ratios = jnp.minimum(1.0, jnp.exp(taken - behave))

    def later(series, by):
        return pltpu.roll(series, rows - by, 1)

    deltas = inside * ratios * (reward + GAMMA * later(values, 1) * beyond - values)
    decay = GAMMA * ratios * inside
    corrections = deltas
    reach = 1
    while reach < slots:
        within = step + reach < slots
        corrections = corrections + decay * jnp.where(within, later(corrections, reach), 0.0)
        decay = decay * jnp.where(within, later(decay, reach), 0.0)
        reach *= 2
    targets = values + corrections
    advantage = ratios * (reward + GAMMA * later(targets, 1) * beyond - values)
    scale = weight * inside
    grad = scale * (
        -advantage * (onehot.astype(F32) - probs) + ENTROPY_COEF * probs * (logprob + entropy)
    )
    return grad, scale * (values - targets)


def forward(frames, embed_t, head_t, frames_t, hidden_t):
    width = embed_t.shape[0]
    tile = 256
    for index, block in enumerate(frames):
        frames_t[:, index * BLOCK : (index + 1) * BLOCK] = block[...].T
    for start in range(0, width, tile):
        here = slice(start, start + tile)
        hidden_t[here, :] = jnp.maximum(mm(embed_t[here, :], frames_t[...]), 0.0).astype(BF16)
    return mm(head_t[...], hidden_t[...])


def backward(slots, logits, side, weights, head, frames_t, hidden_t, preact_t, add):
    width, feats = head.shape[0], frames_t.shape[0]
    nact = logits.shape[0] - PAD
    tile = 256
    grad, grad_values = vtrace(
        slots, nact, side, weights, logits[0:nact, :], logits[nact : nact + 1, :]
    )
    pad = jnp.zeros((PAD - 1, grad.shape[1]), F32)
    grad_t = jnp.concatenate([grad, grad_values, pad], axis=0).astype(BF16)
    for start in range(0, width, tile):
        here = slice(start, start + tile)
        back = mm(head[here, :], grad_t)
        alive = hidden_t[here, :].astype(F32) > 0.0
        preact_t[here, :] = jnp.where(alive, back, 0.0).astype(BF16)
    for index in range(frames_t.shape[1] // BLOCK):
        lanes = slice(index * BLOCK, (index + 1) * BLOCK)
        add(index, slice(0, feats), mm_nt(frames_t[:, lanes], preact_t[:, lanes]))
        add(index, slice(feats, feats + nact + PAD), mm_nt(grad_t[:, lanes], hidden_t[:, lanes]))


def work(slots, frames, side, weights, embed_t, head, head_t, frames_t, hidden_t, preact_t, add):
    logits = forward(frames, embed_t, head_t, frames_t, hidden_t)
    backward(slots, logits, side, weights, head, frames_t, hidden_t, preact_t, add)


def side_of(sides, mask):
    return sides[8 * mask : 8 * mask + 8, :]


def ahead_kernel(*refs):
    (*frames, embed_t, head_t, frames_t, hidden_t, logits) = refs
    logits[...] = forward(frames, embed_t, head_t, frames_t, hidden_t)


def ahead(frames, embed_t, head_t):
    width, feats = embed_t.shape
    rows = len(frames) * BLOCK
    return pl.pallas_call(
        ahead_kernel,
        out_shape=(
            jax.ShapeDtypeStruct((feats, rows), BF16),
            jax.ShapeDtypeStruct((width, rows), BF16),
            jax.ShapeDtypeStruct((head_t.shape[0], rows), F32),
        ),
        in_specs=[VMEM] * (len(frames) + 2),
        out_specs=(VMEM,) * 3,
        compiler_params=params(20),
        cost_estimate=cost(1.6),
        name="ahead",
    )(*frames, embed_t, head_t)


def first_kernel(slots, *refs):
    (frames_t, hidden_t, logits, *pieces), mats, (sum_01, sum_2, weights, sides), scratch = (
        refs[0:7], refs[7:10], refs[10:14], refs[14:17])
    start = 0
    for piece in pieces:
        sides[start : start + piece.shape[0], :] = piece[...]
        start += piece.shape[0]
    learner_weights(slots, sides, weights)

    def add(index, rows, value):
        if index == 0:
            sum_01[rows, :] = value
        elif index == 1:
            sum_01[rows, :] += value
        else:
            sum_2[rows, :] = value

    side = jnp.concatenate([side_of(sides, mask) for mask in (0, 1, 2)], axis=1)
    backward(slots, logits[...], side, weights, mats[1], frames_t, hidden_t, scratch[2], add)


def second_kernel(slots, *refs):
    frames, (sides, weights, sum_01, sum_2), mats, (sum_0123, sum_4), scratch = (
        refs[0:2], refs[2:6], refs[6:9], refs[9:11], refs[11:14])

    def add(index, rows, value):
        if index == 0:
            sum_0123[rows, :] = sum_01[rows, :] + (sum_2[rows, :] + value)
        else:
            sum_4[rows, :] = value

    side = jnp.concatenate([side_of(sides, 3), side_of(sides, 4)], axis=1)
    work(slots, frames, side, weights, *mats, *scratch, add)


def third_kernel(slots, *refs):
    frames, (sides, weights, sum_4), mats, (sum_45, sum_6), scratch = (
        refs[0:2], refs[2:5], refs[5:8], refs[8:10], refs[10:13])

    def add(index, rows, value):
        if index == 0:
            sum_45[rows, :] = sum_4[rows, :] + value
        else:
            sum_6[rows, :] = value

    side = jnp.concatenate([side_of(sides, 5), side_of(sides, 6)], axis=1)
    work(slots, frames, side, weights, *mats, *scratch, add)


def fourth_kernel(slots, *refs):
    frames, (sides, weights, sum_0123, sum_45, sum_6), mats, out, scratch = (
        refs[0:1], refs[1:6], refs[6:9], refs[9], refs[10:13])

    def add(index, rows, value):
        out[rows, :] = (
            sum_0123[rows, :] + (sum_45[rows, :] + (sum_6[rows, :] + value))
        ).astype(BF16)

    work(slots, frames, side_of(sides, 7), weights, *mats, *scratch, add)


def local_kernel(slots, frames, side, weights, embed_t, head, head_t, out, *scratch):
    def add(index, rows, value):
        if index == 0:
            out[rows, :] = value
        else:
            out[rows, :] += value

    blocks = [frames.at[index] for index in range(frames.shape[0])]
    work(slots, blocks, side, weights, embed_t, head, head_t, *scratch, add)


def call(kernel, name, slots, blocks, args, mats, outs):
    width, feats = mats[0].shape
    rows = blocks * BLOCK
    return pl.pallas_call(
        functools.partial(kernel, slots),
        out_shape=outs,
        in_specs=[VMEM] * (len(args) + 3),
        out_specs=jax.tree.map(lambda leaf: VMEM, outs),
        scratch_shapes=[
            pltpu.VMEM((feats, rows), BF16),
            pltpu.VMEM((width, rows), BF16),
            pltpu.VMEM((width, rows), BF16),
        ],
        compiler_params=params(32),
        cost_estimate=cost(1.2 * blocks + 0.4),
        name=name,
    )(*args, *mats)


def update_kernel(
    feats, nact, mine, theirs, master_embed, master_policy, master_value,
    embed_moment, policy_moment, value_moment, next_obs,
    next_logits, new_embed, new_policy, new_value, new_em, new_pm, new_vm,
):
    def step(grad, moment, master, new_moment, new_master):
        held = MOMENTUM * moment[...] + grad
        new_moment[...] = held
        fresh = master[...] - LEARN_RATE * held
        new_master[...] = fresh
        return fresh

    def grad(start, size):
        return mine[start : start + size, :].astype(F32) + theirs[start : start + size, :].astype(F32)

    embed = step(grad(0, feats), embed_moment, master_embed, new_em, new_embed)
    hidden = jnp.maximum(mm(next_obs[...], embed.astype(BF16)), 0.0).astype(BF16)
    policy = step(grad(feats, nact).T, policy_moment, master_policy, new_pm, new_policy)
    step(grad(feats + nact, PAD)[0:1, :], value_moment, master_value, new_vm, new_value)
    next_logits[...] = mm(hidden, policy.astype(BF16)).astype(BF16)


def update(mine, theirs, *args):
    embed, policy, value = args[0], args[1], args[2]
    next_obs = args[6]
    feats, nact = embed.shape[0], policy.shape[1]
    shapes = [jax.ShapeDtypeStruct(array.shape, F32) for array in (embed, policy, value)]
    return pl.pallas_call(
        functools.partial(update_kernel, feats, nact),
        out_shape=(jax.ShapeDtypeStruct((next_obs.shape[0], nact), BF16), *shapes, *shapes),
        in_specs=[VMEM] * 9,
        out_specs=(VMEM,) * 7,
        compiler_params=params(32),
        cost_estimate=cost(3.4),
        name="update",
    )(mine, theirs, *args)


def gathered_grads(slots, own, side, mats):
    def exchange(array, mask, name):
        with jax.named_scope(name):
            return lax.ppermute(array, "hst", [(at, at ^ mask) for at in range(8)])

    b2 = exchange(own, 2, "b2")
    b1 = exchange(own, 1, "b1")
    pair = jnp.concatenate([side, exchange(side, 1, "side_y")], axis=0)
    pair, _, _ = lax.optimization_barrier((pair, b2, b1))
    pieces = [pair] + [exchange(pair, 2 * mask, "side_z") for mask in (1, 2, 3)]
    again, _ = lax.optimization_barrier((own, side))
    b4 = exchange(again, 4, "b4")
    b3 = exchange(b2, 1, "b3")
    b5 = exchange(b4, 1, "b5")
    b6 = exchange(b4, 2, "b6")
    pieces, b3 = lax.optimization_barrier((pieces, b3))
    width, feats = mats[0].shape
    grads = jax.ShapeDtypeStruct((feats + mats[2].shape[0], width), F32)
    weights = jax.ShapeDtypeStruct((16, 128), F32)
    sides = jax.ShapeDtypeStruct((64, side.shape[1]), F32)
    done = ahead((own, b1, b2), mats[0], mats[2])
    sum_01, sum_2, weights, sides = call(
        first_kernel, "first", slots, 3, (*done, *pieces), mats, (grads, grads, weights, sides),
    )
    b6, sum_2 = lax.optimization_barrier((b6, sum_2))
    b3, _ = lax.optimization_barrier((b3, b6))
    sum_0123, sum_4 = call(
        second_kernel, "second", slots, 2, (b3, b4, sides, weights, sum_01, sum_2), mats,
        (grads, grads),
    )
    b7 = exchange(b6, 1, "b7")
    sum_45, sum_6 = call(
        third_kernel, "third", slots, 2, (b5, b6, sides, weights, sum_4), mats, (grads, grads),
    )
    return call(
        fourth_kernel, "fourth", slots, 1, (b7, sides, weights, sum_0123, sum_45, sum_6), mats,
        jax.ShapeDtypeStruct(grads.shape, BF16),
    )


def body(
    n_hst, n_cores, observations, lengths, actions, rewards, assign, actor_embed, actor_policy,
    master_embed, master_policy, master_value, embed_moment, policy_moment, value_moment, next_obs,
):
    traj, slots, feats = observations.shape
    learners = n_hst * n_cores
    rows = traj * slots
    own = observations.reshape(rows, feats)
    value_row = master_value.reshape(1, -1)
    spread, owner = select(traj, slots)
    flip = [(core, core ^ 1) for core in range(n_cores)]
    there = [lax.ppermute(array, "cores", flip) for array in (lengths, assign)]
    gather = n_hst == 8 and n_cores == 2 and rows == BLOCK
    side = side_data(
        spread, owner, own, *[array.reshape(1, -1) for array in (lengths, assign, *there)],
        actions, rewards, actor_embed, actor_policy,
    )
    late_row, _ = lax.optimization_barrier((value_row, side))
    mats = convert(master_embed, master_policy, late_row)
    if gather:
        mine = gathered_grads(slots, own, side, mats)
        theirs = lax.ppermute(mine, "cores", flip)
    else:
        named = (assign[:, None] == jnp.arange(learners)[None, :]).astype(F32)
        totals = lax.psum(jnp.sum(named * lengths[:, None].astype(F32), axis=0), AXES)
        weights = jnp.broadcast_to((1.0 / (learners * totals))[:, None], (learners, 128))
        grads = call(
            local_kernel, "local", slots, rows // BLOCK,
            (own.reshape(-1, BLOCK, feats), side, weights), mats,
            jax.ShapeDtypeStruct((feats + mats[2].shape[0], mats[0].shape[0]), F32),
        )
        mine = lax.psum(grads, AXES)
        theirs = jnp.zeros_like(mine)
    outs = update(
        mine, theirs, master_embed, master_policy, value_row, embed_moment, policy_moment,
        value_moment.reshape(1, -1), next_obs,
    )
    logits, new_embed, new_policy, new_value, new_em, new_pm, new_vm = outs
    return logits, new_embed, new_policy, new_value.reshape(-1), new_em, new_pm, new_vm.reshape(-1)


def solution(mesh):
    split = P(("group", "hst", "cores"))
    whole = P("group")
    return jax.shard_map(
        functools.partial(body, mesh.shape["hst"], mesh.shape["cores"]),
        mesh=mesh,
        in_specs=(split,) * 5 + (whole,) * 8 + (split,),
        out_specs=(split,) + (whole,) * 6,
        check_vma=False,
    )
```

```python
import functools

import jax
import jax.numpy as jnp
from jax import lax
from jax.experimental import pallas as pl
from jax.experimental.pallas import tpu as pltpu
from jax.sharding import PartitionSpec as P

GAMMA = 0.99
ENTROPY_COEF = 0.1
MOMENTUM = 0.9
LEARN_RATE = 0.05
AXES = ("hst", "cores")
F32 = jnp.float32
BF16 = jnp.bfloat16
VMEM = pl.BlockSpec(memory_space=pltpu.VMEM)
MIB = 2**20
BLOCK = 256
PAD = 16
BEHAVE, ACTION, REWARD, LENGTH, ASSIGN, LENGTH_2, ASSIGN_2 = range(7)


def iota(shape, dim):
    return lax.broadcasted_iota(jnp.int32, shape, dim)


def mm(a, b):
    return jnp.dot(a, b, preferred_element_type=F32)


def mm_nt(a, b):
    return lax.dot_general(a, b, (((1,), (1,)), ((), ())), preferred_element_type=F32)


def params(mib):
    return pltpu.CompilerParams(vmem_limit_bytes=mib * MIB)


def cost(micros):
    return pl.CostEstimate(flops=int(micros * 1.1e9), bytes_accessed=0, transcendentals=0)


def select_kernel(spread, owner):
    traj, rows = owner.shape
    slots = spread.shape[0]
    spread[...] = (lax.rem(iota((slots, rows), 1), slots) == iota((slots, rows), 0)).astype(F32)
    owner[...] = (lax.div(iota((traj, rows), 1), slots) == iota((traj, rows), 0)).astype(F32)


def select(traj, slots):
    rows = traj * slots
    return pl.pallas_call(
        select_kernel,
        out_shape=(jax.ShapeDtypeStruct((slots, rows), F32), jax.ShapeDtypeStruct((traj, rows), F32)),
        out_specs=(VMEM, VMEM),
        compiler_params=params(4),
        cost_estimate=cost(40),
        name="select",
    )()


def side_kernel(
    lengths, assign, lengths_2, assign_2, actions, rewards, actor_embed, actor_policy,
    spread, owner, obs, side,
):

    def flat(series):
        wide = jnp.dot(
            series, spread[...], precision=lax.Precision.HIGHEST, preferred_element_type=F32
        )
        return jnp.sum(wide * owner[...], axis=0, keepdims=True)

    def repeat(series):
        return jnp.dot(
            series.astype(F32), owner[...],
            precision=lax.Precision.HIGHEST, preferred_element_type=F32,
        )

    action = flat(actions[...].astype(F32))
    hidden = jnp.maximum(mm(obs[...], actor_embed[...]), 0.0).astype(BF16)
    logits = mm(hidden, actor_policy[...]).T
    top = jnp.max(logits, axis=0, keepdims=True)
    shifted = logits - top
    norm = jnp.log(jnp.sum(jnp.exp(shifted), axis=0, keepdims=True))
    onehot = iota(logits.shape, 0) == action.astype(jnp.int32)
    side[...] = jnp.zeros_like(side)
    side[BEHAVE : BEHAVE + 1, :] = (
        jnp.sum(jnp.where(onehot, shifted, 0.0), axis=0, keepdims=True) - norm
    )
    side[ACTION : ACTION + 1, :] = action
    side[REWARD : REWARD + 1, :] = flat(rewards[...])
    side[LENGTH : LENGTH + 1, :] = repeat(lengths[...])
    side[ASSIGN : ASSIGN + 1, :] = repeat(assign[...])
    side[LENGTH_2 : LENGTH_2 + 1, :] = repeat(lengths_2[...])
    side[ASSIGN_2 : ASSIGN_2 + 1, :] = repeat(assign_2[...])


def side_data(spread, owner, obs, *args):
    count = len(args) + 3
    return pl.pallas_call(
        side_kernel,
        out_shape=jax.ShapeDtypeStruct((8, spread.shape[1]), F32),
        in_specs=[VMEM] * count,
        out_specs=VMEM,
        compiler_params=params(12),
        cost_estimate=cost(1.3),
        name="side",
    )(*args, spread, owner, obs)


def convert_kernel(master_embed, master_policy, master_value, embed_t, head, head_t):
    embed_t[...] = master_embed[...].T.astype(BF16)
    nact = master_policy.shape[1]
    wide = jnp.concatenate(
        [
            master_policy[...].T,
            master_value[...],
            jnp.zeros((PAD - 1, head_t.shape[1]), F32),
        ],
        axis=0,
    )
    head_t[...] = wide.astype(BF16)
    head[:, 0:nact] = master_policy[...].astype(BF16)
    head[:, nact:] = wide[nact:, :].T.astype(BF16)


def convert(master_embed, master_policy, master_value):
    feats, width = master_embed.shape
    nact = master_policy.shape[1]
    return pl.pallas_call(
        convert_kernel,
        out_shape=(
            jax.ShapeDtypeStruct((width, feats), BF16),
            jax.ShapeDtypeStruct((width, nact + PAD), BF16),
            jax.ShapeDtypeStruct((nact + PAD, width), BF16),
        ),
        in_specs=[VMEM] * 3,
        out_specs=(VMEM,) * 3,
        compiler_params=params(12),
        cost_estimate=cost(0.6),
        name="convert",
    )(master_embed, master_policy, master_value)


def learner_weights(slots, sides, out):
    learners, rows = out.shape[0], sides.shape[1]
    total = jnp.zeros((learners, rows), F32)
    first = lax.rem(iota((1, rows), 1), slots) == 0
    for place in range(0, sides.shape[0], 8):
        for length_at, assign_at in ((LENGTH, ASSIGN), (LENGTH_2, ASSIGN_2)):
            assign = sides[place + assign_at : place + assign_at + 1, :].astype(jnp.int32)
            length = jnp.where(first, sides[place + length_at : place + length_at + 1, :], 0.0)
            total = total + jnp.where(iota((learners, rows), 0) == assign, length, 0.0)
    summed = jnp.sum(total, axis=1, keepdims=True)
    out[...] = jnp.broadcast_to(1.0 / (learners * summed), out.shape)


def vtrace(slots, nact, side, weights, logits, values):
    rows = logits.shape[1]
    learners = weights.shape[0]
    behave = side[BEHAVE : BEHAVE + 1, :]
    reward = side[REWARD : REWARD + 1, :]
    length = side[LENGTH : LENGTH + 1, :].astype(jnp.int32)
    assign = side[ASSIGN : ASSIGN + 1, :].astype(jnp.int32)
    action = side[ACTION : ACTION + 1, :].astype(jnp.int32)
    weight = jnp.sum(
        jnp.where(iota((learners, rows), 0) == assign, weights[:, 0:1], 0.0), axis=0, keepdims=True
    )
    top = jnp.max(logits, axis=0, keepdims=True)
    exps = jnp.exp(logits - top)
    norm = jnp.sum(exps, axis=0, keepdims=True)
    logprob = logits - (top + jnp.log(norm))
    probs = exps * (1.0 / norm)
    onehot = iota(logits.shape, 0) == action
    taken = jnp.sum(jnp.where(onehot, logprob, 0.0), axis=0, keepdims=True)
    entropy = -jnp.sum(probs * logprob, axis=0, keepdims=True)
    step = lax.rem(iota((1, rows), 1), slots)
    inside = (step < length).astype(F32)
    beyond = (step + 1 < length).astype(F32)
    ratios = jnp.minimum(1.0, jnp.exp(taken - behave))

    def later(series, by):
        return pltpu.roll(series, rows - by, 1)

    deltas = inside * ratios * (reward + GAMMA * later(values, 1) * beyond - values)
    decay = GAMMA * ratios * inside
    corrections = deltas
    reach = 1
    while reach < slots:
        within = step + reach < slots
        corrections = corrections + decay * jnp.where(within, later(corrections, reach), 0.0)
        decay = decay * jnp.where(within, later(decay, reach), 0.0)
        reach *= 2
    targets = values + corrections
    advantage = ratios * (reward + GAMMA * later(targets, 1) * beyond - values)
    scale = weight * inside
    grad = scale * (
        -advantage * (onehot.astype(F32) - probs) + ENTROPY_COEF * probs * (logprob + entropy)
    )
    return grad, scale * (values - targets)


def forward(frames, embed_t, head_t, frames_t, hidden_t):
    width = embed_t.shape[0]
    tile = 256
    for index, block in enumerate(frames):
        frames_t[:, index * BLOCK : (index + 1) * BLOCK] = block[...].T
    for start in range(0, width, tile):
        here = slice(start, start + tile)
        hidden_t[here, :] = jnp.maximum(mm(embed_t[here, :], frames_t[...]), 0.0).astype(BF16)
    return mm(head_t[...], hidden_t[...])


def backward(slots, logits, side, weights, head, frames_t, hidden_t, preact_t, add):
    width, feats = head.shape[0], frames_t.shape[0]
    nact = logits.shape[0] - PAD
    tile = 256
    grad, grad_values = vtrace(
        slots, nact, side, weights, logits[0:nact, :], logits[nact : nact + 1, :]
    )
    pad = jnp.zeros((PAD - 1, grad.shape[1]), F32)
    grad_t = jnp.concatenate([grad, grad_values, pad], axis=0).astype(BF16)
    for start in range(0, width, tile):
        here = slice(start, start + tile)
        back = mm(head[here, :], grad_t)
        alive = hidden_t[here, :].astype(F32) > 0.0
        preact_t[here, :] = jnp.where(alive, back, 0.0).astype(BF16)
    for index in range(frames_t.shape[1] // BLOCK):
        lanes = slice(index * BLOCK, (index + 1) * BLOCK)
        add(index, slice(0, feats), mm_nt(frames_t[:, lanes], preact_t[:, lanes]))
        add(index, slice(feats, feats + nact + PAD), mm_nt(grad_t[:, lanes], hidden_t[:, lanes]))


def work(slots, frames, side, weights, embed_t, head, head_t, frames_t, hidden_t, preact_t, add):
    logits = forward(frames, embed_t, head_t, frames_t, hidden_t)
    backward(slots, logits, side, weights, head, frames_t, hidden_t, preact_t, add)


def side_of(sides, back, flip):
    line = lax.div(lax.axis_index("hst"), 2)
    there = lax.bitwise_xor(line, lax.bitwise_and(line + 4 - back, 3))
    return sides[pl.ds(pl.multiple_of(8 * (2 * there + flip), 8), 8), :]


def ahead_kernel(*refs):
    (*frames, embed_t, head_t, frames_t, hidden_t, logits) = refs
    logits[...] = forward(frames, embed_t, head_t, frames_t, hidden_t)


def ahead(frames, embed_t, head_t):
    width, feats = embed_t.shape
    rows = len(frames) * BLOCK
    return pl.pallas_call(
        ahead_kernel,
        out_shape=(
            jax.ShapeDtypeStruct((feats, rows), BF16),
            jax.ShapeDtypeStruct((width, rows), BF16),
            jax.ShapeDtypeStruct((head_t.shape[0], rows), F32),
        ),
        in_specs=[VMEM] * (len(frames) + 2),
        out_specs=(VMEM,) * 3,
        compiler_params=params(20),
        cost_estimate=cost(1.6),
        name="ahead",
    )(*frames, embed_t, head_t)


def first_kernel(slots, *refs):
    (frames_t, hidden_t, logits, *pieces), mats, (sum_0, sum_1, weights, sides), scratch = (
        refs[0:7], refs[7:10], refs[10:14], refs[14:17])
    start = 0
    for piece in pieces:
        sides[start : start + piece.shape[0], :] = piece[...]
        start += piece.shape[0]
    learner_weights(slots, sides, weights)

    def add(index, rows, value):
        if index == 0:
            sum_0[rows, :] = value
        elif index == 1:
            sum_0[rows, :] += value
        else:
            sum_1[rows, :] = value

    side = jnp.concatenate([side_of(sides, *at) for at in ((0, 0), (0, 1), (1, 0))], axis=1)
    backward(slots, logits[...], side, weights, mats[1], frames_t, hidden_t, scratch[2], add)


def second_kernel(slots, *refs):
    frames, (sides, weights, sum_1), mats, (sum_1y, sum_2), scratch = (
        refs[0:2], refs[2:5], refs[5:8], refs[8:10], refs[10:13])

    def add(index, rows, value):
        if index == 0:
            sum_1y[rows, :] = sum_1[rows, :] + value
        else:
            sum_2[rows, :] = value

    side = jnp.concatenate([side_of(sides, 1, 1), side_of(sides, 2, 0)], axis=1)
    work(slots, frames, side, weights, *mats, *scratch, add)


def third_kernel(slots, *refs):
    frames, (sides, weights, sum_0, sum_2), mats, (even, sum_3), scratch = (
        refs[0:2], refs[2:6], refs[6:9], refs[9:11], refs[11:14])

    def add(index, rows, value):
        if index == 0:
            even[rows, :] = sum_0[rows, :] + (sum_2[rows, :] + value)
        else:
            sum_3[rows, :] = value

    side = jnp.concatenate([side_of(sides, 2, 1), side_of(sides, 3, 0)], axis=1)
    work(slots, frames, side, weights, *mats, *scratch, add)


def fourth_kernel(slots, *refs):
    frames, (sides, weights, even, sum_1y, sum_3), mats, out, scratch = (
        refs[0:1], refs[1:6], refs[6:9], refs[9], refs[10:13])

    def add(index, rows, value):
        out[rows, :] = (
            even[rows, :] + (sum_1y[rows, :] + (sum_3[rows, :] + value))
        ).astype(BF16)

    work(slots, frames, side_of(sides, 3, 1), weights, *mats, *scratch, add)


def local_kernel(slots, frames, side, weights, embed_t, head, head_t, out, *scratch):
    def add(index, rows, value):
        if index == 0:
            out[rows, :] = value
        else:
            out[rows, :] += value

    blocks = [frames.at[index] for index in range(frames.shape[0])]
    work(slots, blocks, side, weights, embed_t, head, head_t, *scratch, add)


def call(kernel, name, slots, blocks, args, mats, outs):
    width, feats = mats[0].shape
    rows = blocks * BLOCK
    return pl.pallas_call(
        functools.partial(kernel, slots),
        out_shape=outs,
        in_specs=[VMEM] * (len(args) + 3),
        out_specs=jax.tree.map(lambda leaf: VMEM, outs),
        scratch_shapes=[
            pltpu.VMEM((feats, rows), BF16),
            pltpu.VMEM((width, rows), BF16),
            pltpu.VMEM((width, rows), BF16),
        ],
        compiler_params=params(32),
        cost_estimate=cost(1.2 * blocks + 0.4),
        name=name,
    )(*args, *mats)


def update_kernel(
    feats, nact, mine, theirs, master_embed, master_policy, master_value,
    embed_moment, policy_moment, value_moment, next_obs,
    next_logits, new_embed, new_policy, new_value, new_em, new_pm, new_vm,
):
    def step(grad, moment, master, new_moment, new_master):
        held = MOMENTUM * moment[...] + grad
        new_moment[...] = held
        fresh = master[...] - LEARN_RATE * held
        new_master[...] = fresh
        return fresh

    def grad(start, size):
        return mine[start : start + size, :].astype(F32) + theirs[start : start + size, :].astype(F32)

    embed = step(grad(0, feats), embed_moment, master_embed, new_em, new_embed)
    hidden = jnp.maximum(mm(next_obs[...], embed.astype(BF16)), 0.0).astype(BF16)
    policy = step(grad(feats, nact).T, policy_moment, master_policy, new_pm, new_policy)
    step(grad(feats + nact, PAD)[0:1, :], value_moment, master_value, new_vm, new_value)
    next_logits[...] = mm(hidden, policy.astype(BF16)).astype(BF16)


def update(mine, theirs, *args):
    embed, policy, value = args[0], args[1], args[2]
    next_obs = args[6]
    feats, nact = embed.shape[0], policy.shape[1]
    shapes = [jax.ShapeDtypeStruct(array.shape, F32) for array in (embed, policy, value)]
    return pl.pallas_call(
        functools.partial(update_kernel, feats, nact),
        out_shape=(jax.ShapeDtypeStruct((next_obs.shape[0], nact), BF16), *shapes, *shapes),
        in_specs=[VMEM] * 9,
        out_specs=(VMEM,) * 7,
        compiler_params=params(32),
        cost_estimate=cost(3.4),
        name="update",
    )(mine, theirs, *args)


def gathered_grads(slots, own, side, mats):
    def exchange(array, mask, name):
        with jax.named_scope(name):
            return lax.ppermute(array, "hst", [(at, at ^ mask) for at in range(8)])

    def shift(array, name):
        with jax.named_scope(name):
            return lax.ppermute(array, "hst", [(at, (at + 2) % 8) for at in range(8)])

    one = shift(own, "one")
    own_y = exchange(own, 1, "own_y")
    pair = jnp.concatenate([side, exchange(side, 1, "side_y")], axis=0)
    pair, _, _ = lax.optimization_barrier((pair, one, own_y))
    pieces = [pair] + [exchange(pair, 2 * mask, "side_z") for mask in (1, 2, 3)]
    two = shift(one, "two")
    one_y = exchange(one, 1, "one_y")
    width, feats = mats[0].shape
    grads = jax.ShapeDtypeStruct((feats + mats[2].shape[0], width), F32)
    weights = jax.ShapeDtypeStruct((16, 128), F32)
    sides = jax.ShapeDtypeStruct((64, side.shape[1]), F32)
    done = ahead((own, own_y, one), mats[0], mats[2])
    done, one_y, two = lax.optimization_barrier((done, one_y, two))
    three = shift(two, "three")
    two_y = exchange(two, 1, "two_y")
    sum_0, sum_1, weights, sides = call(
        first_kernel, "first", slots, 3, (*done, *pieces), mats, (grads, grads, weights, sides),
    )
    sum_1y, sum_2 = call(
        second_kernel, "second", slots, 2, (one_y, two, sides, weights, sum_1), mats,
        (grads, grads),
    )
    three_y = exchange(three, 1, "three_y")
    even, sum_3 = call(
        third_kernel, "third", slots, 2, (two_y, three, sides, weights, sum_0, sum_2), mats,
        (grads, grads),
    )
    return call(
        fourth_kernel, "fourth", slots, 1, (three_y, sides, weights, even, sum_1y, sum_3), mats,
        jax.ShapeDtypeStruct(grads.shape, BF16),
    )


def body(
    n_hst, n_cores, observations, lengths, actions, rewards, assign, actor_embed, actor_policy,
    master_embed, master_policy, master_value, embed_moment, policy_moment, value_moment, next_obs,
):
    traj, slots, feats = observations.shape
    learners = n_hst * n_cores
    rows = traj * slots
    own = observations.reshape(rows, feats)
    value_row = master_value.reshape(1, -1)
    spread, owner = select(traj, slots)
    flip = [(core, core ^ 1) for core in range(n_cores)]
    there = [lax.ppermute(array, "cores", flip) for array in (lengths, assign)]
    gather = n_hst == 8 and n_cores == 2 and rows == BLOCK
    side = side_data(
        spread, owner, own, *[array.reshape(1, -1) for array in (lengths, assign, *there)],
        actions, rewards, actor_embed, actor_policy,
    )
    late_row, _ = lax.optimization_barrier((value_row, side))
    mats = convert(master_embed, master_policy, late_row)
    if gather:
        mine = gathered_grads(slots, own, side, mats)
        theirs = lax.ppermute(mine, "cores", flip)
    else:
        named = (assign[:, None] == jnp.arange(learners)[None, :]).astype(F32)
        totals = lax.psum(jnp.sum(named * lengths[:, None].astype(F32), axis=0), AXES)
        weights = jnp.broadcast_to((1.0 / (learners * totals))[:, None], (learners, 128))
        grads = call(
            local_kernel, "local", slots, rows // BLOCK,
            (own.reshape(-1, BLOCK, feats), side, weights), mats,
            jax.ShapeDtypeStruct((feats + mats[2].shape[0], mats[0].shape[0]), F32),
        )
        mine = lax.psum(grads, AXES)
        theirs = jnp.zeros_like(mine)
    outs = update(
        mine, theirs, master_embed, master_policy, value_row, embed_moment, policy_moment,
        value_moment.reshape(1, -1), next_obs,
    )
    logits, new_embed, new_policy, new_value, new_em, new_pm, new_vm = outs
    return logits, new_embed, new_policy, new_value.reshape(-1), new_em, new_pm, new_vm.reshape(-1)


def solution(mesh):
    split = P(("group", "hst", "cores"))
    whole = P("group")
    return jax.shard_map(
        functools.partial(body, mesh.shape["hst"], mesh.shape["cores"]),
        mesh=mesh,
        in_specs=(split,) * 5 + (whole,) * 8 + (split,),
        out_specs=(split,) + (whole,) * 6,
        check_vma=False,
    )
```

```python
import functools

import jax
import jax.numpy as jnp
from jax import lax
from jax.experimental import pallas as pl
from jax.experimental.pallas import tpu as pltpu
from jax.sharding import PartitionSpec as P

GAMMA = 0.99
ENTROPY_COEF = 0.1
MOMENTUM = 0.9
LEARN_RATE = 0.05
AXES = ("hst", "cores")
F32 = jnp.float32
BF16 = jnp.bfloat16
VMEM = pl.BlockSpec(memory_space=pltpu.VMEM)
MIB = 2**20
BLOCK = 256
PAD = 16
BEHAVE, ACTION, REWARD, LENGTH, ASSIGN, LENGTH_2, ASSIGN_2 = range(7)


def iota(shape, dim):
    return lax.broadcasted_iota(jnp.int32, shape, dim)


def mm(a, b):
    return jnp.dot(a, b, preferred_element_type=F32)


def mm_nt(a, b):
    return lax.dot_general(a, b, (((1,), (1,)), ((), ())), preferred_element_type=F32)


def params(mib):
    return pltpu.CompilerParams(vmem_limit_bytes=mib * MIB)


def cost(micros):
    return pl.CostEstimate(flops=int(micros * 1.1e9), bytes_accessed=0, transcendentals=0)


def select_kernel(spread, owner):
    traj, rows = owner.shape
    slots = spread.shape[0]
    spread[...] = (lax.rem(iota((slots, rows), 1), slots) == iota((slots, rows), 0)).astype(F32)
    owner[...] = (lax.div(iota((traj, rows), 1), slots) == iota((traj, rows), 0)).astype(F32)


def select(traj, slots):
    rows = traj * slots
    return pl.pallas_call(
        select_kernel,
        out_shape=(jax.ShapeDtypeStruct((slots, rows), F32), jax.ShapeDtypeStruct((traj, rows), F32)),
        out_specs=(VMEM, VMEM),
        compiler_params=params(4),
        cost_estimate=cost(40),
        name="select",
    )()


def side_kernel(
    lengths, assign, lengths_2, assign_2, actions, rewards, actor_embed, actor_policy,
    spread, owner, obs, side,
):

    def flat(series):
        wide = jnp.dot(
            series, spread[...], precision=lax.Precision.HIGHEST, preferred_element_type=F32
        )
        return jnp.sum(wide * owner[...], axis=0, keepdims=True)

    def repeat(series):
        return jnp.dot(
            series.astype(F32), owner[...],
            precision=lax.Precision.HIGHEST, preferred_element_type=F32,
        )

    action = flat(actions[...].astype(F32))
    hidden = jnp.maximum(mm(obs[...], actor_embed[...]), 0.0).astype(BF16)
    logits = mm(hidden, actor_policy[...]).T
    top = jnp.max(logits, axis=0, keepdims=True)
    shifted = logits - top
    norm = jnp.log(jnp.sum(jnp.exp(shifted), axis=0, keepdims=True))
    onehot = iota(logits.shape, 0) == action.astype(jnp.int32)
    side[...] = jnp.zeros_like(side)
    side[BEHAVE : BEHAVE + 1, :] = (
        jnp.sum(jnp.where(onehot, shifted, 0.0), axis=0, keepdims=True) - norm
    )
    side[ACTION : ACTION + 1, :] = action
    side[REWARD : REWARD + 1, :] = flat(rewards[...])
    side[LENGTH : LENGTH + 1, :] = repeat(lengths[...])
    side[ASSIGN : ASSIGN + 1, :] = repeat(assign[...])
    side[LENGTH_2 : LENGTH_2 + 1, :] = repeat(lengths_2[...])
    side[ASSIGN_2 : ASSIGN_2 + 1, :] = repeat(assign_2[...])


def side_data(spread, owner, obs, *args):
    count = len(args) + 3
    return pl.pallas_call(
        side_kernel,
        out_shape=jax.ShapeDtypeStruct((8, spread.shape[1]), F32),
        in_specs=[VMEM] * count,
        out_specs=VMEM,
        compiler_params=params(12),
        cost_estimate=cost(1.3),
        name="side",
    )(*args, spread, owner, obs)


def convert_kernel(master_embed, master_policy, master_value, embed_t, head, head_t):
    embed_t[...] = master_embed[...].T.astype(BF16)
    nact = master_policy.shape[1]
    wide = jnp.concatenate(
        [
            master_policy[...].T,
            master_value[...],
            jnp.zeros((PAD - 1, head_t.shape[1]), F32),
        ],
        axis=0,
    )
    head_t[...] = wide.astype(BF16)
    head[:, 0:nact] = master_policy[...].astype(BF16)
    head[:, nact:] = wide[nact:, :].T.astype(BF16)


def convert(master_embed, master_policy, master_value):
    feats, width = master_embed.shape
    nact = master_policy.shape[1]
    return pl.pallas_call(
        convert_kernel,
        out_shape=(
            jax.ShapeDtypeStruct((width, feats), BF16),
            jax.ShapeDtypeStruct((width, nact + PAD), BF16),
            jax.ShapeDtypeStruct((nact + PAD, width), BF16),
        ),
        in_specs=[VMEM] * 3,
        out_specs=(VMEM,) * 3,
        compiler_params=params(12),
        cost_estimate=cost(0.6),
        name="convert",
    )(master_embed, master_policy, master_value)


def learner_weights(slots, sides, out):
    learners, rows = out.shape[0], sides.shape[1]
    total = jnp.zeros((learners, rows), F32)
    first = lax.rem(iota((1, rows), 1), slots) == 0
    for place in range(0, sides.shape[0], 8):
        for length_at, assign_at in ((LENGTH, ASSIGN), (LENGTH_2, ASSIGN_2)):
            assign = sides[place + assign_at : place + assign_at + 1, :].astype(jnp.int32)
            length = jnp.where(first, sides[place + length_at : place + length_at + 1, :], 0.0)
            total = total + jnp.where(iota((learners, rows), 0) == assign, length, 0.0)
    summed = jnp.sum(total, axis=1, keepdims=True)
    out[...] = jnp.broadcast_to(1.0 / (learners * summed), out.shape)


def vtrace(slots, nact, side, weights, logits, values):
    rows = logits.shape[1]
    learners = weights.shape[0]
    behave = side[BEHAVE : BEHAVE + 1, :]
    reward = side[REWARD : REWARD + 1, :]
    length = side[LENGTH : LENGTH + 1, :].astype(jnp.int32)
    assign = side[ASSIGN : ASSIGN + 1, :].astype(jnp.int32)
    action = side[ACTION : ACTION + 1, :].astype(jnp.int32)
    weight = jnp.sum(
        jnp.where(iota((learners, rows), 0) == assign, weights[:, 0:1], 0.0), axis=0, keepdims=True
    )
    top = jnp.max(logits, axis=0, keepdims=True)
    exps = jnp.exp(logits - top)
    norm = jnp.sum(exps, axis=0, keepdims=True)
    logprob = logits - (top + jnp.log(norm))
    probs = exps * (1.0 / norm)
    onehot = iota(logits.shape, 0) == action
    taken = jnp.sum(jnp.where(onehot, logprob, 0.0), axis=0, keepdims=True)
    entropy = -jnp.sum(probs * logprob, axis=0, keepdims=True)
    step = lax.rem(iota((1, rows), 1), slots)
    inside = (step < length).astype(F32)
    beyond = (step + 1 < length).astype(F32)
    ratios = jnp.minimum(1.0, jnp.exp(taken - behave))

    def later(series, by):
        return pltpu.roll(series, rows - by, 1)

    deltas = inside * ratios * (reward + GAMMA * later(values, 1) * beyond - values)
    decay = GAMMA * ratios * inside
    corrections = deltas
    reach = 1
    while reach < slots:
        within = step + reach < slots
        corrections = corrections + decay * jnp.where(within, later(corrections, reach), 0.0)
        decay = decay * jnp.where(within, later(decay, reach), 0.0)
        reach *= 2
    targets = values + corrections
    advantage = ratios * (reward + GAMMA * later(targets, 1) * beyond - values)
    scale = weight * inside
    grad = scale * (
        -advantage * (onehot.astype(F32) - probs) + ENTROPY_COEF * probs * (logprob + entropy)
    )
    return grad, scale * (values - targets)


def forward(frames, embed_t, head_t, frames_t, hidden_t):
    width = embed_t.shape[0]
    tile = 256
    for index, block in enumerate(frames):
        frames_t[:, index * BLOCK : (index + 1) * BLOCK] = block[...].T
    for start in range(0, width, tile):
        here = slice(start, start + tile)
        hidden_t[here, :] = jnp.maximum(mm(embed_t[here, :], frames_t[...]), 0.0).astype(BF16)
    return mm(head_t[...], hidden_t[...])


def backward(slots, logits, side, weights, head, frames_t, hidden_t, preact_t, add):
    width, feats = head.shape[0], frames_t.shape[0]
    nact = logits.shape[0] - PAD
    tile = 256
    grad, grad_values = vtrace(
        slots, nact, side, weights, logits[0:nact, :], logits[nact : nact + 1, :]
    )
    pad = jnp.zeros((PAD - 1, grad.shape[1]), F32)
    grad_t = jnp.concatenate([grad, grad_values, pad], axis=0).astype(BF16)
    for start in range(0, width, tile):
        here = slice(start, start + tile)
        back = mm(head[here, :], grad_t)
        alive = hidden_t[here, :].astype(F32) > 0.0
        preact_t[here, :] = jnp.where(alive, back, 0.0).astype(BF16)
    for index in range(frames_t.shape[1] // BLOCK):
        lanes = slice(index * BLOCK, (index + 1) * BLOCK)
        add(index, slice(0, feats), mm_nt(frames_t[:, lanes], preact_t[:, lanes]))
        add(index, slice(feats, feats + nact + PAD), mm_nt(grad_t[:, lanes], hidden_t[:, lanes]))


def work(slots, frames, side, weights, embed_t, head, head_t, frames_t, hidden_t, preact_t, add):
    logits = forward(frames, embed_t, head_t, frames_t, hidden_t)
    backward(slots, logits, side, weights, head, frames_t, hidden_t, preact_t, add)


def on_mid():
    line = lax.div(lax.axis_index("hst"), 2)
    return jnp.logical_or(line == 1, line == 2)


def side_of(sides, mask):
    if mask >= 4:
        mask = lax.bitwise_xor(mask, jnp.where(on_mid(), 2, 0))
        return sides[pl.ds(pl.multiple_of(8 * mask, 8), 8), :]
    return sides[8 * mask : 8 * mask + 8, :]


def ahead_kernel(*refs):
    (*frames, embed_t, head_t, frames_t, hidden_t, logits) = refs
    logits[...] = forward(frames, embed_t, head_t, frames_t, hidden_t)


def ahead(frames, embed_t, head_t):
    width, feats = embed_t.shape
    rows = len(frames) * BLOCK
    return pl.pallas_call(
        ahead_kernel,
        out_shape=(
            jax.ShapeDtypeStruct((feats, rows), BF16),
            jax.ShapeDtypeStruct((width, rows), BF16),
            jax.ShapeDtypeStruct((head_t.shape[0], rows), F32),
        ),
        in_specs=[VMEM] * (len(frames) + 2),
        out_specs=(VMEM,) * 3,
        compiler_params=params(20),
        cost_estimate=cost(1.6),
        name="ahead",
    )(*frames, embed_t, head_t)


def first_kernel(slots, *refs):
    (frames_t, hidden_t, logits, *pieces), mats, (sum_01, sum_2, weights, sides), scratch = (
        refs[0:6], refs[6:9], refs[9:13], refs[13:16])
    start = 0
    for piece in pieces:
        sides[start : start + piece.shape[0], :] = piece[...]
        start += piece.shape[0]
    learner_weights(slots, sides, weights)

    def add(index, rows, value):
        if index == 0:
            sum_01[rows, :] = value
        elif index == 1:
            sum_01[rows, :] += value
        else:
            sum_2[rows, :] = value

    side = jnp.concatenate([side_of(sides, mask) for mask in (0, 1, 2)], axis=1)
    backward(slots, logits[...], side, weights, mats[1], frames_t, hidden_t, scratch[2], add)


def second_kernel(slots, *refs):
    frames, (sides, weights, sum_01, sum_2), mats, (sum_0123, sum_4), scratch = (
        refs[0:2], refs[2:6], refs[6:9], refs[9:11], refs[11:14])

    def add(index, rows, value):
        if index == 0:
            sum_0123[rows, :] = sum_01[rows, :] + (sum_2[rows, :] + value)
        else:
            sum_4[rows, :] = value

    side = jnp.concatenate([side_of(sides, 3), side_of(sides, 4)], axis=1)
    work(slots, frames, side, weights, *mats, *scratch, add)


def third_kernel(slots, *refs):
    frames, (sides, weights, sum_4), mats, (sum_45, sum_6), scratch = (
        refs[0:2], refs[2:5], refs[5:8], refs[8:10], refs[10:13])

    def add(index, rows, value):
        if index == 0:
            sum_45[rows, :] = sum_4[rows, :] + value
        else:
            sum_6[rows, :] = value

    side = jnp.concatenate([side_of(sides, 5), side_of(sides, 6)], axis=1)
    work(slots, frames, side, weights, *mats, *scratch, add)


def fourth_kernel(slots, *refs):
    frames, (sides, weights, sum_0123, sum_45, sum_6), mats, out, scratch = (
        refs[0:1], refs[1:6], refs[6:9], refs[9], refs[10:13])

    def add(index, rows, value):
        out[rows, :] = (
            sum_0123[rows, :] + (sum_45[rows, :] + (sum_6[rows, :] + value))
        ).astype(BF16)

    work(slots, frames, side_of(sides, 7), weights, *mats, *scratch, add)


def local_kernel(slots, frames, side, weights, embed_t, head, head_t, out, *scratch):
    def add(index, rows, value):
        if index == 0:
            out[rows, :] = value
        else:
            out[rows, :] += value

    blocks = [frames.at[index] for index in range(frames.shape[0])]
    work(slots, blocks, side, weights, embed_t, head, head_t, *scratch, add)


def call(kernel, name, slots, blocks, args, mats, outs):
    width, feats = mats[0].shape
    rows = blocks * BLOCK
    return pl.pallas_call(
        functools.partial(kernel, slots),
        out_shape=outs,
        in_specs=[VMEM] * (len(args) + 3),
        out_specs=jax.tree.map(lambda leaf: VMEM, outs),
        scratch_shapes=[
            pltpu.VMEM((feats, rows), BF16),
            pltpu.VMEM((width, rows), BF16),
            pltpu.VMEM((width, rows), BF16),
        ],
        compiler_params=params(32),
        cost_estimate=cost(1.2 * blocks + 0.4),
        name=name,
    )(*args, *mats)


def update_kernel(
    feats, nact, mine, theirs, master_embed, master_policy, master_value,
    embed_moment, policy_moment, value_moment, next_obs,
    next_logits, new_embed, new_policy, new_value, new_em, new_pm, new_vm,
):
    def step(grad, moment, master, new_moment, new_master):
        held = MOMENTUM * moment[...] + grad
        new_moment[...] = held
        fresh = master[...] - LEARN_RATE * held
        new_master[...] = fresh
        return fresh

    def grad(start, size):
        return mine[start : start + size, :].astype(F32) + theirs[start : start + size, :].astype(F32)

    embed = step(grad(0, feats), embed_moment, master_embed, new_em, new_embed)
    hidden = jnp.maximum(mm(next_obs[...], embed.astype(BF16)), 0.0).astype(BF16)
    policy = step(grad(feats, nact).T, policy_moment, master_policy, new_pm, new_policy)
    step(grad(feats + nact, PAD)[0:1, :], value_moment, master_value, new_vm, new_value)
    next_logits[...] = mm(hidden, policy.astype(BF16)).astype(BF16)


def update(mine, theirs, *args):
    embed, policy, value = args[0], args[1], args[2]
    next_obs = args[6]
    feats, nact = embed.shape[0], policy.shape[1]
    shapes = [jax.ShapeDtypeStruct(array.shape, F32) for array in (embed, policy, value)]
    return pl.pallas_call(
        functools.partial(update_kernel, feats, nact),
        out_shape=(jax.ShapeDtypeStruct((next_obs.shape[0], nact), BF16), *shapes, *shapes),
        in_specs=[VMEM] * 9,
        out_specs=(VMEM,) * 7,
        compiler_params=params(32),
        cost_estimate=cost(3.4),
        name="update",
    )(mine, theirs, *args)


def gathered_grads(slots, own, side, mats):
    def exchange(array, mask, name):
        with jax.named_scope(name):
            return lax.ppermute(array, "hst", [(at, at ^ mask) for at in range(8)])

    def middle(array, name):
        with jax.named_scope(name):
            pairs = [(at, at ^ 6 if at in (2, 3, 4, 5) else at) for at in range(8)]
            return lax.ppermute(array, "hst", pairs)

    b2 = exchange(own, 2, "b2")
    over = middle(own, "over")
    b1 = exchange(own, 1, "b1")
    pair = jnp.concatenate([side, exchange(side, 1, "side_y")], axis=0)
    pair, _, _ = lax.optimization_barrier((pair, b2, b1))
    pieces = [pair, exchange(pair, 2, "side_z")]
    four = jnp.concatenate(pieces, axis=0)
    pieces.append(exchange(four, 4, "side_zz"))
    b3 = exchange(b2, 1, "b3")
    end_4 = exchange(over, 2, "end_4")
    mid_6 = middle(b2, "mid_6")
    width, feats = mats[0].shape
    grads = jax.ShapeDtypeStruct((feats + mats[2].shape[0], width), F32)
    weights = jax.ShapeDtypeStruct((16, 128), F32)
    sides = jax.ShapeDtypeStruct((64, side.shape[1]), F32)
    done = ahead((own, b1, b2), mats[0], mats[2])
    end_6 = exchange(mid_6, 2, "end_6")
    b4 = jnp.where(on_mid(), over, end_4)
    b5 = exchange(b4, 1, "b5")
    done, b3, b4 = lax.optimization_barrier((done, b3, b4))
    sum_01, sum_2, weights, sides = call(
        first_kernel, "first", slots, 3, (*done, *pieces), mats, (grads, grads, weights, sides),
    )
    sum_0123, sum_4 = call(
        second_kernel, "second", slots, 2, (b3, b4, sides, weights, sum_01, sum_2), mats,
        (grads, grads),
    )
    b6 = jnp.where(on_mid(), mid_6, end_6)
    b7 = exchange(b6, 1, "b7")
    sum_45, sum_6 = call(
        third_kernel, "third", slots, 2, (b5, b6, sides, weights, sum_4), mats, (grads, grads),
    )
    return call(
        fourth_kernel, "fourth", slots, 1, (b7, sides, weights, sum_0123, sum_45, sum_6), mats,
        jax.ShapeDtypeStruct(grads.shape, BF16),
    )


def body(
    n_hst, n_cores, observations, lengths, actions, rewards, assign, actor_embed, actor_policy,
    master_embed, master_policy, master_value, embed_moment, policy_moment, value_moment, next_obs,
):
    traj, slots, feats = observations.shape
    learners = n_hst * n_cores
    rows = traj * slots
    own = observations.reshape(rows, feats)
    value_row = master_value.reshape(1, -1)
    spread, owner = select(traj, slots)
    flip = [(core, core ^ 1) for core in range(n_cores)]
    there = [lax.ppermute(array, "cores", flip) for array in (lengths, assign)]
    gather = n_hst == 8 and n_cores == 2 and rows == BLOCK
    side = side_data(
        spread, owner, own, *[array.reshape(1, -1) for array in (lengths, assign, *there)],
        actions, rewards, actor_embed, actor_policy,
    )
    late_row, _ = lax.optimization_barrier((value_row, side))
    mats = convert(master_embed, master_policy, late_row)
    if gather:
        mine = gathered_grads(slots, own, side, mats)
        theirs = lax.ppermute(mine, "cores", flip)
    else:
        named = (assign[:, None] == jnp.arange(learners)[None, :]).astype(F32)
        totals = lax.psum(jnp.sum(named * lengths[:, None].astype(F32), axis=0), AXES)
        weights = jnp.broadcast_to((1.0 / (learners * totals))[:, None], (learners, 128))
        grads = call(
            local_kernel, "local", slots, rows // BLOCK,
            (own.reshape(-1, BLOCK, feats), side, weights), mats,
            jax.ShapeDtypeStruct((feats + mats[2].shape[0], mats[0].shape[0]), F32),
        )
        mine = lax.psum(grads, AXES)
        theirs = jnp.zeros_like(mine)
    outs = update(
        mine, theirs, master_embed, master_policy, value_row, embed_moment, policy_moment,
        value_moment.reshape(1, -1), next_obs,
    )
    logits, new_embed, new_policy, new_value, new_em, new_pm, new_vm = outs
    return logits, new_embed, new_policy, new_value.reshape(-1), new_em, new_pm, new_vm.reshape(-1)


def solution(mesh):
    split = P(("group", "hst", "cores"))
    whole = P("group")
    return jax.shard_map(
        functools.partial(body, mesh.shape["hst"], mesh.shape["cores"]),
        mesh=mesh,
        in_specs=(split,) * 5 + (whole,) * 8 + (split,),
        out_specs=(split,) + (whole,) * 6,
        check_vma=False,
    )
```

```python
import functools

import jax
import jax.numpy as jnp
from jax import lax
from jax.experimental import pallas as pl
from jax.experimental.pallas import tpu as pltpu
from jax.sharding import PartitionSpec as P

GAMMA = 0.99
ENTROPY_COEF = 0.1
MOMENTUM = 0.9
LEARN_RATE = 0.05
AXES = ("hst", "cores")
F32 = jnp.float32
BF16 = jnp.bfloat16
VMEM = pl.BlockSpec(memory_space=pltpu.VMEM)
MIB = 2**20
BLOCK = 256
PAD = 16
BEHAVE, ACTION, REWARD, LENGTH, ASSIGN, LENGTH_2, ASSIGN_2 = range(7)


def iota(shape, dim):
    return lax.broadcasted_iota(jnp.int32, shape, dim)


def mm(a, b):
    return jnp.dot(a, b, preferred_element_type=F32)


def mm_nt(a, b):
    return lax.dot_general(a, b, (((1,), (1,)), ((), ())), preferred_element_type=F32)


def params(mib):
    return pltpu.CompilerParams(vmem_limit_bytes=mib * MIB)


def cost(micros):
    return pl.CostEstimate(flops=int(micros * 1.1e9), bytes_accessed=0, transcendentals=0)


def select_kernel(spread, owner):
    traj, rows = owner.shape
    slots = spread.shape[0]
    spread[...] = (lax.rem(iota((slots, rows), 1), slots) == iota((slots, rows), 0)).astype(F32)
    owner[...] = (lax.div(iota((traj, rows), 1), slots) == iota((traj, rows), 0)).astype(F32)


def select(traj, slots):
    rows = traj * slots
    return pl.pallas_call(
        select_kernel,
        out_shape=(jax.ShapeDtypeStruct((slots, rows), F32), jax.ShapeDtypeStruct((traj, rows), F32)),
        out_specs=(VMEM, VMEM),
        compiler_params=params(4),
        cost_estimate=cost(40),
        name="select",
    )()


def side_kernel(
    lengths, assign, lengths_2, assign_2, actions, rewards, actor_embed, actor_policy,
    spread, owner, obs, side,
):

    def flat(series):
        wide = jnp.dot(
            series, spread[...], precision=lax.Precision.HIGHEST, preferred_element_type=F32
        )
        return jnp.sum(wide * owner[...], axis=0, keepdims=True)

    def repeat(series):
        return jnp.dot(
            series.astype(F32), owner[...],
            precision=lax.Precision.HIGHEST, preferred_element_type=F32,
        )

    action = flat(actions[...].astype(F32))
    hidden = jnp.maximum(mm(obs[...], actor_embed[...]), 0.0).astype(BF16)
    logits = mm(hidden, actor_policy[...]).T
    top = jnp.max(logits, axis=0, keepdims=True)
    shifted = logits - top
    norm = jnp.log(jnp.sum(jnp.exp(shifted), axis=0, keepdims=True))
    onehot = iota(logits.shape, 0) == action.astype(jnp.int32)
    side[...] = jnp.zeros_like(side)
    side[BEHAVE : BEHAVE + 1, :] = (
        jnp.sum(jnp.where(onehot, shifted, 0.0), axis=0, keepdims=True) - norm
    )
    side[ACTION : ACTION + 1, :] = action
    side[REWARD : REWARD + 1, :] = flat(rewards[...])
    side[LENGTH : LENGTH + 1, :] = repeat(lengths[...])
    side[ASSIGN : ASSIGN + 1, :] = repeat(assign[...])
    side[LENGTH_2 : LENGTH_2 + 1, :] = repeat(lengths_2[...])
    side[ASSIGN_2 : ASSIGN_2 + 1, :] = repeat(assign_2[...])


def side_data(spread, owner, obs, *args):
    count = len(args) + 3
    return pl.pallas_call(
        side_kernel,
        out_shape=jax.ShapeDtypeStruct((8, spread.shape[1]), F32),
        in_specs=[VMEM] * count,
        out_specs=VMEM,
        compiler_params=params(12),
        cost_estimate=cost(1.3),
        name="side",
    )(*args, spread, owner, obs)


def convert_kernel(master_embed, master_policy, master_value, embed_t, head, head_t):
    embed_t[...] = master_embed[...].T.astype(BF16)
    nact = master_policy.shape[1]
    wide = jnp.concatenate(
        [
            master_policy[...].T,
            master_value[...],
            jnp.zeros((PAD - 1, head_t.shape[1]), F32),
        ],
        axis=0,
    )
    head_t[...] = wide.astype(BF16)
    head[:, 0:nact] = master_policy[...].astype(BF16)
    head[:, nact:] = wide[nact:, :].T.astype(BF16)


def convert(master_embed, master_policy, master_value):
    feats, width = master_embed.shape
    nact = master_policy.shape[1]
    return pl.pallas_call(
        convert_kernel,
        out_shape=(
            jax.ShapeDtypeStruct((width, feats), BF16),
            jax.ShapeDtypeStruct((width, nact + PAD), BF16),
            jax.ShapeDtypeStruct((nact + PAD, width), BF16),
        ),
        in_specs=[VMEM] * 3,
        out_specs=(VMEM,) * 3,
        compiler_params=params(12),
        cost_estimate=cost(0.6),
        name="convert",
    )(master_embed, master_policy, master_value)


def learner_weights(slots, sides, out):
    learners, rows = out.shape[0], sides.shape[1]
    total = jnp.zeros((learners, rows), F32)
    first = lax.rem(iota((1, rows), 1), slots) == 0
    for place in range(0, sides.shape[0], 8):
        for length_at, assign_at in ((LENGTH, ASSIGN), (LENGTH_2, ASSIGN_2)):
            assign = sides[place + assign_at : place + assign_at + 1, :].astype(jnp.int32)
            length = jnp.where(first, sides[place + length_at : place + length_at + 1, :], 0.0)
            total = total + jnp.where(iota((learners, rows), 0) == assign, length, 0.0)
    summed = jnp.sum(total, axis=1, keepdims=True)
    out[...] = jnp.broadcast_to(1.0 / (learners * summed), out.shape)


def vtrace(slots, nact, side, weights, logits, values):
    rows = logits.shape[1]
    learners = weights.shape[0]
    behave = side[BEHAVE : BEHAVE + 1, :]
    reward = side[REWARD : REWARD + 1, :]
    length = side[LENGTH : LENGTH + 1, :].astype(jnp.int32)
    assign = side[ASSIGN : ASSIGN + 1, :].astype(jnp.int32)
    action = side[ACTION : ACTION + 1, :].astype(jnp.int32)
    weight = jnp.sum(
        jnp.where(iota((learners, rows), 0) == assign, weights[:, 0:1], 0.0), axis=0, keepdims=True
    )
    top = jnp.max(logits, axis=0, keepdims=True)
    exps = jnp.exp(logits - top)
    norm = jnp.sum(exps, axis=0, keepdims=True)
    logprob = logits - (top + jnp.log(norm))
    probs = exps * (1.0 / norm)
    onehot = iota(logits.shape, 0) == action
    taken = jnp.sum(jnp.where(onehot, logprob, 0.0), axis=0, keepdims=True)
    entropy = -jnp.sum(probs * logprob, axis=0, keepdims=True)
    step = lax.rem(iota((1, rows), 1), slots)
    inside = (step < length).astype(F32)
    beyond = (step + 1 < length).astype(F32)
    ratios = jnp.minimum(1.0, jnp.exp(taken - behave))

    def later(series, by):
        return pltpu.roll(series, rows - by, 1)

    deltas = inside * ratios * (reward + GAMMA * later(values, 1) * beyond - values)
    decay = GAMMA * ratios * inside
    corrections = deltas
    reach = 1
    while reach < slots:
        within = step + reach < slots
        corrections = corrections + decay * jnp.where(within, later(corrections, reach), 0.0)
        decay = decay * jnp.where(within, later(decay, reach), 0.0)
        reach *= 2
    targets = values + corrections
    advantage = ratios * (reward + GAMMA * later(targets, 1) * beyond - values)
    scale = weight * inside
    grad = scale * (
        -advantage * (onehot.astype(F32) - probs) + ENTROPY_COEF * probs * (logprob + entropy)
    )
    return grad, scale * (values - targets)


def forward(frames, embed_t, head_t, frames_t, hidden_t):
    width = embed_t.shape[0]
    tile = 256
    for index, block in enumerate(frames):
        frames_t[:, index * BLOCK : (index + 1) * BLOCK] = block[...].T
    for start in range(0, width, tile):
        here = slice(start, start + tile)
        hidden_t[here, :] = jnp.maximum(mm(embed_t[here, :], frames_t[...]), 0.0).astype(BF16)
    return mm(head_t[...], hidden_t[...])


def backward(slots, logits, side, weights, head, frames_t, hidden_t, preact_t, add):
    width, feats = head.shape[0], frames_t.shape[0]
    nact = logits.shape[0] - PAD
    tile = 256
    grad, grad_values = vtrace(
        slots, nact, side, weights, logits[0:nact, :], logits[nact : nact + 1, :]
    )
    pad = jnp.zeros((PAD - 1, grad.shape[1]), F32)
    grad_t = jnp.concatenate([grad, grad_values, pad], axis=0).astype(BF16)
    for start in range(0, width, tile):
        here = slice(start, start + tile)
        back = mm(head[here, :], grad_t)
        alive = hidden_t[here, :].astype(F32) > 0.0
        preact_t[here, :] = jnp.where(alive, back, 0.0).astype(BF16)
    for index in range(frames_t.shape[1] // BLOCK):
        lanes = slice(index * BLOCK, (index + 1) * BLOCK)
        add(index, slice(0, feats), mm_nt(frames_t[:, lanes], preact_t[:, lanes]))
        add(index, slice(feats, feats + nact + PAD), mm_nt(grad_t[:, lanes], hidden_t[:, lanes]))


def work(slots, frames, side, weights, embed_t, head, head_t, frames_t, hidden_t, preact_t, add):
    logits = forward(frames, embed_t, head_t, frames_t, hidden_t)
    backward(slots, logits, side, weights, head, frames_t, hidden_t, preact_t, add)


def side_of(sides, back, flip):
    line = lax.div(lax.axis_index("hst"), 2)
    there = lax.bitwise_xor(line, lax.bitwise_and(line + 4 - back, 3))
    return sides[pl.ds(pl.multiple_of(8 * (4 * flip + there), 8), 8), :]


def ahead_kernel(*refs):
    (*frames, embed_t, head_t, frames_t, hidden_t, logits) = refs
    logits[...] = forward(frames, embed_t, head_t, frames_t, hidden_t)


def ahead(frames, embed_t, head_t):
    width, feats = embed_t.shape
    rows = len(frames) * BLOCK
    return pl.pallas_call(
        ahead_kernel,
        out_shape=(
            jax.ShapeDtypeStruct((feats, rows), BF16),
            jax.ShapeDtypeStruct((width, rows), BF16),
            jax.ShapeDtypeStruct((head_t.shape[0], rows), F32),
        ),
        in_specs=[VMEM] * (len(frames) + 2),
        out_specs=(VMEM,) * 3,
        compiler_params=params(20),
        cost_estimate=cost(1.6),
        name="ahead",
    )(*frames, embed_t, head_t)


def first_kernel(slots, *refs):
    (frames_t, hidden_t, logits, *pieces), mats, (sum_0, sum_1, weights, sides), scratch = (
        refs[0:5], refs[5:8], refs[8:12], refs[12:15])
    start = 0
    for piece in pieces:
        sides[start : start + piece.shape[0], :] = piece[...]
        start += piece.shape[0]
    learner_weights(slots, sides, weights)

    def add(index, rows, value):
        if index == 0:
            sum_0[rows, :] = value
        elif index == 1:
            sum_0[rows, :] += value
        else:
            sum_1[rows, :] = value

    side = jnp.concatenate([side_of(sides, *at) for at in ((0, 0), (0, 1), (1, 0))], axis=1)
    backward(slots, logits[...], side, weights, mats[1], frames_t, hidden_t, scratch[2], add)


def second_kernel(slots, *refs):
    frames, (sides, weights, sum_1), mats, (sum_1y, sum_3), scratch = (
        refs[0:2], refs[2:5], refs[5:8], refs[8:10], refs[10:13])

    def add(index, rows, value):
        if index == 0:
            sum_1y[rows, :] = sum_1[rows, :] + value
        else:
            sum_3[rows, :] = value

    side = jnp.concatenate([side_of(sides, 1, 1), side_of(sides, 3, 0)], axis=1)
    work(slots, frames, side, weights, *mats, *scratch, add)


def third_kernel(slots, *refs):
    frames, (sides, weights, sum_1y, sum_3), mats, (odd, sum_2), scratch = (
        refs[0:2], refs[2:6], refs[6:9], refs[9:11], refs[11:14])

    def add(index, rows, value):
        if index == 0:
            odd[rows, :] = sum_1y[rows, :] + (sum_3[rows, :] + value)
        else:
            sum_2[rows, :] = value

    side = jnp.concatenate([side_of(sides, 3, 1), side_of(sides, 2, 0)], axis=1)
    work(slots, frames, side, weights, *mats, *scratch, add)


def fourth_kernel(slots, *refs):
    frames, (sides, weights, odd, sum_0, sum_2), mats, out, scratch = (
        refs[0:1], refs[1:6], refs[6:9], refs[9], refs[10:13])

    def add(index, rows, value):
        out[rows, :] = (
            odd[rows, :] + (sum_0[rows, :] + (sum_2[rows, :] + value))
        ).astype(BF16)

    work(slots, frames, side_of(sides, 2, 1), weights, *mats, *scratch, add)


def local_kernel(slots, frames, side, weights, embed_t, head, head_t, out, *scratch):
    def add(index, rows, value):
        if index == 0:
            out[rows, :] = value
        else:
            out[rows, :] += value

    blocks = [frames.at[index] for index in range(frames.shape[0])]
    work(slots, blocks, side, weights, embed_t, head, head_t, *scratch, add)


def call(kernel, name, slots, blocks, args, mats, outs):
    width, feats = mats[0].shape
    rows = blocks * BLOCK
    return pl.pallas_call(
        functools.partial(kernel, slots),
        out_shape=outs,
        in_specs=[VMEM] * (len(args) + 3),
        out_specs=jax.tree.map(lambda leaf: VMEM, outs),
        scratch_shapes=[
            pltpu.VMEM((feats, rows), BF16),
            pltpu.VMEM((width, rows), BF16),
            pltpu.VMEM((width, rows), BF16),
        ],
        compiler_params=params(32),
        cost_estimate=cost(1.2 * blocks + 0.4),
        name=name,
    )(*args, *mats)


def update_kernel(
    feats, nact, mine, theirs, master_embed, master_policy, master_value,
    embed_moment, policy_moment, value_moment, next_obs,
    next_logits, new_embed, new_policy, new_value, new_em, new_pm, new_vm,
):
    def step(grad, moment, master, new_moment, new_master):
        held = MOMENTUM * moment[...] + grad
        new_moment[...] = held
        fresh = master[...] - LEARN_RATE * held
        new_master[...] = fresh
        return fresh

    def grad(start, size):
        return mine[start : start + size, :].astype(F32) + theirs[start : start + size, :].astype(F32)

    embed = step(grad(0, feats), embed_moment, master_embed, new_em, new_embed)
    hidden = jnp.maximum(mm(next_obs[...], embed.astype(BF16)), 0.0).astype(BF16)
    policy = step(grad(feats, nact).T, policy_moment, master_policy, new_pm, new_policy)
    step(grad(feats + nact, PAD)[0:1, :], value_moment, master_value, new_vm, new_value)
    next_logits[...] = mm(hidden, policy.astype(BF16)).astype(BF16)


def update(mine, theirs, *args):
    embed, policy, value = args[0], args[1], args[2]
    next_obs = args[6]
    feats, nact = embed.shape[0], policy.shape[1]
    shapes = [jax.ShapeDtypeStruct(array.shape, F32) for array in (embed, policy, value)]
    return pl.pallas_call(
        functools.partial(update_kernel, feats, nact),
        out_shape=(jax.ShapeDtypeStruct((next_obs.shape[0], nact), BF16), *shapes, *shapes),
        in_specs=[VMEM] * 9,
        out_specs=(VMEM,) * 7,
        compiler_params=params(32),
        cost_estimate=cost(3.4),
        name="update",
    )(mine, theirs, *args)


def gathered_grads(slots, own, side, mats):
    def exchange(array, mask, name):
        with jax.named_scope(name):
            return lax.ppermute(array, "hst", [(at, at ^ mask) for at in range(8)])

    def shift(array, by, name):
        with jax.named_scope(name):
            return lax.ppermute(array, "hst", [(at, (at + 2 * by) % 8) for at in range(8)])

    one = shift(own, 1, "one")
    own_y = exchange(own, 1, "own_y")
    pieces = [side] + [exchange(side, 2 * mask, "side_z") for mask in (1, 2, 3)]
    line = jnp.concatenate(pieces, axis=0)
    line, _ = lax.optimization_barrier((line, side))
    one, _ = lax.optimization_barrier((one, pieces[1]))
    again, _ = lax.optimization_barrier((own, pieces[1]))
    line_y = exchange(line, 1, "side_y")
    three = shift(again, -1, "three")
    one_y = exchange(one, 1, "one_y")
    two = shift(one, 1, "two")
    three_y = exchange(three, 1, "three_y")

    width, feats = mats[0].shape
    grads = jax.ShapeDtypeStruct((feats + mats[2].shape[0], width), F32)
    weights = jax.ShapeDtypeStruct((16, 128), F32)
    sides = jax.ShapeDtypeStruct((64, side.shape[1]), F32)
    done = ahead((own, own_y, one), mats[0], mats[2])
    sum_0, sum_1, weights, sides = call(
        first_kernel, "first", slots, 3, (*done, line, line_y), mats,
        (grads, grads, weights, sides),
    )
    sum_1y, sum_3 = call(
        second_kernel, "second", slots, 2, (one_y, three, sides, weights, sum_1), mats,
        (grads, grads),
    )
    two, sum_3 = lax.optimization_barrier((two, sum_3))
    two_y = exchange(two, 1, "two_y")
    odd, sum_2 = call(
        third_kernel, "third", slots, 2, (three_y, two, sides, weights, sum_1y, sum_3), mats,
        (grads, grads),
    )
    return call(
        fourth_kernel, "fourth", slots, 1, (two_y, sides, weights, odd, sum_0, sum_2), mats,
        jax.ShapeDtypeStruct(grads.shape, BF16),
    )


def body(
    n_hst, n_cores, observations, lengths, actions, rewards, assign, actor_embed, actor_policy,
    master_embed, master_policy, master_value, embed_moment, policy_moment, value_moment, next_obs,
):
    traj, slots, feats = observations.shape
    learners = n_hst * n_cores
    rows = traj * slots
    own = observations.reshape(rows, feats)
    value_row = master_value.reshape(1, -1)
    spread, owner = select(traj, slots)
    flip = [(core, core ^ 1) for core in range(n_cores)]
    there = [lax.ppermute(array, "cores", flip) for array in (lengths, assign)]
    gather = n_hst == 8 and n_cores == 2 and rows == BLOCK
    side = side_data(
        spread, owner, own, *[array.reshape(1, -1) for array in (lengths, assign, *there)],
        actions, rewards, actor_embed, actor_policy,
    )
    late_row, _ = lax.optimization_barrier((value_row, side))
    mats = convert(master_embed, master_policy, late_row)
    if gather:
        mine = gathered_grads(slots, own, side, mats)
        theirs = lax.ppermute(mine, "cores", flip)
    else:
        named = (assign[:, None] == jnp.arange(learners)[None, :]).astype(F32)
        totals = lax.psum(jnp.sum(named * lengths[:, None].astype(F32), axis=0), AXES)
        weights = jnp.broadcast_to((1.0 / (learners * totals))[:, None], (learners, 128))
        grads = call(
            local_kernel, "local", slots, rows // BLOCK,
            (own.reshape(-1, BLOCK, feats), side, weights), mats,
            jax.ShapeDtypeStruct((feats + mats[2].shape[0], mats[0].shape[0]), F32),
        )
        mine = lax.psum(grads, AXES)
        theirs = jnp.zeros_like(mine)
    outs = update(
        mine, theirs, master_embed, master_policy, value_row, embed_moment, policy_moment,
        value_moment.reshape(1, -1), next_obs,
    )
    logits, new_embed, new_policy, new_value, new_em, new_pm, new_vm = outs
    return logits, new_embed, new_policy, new_value.reshape(-1), new_em, new_pm, new_vm.reshape(-1)


def solution(mesh):
    split = P(("group", "hst", "cores"))
    whole = P("group")
    return jax.shard_map(
        functools.partial(body, mesh.shape["hst"], mesh.shape["cores"]),
        mesh=mesh,
        in_specs=(split,) * 5 + (whole,) * 8 + (split,),
        out_specs=(split,) + (whole,) * 6,
        check_vma=False,
    )
```

```python
import functools

import jax
import jax.numpy as jnp
from jax import lax
from jax.experimental import pallas as pl
from jax.experimental.pallas import tpu as pltpu
from jax.sharding import PartitionSpec as P

GAMMA = 0.99
ENTROPY_COEF = 0.1
MOMENTUM = 0.9
LEARN_RATE = 0.05
AXES = ("hst", "cores")
F32 = jnp.float32
BF16 = jnp.bfloat16
VMEM = pl.BlockSpec(memory_space=pltpu.VMEM)
MIB = 2**20
BLOCK = 256
PAD = 16
BEHAVE, ACTION, REWARD, LENGTH, ASSIGN, LENGTH_2, ASSIGN_2 = range(7)


def iota(shape, dim):
    return lax.broadcasted_iota(jnp.int32, shape, dim)


def mm(a, b):
    return jnp.dot(a, b, preferred_element_type=F32)


def mm_nt(a, b):
    return lax.dot_general(a, b, (((1,), (1,)), ((), ())), preferred_element_type=F32)


def params(mib):
    return pltpu.CompilerParams(vmem_limit_bytes=mib * MIB)


def cost(micros):
    return pl.CostEstimate(flops=int(micros * 1.1e9), bytes_accessed=0, transcendentals=0)


def select_kernel(spread, owner):
    traj, rows = owner.shape
    slots = spread.shape[0]
    spread[...] = (lax.rem(iota((slots, rows), 1), slots) == iota((slots, rows), 0)).astype(F32)
    owner[...] = (lax.div(iota((traj, rows), 1), slots) == iota((traj, rows), 0)).astype(F32)


def select(traj, slots):
    rows = traj * slots
    return pl.pallas_call(
        select_kernel,
        out_shape=(jax.ShapeDtypeStruct((slots, rows), F32), jax.ShapeDtypeStruct((traj, rows), F32)),
        out_specs=(VMEM, VMEM),
        compiler_params=params(4),
        cost_estimate=cost(40),
        name="select",
    )()


def side_kernel(
    lengths, assign, lengths_2, assign_2, actions, rewards, actor_embed, actor_policy,
    spread, owner, obs, side,
):

    def flat(series):
        wide = jnp.dot(
            series, spread[...], precision=lax.Precision.HIGHEST, preferred_element_type=F32
        )
        return jnp.sum(wide * owner[...], axis=0, keepdims=True)

    def repeat(series):
        return jnp.dot(
            series.astype(F32), owner[...],
            precision=lax.Precision.HIGHEST, preferred_element_type=F32,
        )

    action = flat(actions[...].astype(F32))
    hidden = jnp.maximum(mm(obs[...], actor_embed[...]), 0.0).astype(BF16)
    logits = mm(hidden, actor_policy[...]).T
    top = jnp.max(logits, axis=0, keepdims=True)
    shifted = logits - top
    norm = jnp.log(jnp.sum(jnp.exp(shifted), axis=0, keepdims=True))
    onehot = iota(logits.shape, 0) == action.astype(jnp.int32)
    side[...] = jnp.zeros_like(side)
    side[BEHAVE : BEHAVE + 1, :] = (
        jnp.sum(jnp.where(onehot, shifted, 0.0), axis=0, keepdims=True) - norm
    )
    side[ACTION : ACTION + 1, :] = action
    side[REWARD : REWARD + 1, :] = flat(rewards[...])
    side[LENGTH : LENGTH + 1, :] = repeat(lengths[...])
    side[ASSIGN : ASSIGN + 1, :] = repeat(assign[...])
    side[LENGTH_2 : LENGTH_2 + 1, :] = repeat(lengths_2[...])
    side[ASSIGN_2 : ASSIGN_2 + 1, :] = repeat(assign_2[...])


def side_data(spread, owner, obs, *args):
    count = len(args) + 3
    return pl.pallas_call(
        side_kernel,
        out_shape=jax.ShapeDtypeStruct((8, spread.shape[1]), F32),
        in_specs=[VMEM] * count,
        out_specs=VMEM,
        compiler_params=params(12),
        cost_estimate=cost(1.3),
        name="side",
    )(*args, spread, owner, obs)


def convert_kernel(master_embed, master_policy, master_value, embed_t, head, head_t):
    embed_t[...] = master_embed[...].T.astype(BF16)
    nact = master_policy.shape[1]
    wide = jnp.concatenate(
        [
            master_policy[...].T,
            master_value[...],
            jnp.zeros((PAD - 1, head_t.shape[1]), F32),
        ],
        axis=0,
    )
    head_t[...] = wide.astype(BF16)
    head[:, 0:nact] = master_policy[...].astype(BF16)
    head[:, nact:] = wide[nact:, :].T.astype(BF16)


def convert(master_embed, master_policy, master_value):
    feats, width = master_embed.shape
    nact = master_policy.shape[1]
    return pl.pallas_call(
        convert_kernel,
        out_shape=(
            jax.ShapeDtypeStruct((width, feats), BF16),
            jax.ShapeDtypeStruct((width, nact + PAD), BF16),
            jax.ShapeDtypeStruct((nact + PAD, width), BF16),
        ),
        in_specs=[VMEM] * 3,
        out_specs=(VMEM,) * 3,
        compiler_params=params(12),
        cost_estimate=cost(0.6),
        name="convert",
    )(master_embed, master_policy, master_value)


def learner_weights(slots, sides, out):
    learners, rows = out.shape[0], sides.shape[1]
    total = jnp.zeros((learners, rows), F32)
    first = lax.rem(iota((1, rows), 1), slots) == 0
    for place in range(0, sides.shape[0], 8):
        for length_at, assign_at in ((LENGTH, ASSIGN), (LENGTH_2, ASSIGN_2)):
            assign = sides[place + assign_at : place + assign_at + 1, :].astype(jnp.int32)
            length = jnp.where(first, sides[place + length_at : place + length_at + 1, :], 0.0)
            total = total + jnp.where(iota((learners, rows), 0) == assign, length, 0.0)
    summed = jnp.sum(total, axis=1, keepdims=True)
    out[...] = jnp.broadcast_to(1.0 / (learners * summed), out.shape)


def vtrace(slots, nact, side, weights, logits, values):
    rows = logits.shape[1]
    learners = weights.shape[0]
    behave = side[BEHAVE : BEHAVE + 1, :]
    reward = side[REWARD : REWARD + 1, :]
    length = side[LENGTH : LENGTH + 1, :].astype(jnp.int32)
    assign = side[ASSIGN : ASSIGN + 1, :].astype(jnp.int32)
    action = side[ACTION : ACTION + 1, :].astype(jnp.int32)
    weight = jnp.sum(
        jnp.where(iota((learners, rows), 0) == assign, weights[:, 0:1], 0.0), axis=0, keepdims=True
    )
    top = jnp.max(logits, axis=0, keepdims=True)
    exps = jnp.exp(logits - top)
    norm = jnp.sum(exps, axis=0, keepdims=True)
    logprob = logits - (top + jnp.log(norm))
    probs = exps * (1.0 / norm)
    onehot = iota(logits.shape, 0) == action
    taken = jnp.sum(jnp.where(onehot, logprob, 0.0), axis=0, keepdims=True)
    entropy = -jnp.sum(probs * logprob, axis=0, keepdims=True)
    step = lax.rem(iota((1, rows), 1), slots)
    inside = (step < length).astype(F32)
    beyond = (step + 1 < length).astype(F32)
    ratios = jnp.minimum(1.0, jnp.exp(taken - behave))

    def later(series, by):
        return pltpu.roll(series, rows - by, 1)

    deltas = inside * ratios * (reward + GAMMA * later(values, 1) * beyond - values)
    decay = GAMMA * ratios * inside
    corrections = deltas
    reach = 1
    while reach < slots:
        within = step + reach < slots
        corrections = corrections + decay * jnp.where(within, later(corrections, reach), 0.0)
        decay = decay * jnp.where(within, later(decay, reach), 0.0)
        reach *= 2
    targets = values + corrections
    advantage = ratios * (reward + GAMMA * later(targets, 1) * beyond - values)
    scale = weight * inside
    grad = scale * (
        -advantage * (onehot.astype(F32) - probs) + ENTROPY_COEF * probs * (logprob + entropy)
    )
    return grad, scale * (values - targets)


def forward(frames, embed_t, head_t, frames_t, hidden_t):
    width = embed_t.shape[0]
    tile = 256
    for index, block in enumerate(frames):
        frames_t[:, index * BLOCK : (index + 1) * BLOCK] = block[...].T
    for start in range(0, width, tile):
        here = slice(start, start + tile)
        hidden_t[here, :] = jnp.maximum(mm(embed_t[here, :], frames_t[...]), 0.0).astype(BF16)
    return mm(head_t[...], hidden_t[...])


def backward(slots, logits, side, weights, head, frames_t, hidden_t, preact_t, add):
    width, feats = head.shape[0], frames_t.shape[0]
    nact = logits.shape[0] - PAD
    tile = 256
    grad, grad_values = vtrace(
        slots, nact, side, weights, logits[0:nact, :], logits[nact : nact + 1, :]
    )
    pad = jnp.zeros((PAD - 1, grad.shape[1]), F32)
    grad_t = jnp.concatenate([grad, grad_values, pad], axis=0).astype(BF16)
    for start in range(0, width, tile):
        here = slice(start, start + tile)
        back = mm(head[here, :], grad_t)
        alive = hidden_t[here, :].astype(F32) > 0.0
        preact_t[here, :] = jnp.where(alive, back, 0.0).astype(BF16)
    for index in range(frames_t.shape[1] // BLOCK):
        lanes = slice(index * BLOCK, (index + 1) * BLOCK)
        add(index, slice(0, feats), mm_nt(frames_t[:, lanes], preact_t[:, lanes]))
        add(index, slice(feats, feats + nact + PAD), mm_nt(grad_t[:, lanes], hidden_t[:, lanes]))


def work(slots, frames, side, weights, embed_t, head, head_t, frames_t, hidden_t, preact_t, add):
    logits = forward(frames, embed_t, head_t, frames_t, hidden_t)
    backward(slots, logits, side, weights, head, frames_t, hidden_t, preact_t, add)


def side_of(sides, back, flip):
    line = lax.div(lax.axis_index("hst"), 2)
    there = lax.bitwise_xor(line, lax.bitwise_and(line + 4 - back, 3))
    return sides[pl.ds(pl.multiple_of(8 * (4 * flip + there), 8), 8), :]


def ahead_kernel(*refs):
    (*frames, embed_t, head_t, frames_t, hidden_t, logits) = refs
    logits[...] = forward(frames, embed_t, head_t, frames_t, hidden_t)


def ahead(frames, embed_t, head_t):
    width, feats = embed_t.shape
    rows = len(frames) * BLOCK
    return pl.pallas_call(
        ahead_kernel,
        out_shape=(
            jax.ShapeDtypeStruct((feats, rows), BF16),
            jax.ShapeDtypeStruct((width, rows), BF16),
            jax.ShapeDtypeStruct((head_t.shape[0], rows), F32),
        ),
        in_specs=[VMEM] * (len(frames) + 2),
        out_specs=(VMEM,) * 3,
        compiler_params=params(20),
        cost_estimate=cost(1.6),
        name="ahead",
    )(*frames, embed_t, head_t)


def first_kernel(slots, *refs):
    (frames_t, hidden_t, logits, *pieces), mats, (sum_0, sum_1, weights, sides), scratch = (
        refs[0:5], refs[5:8], refs[8:12], refs[12:15])
    start = 0
    for piece in pieces:
        sides[start : start + piece.shape[0], :] = piece[...]
        start += piece.shape[0]
    learner_weights(slots, sides, weights)

    def add(index, rows, value):
        if index == 0:
            sum_0[rows, :] = value
        elif index == 1:
            sum_0[rows, :] += value
        else:
            sum_1[rows, :] = value

    side = jnp.concatenate([side_of(sides, *at) for at in ((0, 0), (0, 1), (1, 0))], axis=1)
    backward(slots, logits[...], side, weights, mats[1], frames_t, hidden_t, scratch[2], add)


def second_kernel(slots, *refs):
    frames, (sides, weights, sum_1), mats, (sum_1y, sum_3), scratch = (
        refs[0:2], refs[2:5], refs[5:8], refs[8:10], refs[10:13])

    def add(index, rows, value):
        if index == 0:
            sum_1y[rows, :] = sum_1[rows, :] + value
        else:
            sum_3[rows, :] = value

    side = jnp.concatenate([side_of(sides, 1, 1), side_of(sides, 3, 0)], axis=1)
    work(slots, frames, side, weights, *mats, *scratch, add)


def third_kernel(slots, *refs):
    frames, (sides, weights, sum_1y, sum_3), mats, (odd, sum_2), scratch = (
        refs[0:2], refs[2:6], refs[6:9], refs[9:11], refs[11:14])

    def add(index, rows, value):
        if index == 0:
            odd[rows, :] = sum_1y[rows, :] + (sum_3[rows, :] + value)
        else:
            sum_2[rows, :] = value

    side = jnp.concatenate([side_of(sides, 3, 1), side_of(sides, 2, 0)], axis=1)
    work(slots, frames, side, weights, *mats, *scratch, add)


def fourth_kernel(slots, *refs):
    frames, (sides, weights, odd, sum_0, sum_2), mats, out, scratch = (
        refs[0:1], refs[1:6], refs[6:9], refs[9], refs[10:13])

    def add(index, rows, value):
        out[rows, :] = (
            odd[rows, :] + (sum_0[rows, :] + (sum_2[rows, :] + value))
        ).astype(BF16)

    work(slots, frames, side_of(sides, 2, 1), weights, *mats, *scratch, add)


def local_kernel(slots, frames, side, weights, embed_t, head, head_t, out, *scratch):
    def add(index, rows, value):
        if index == 0:
            out[rows, :] = value
        else:
            out[rows, :] += value

    blocks = [frames.at[index] for index in range(frames.shape[0])]
    work(slots, blocks, side, weights, embed_t, head, head_t, *scratch, add)


def call(kernel, name, slots, blocks, args, mats, outs):
    width, feats = mats[0].shape
    rows = blocks * BLOCK
    return pl.pallas_call(
        functools.partial(kernel, slots),
        out_shape=outs,
        in_specs=[VMEM] * (len(args) + 3),
        out_specs=jax.tree.map(lambda leaf: VMEM, outs),
        scratch_shapes=[
            pltpu.VMEM((feats, rows), BF16),
            pltpu.VMEM((width, rows), BF16),
            pltpu.VMEM((width, rows), BF16),
        ],
        compiler_params=params(32),
        cost_estimate=cost(0.3 * blocks),
        name=name,
    )(*args, *mats)


def update_kernel(
    feats, nact, mine, theirs, master_embed, master_policy, master_value,
    embed_moment, policy_moment, value_moment, next_obs,
    next_logits, new_embed, new_policy, new_value, new_em, new_pm, new_vm,
):
    def step(grad, moment, master, new_moment, new_master):
        held = MOMENTUM * moment[...] + grad
        new_moment[...] = held
        fresh = master[...] - LEARN_RATE * held
        new_master[...] = fresh
        return fresh

    def grad(start, size):
        return mine[start : start + size, :].astype(F32) + theirs[start : start + size, :].astype(F32)

    embed = step(grad(0, feats), embed_moment, master_embed, new_em, new_embed)
    hidden = jnp.maximum(mm(next_obs[...], embed.astype(BF16)), 0.0).astype(BF16)
    policy = step(grad(feats, nact).T, policy_moment, master_policy, new_pm, new_policy)
    step(grad(feats + nact, PAD)[0:1, :], value_moment, master_value, new_vm, new_value)
    next_logits[...] = mm(hidden, policy.astype(BF16)).astype(BF16)


def update(mine, theirs, *args):
    embed, policy, value = args[0], args[1], args[2]
    next_obs = args[6]
    feats, nact = embed.shape[0], policy.shape[1]
    shapes = [jax.ShapeDtypeStruct(array.shape, F32) for array in (embed, policy, value)]
    return pl.pallas_call(
        functools.partial(update_kernel, feats, nact),
        out_shape=(jax.ShapeDtypeStruct((next_obs.shape[0], nact), BF16), *shapes, *shapes),
        in_specs=[VMEM] * 9,
        out_specs=(VMEM,) * 7,
        compiler_params=params(32),
        cost_estimate=cost(3.4),
        name="update",
    )(mine, theirs, *args)


def gathered_grads(slots, own, side, mats):
    def exchange(array, mask, name):
        with jax.named_scope(name):
            return lax.ppermute(array, "hst", [(at, at ^ mask) for at in range(8)])

    def shift(array, by, name):
        with jax.named_scope(name):
            return lax.ppermute(array, "hst", [(at, (at + 2 * by) % 8) for at in range(8)])

    one = shift(own, 1, "one")
    own_y = exchange(own, 1, "own_y")
    pieces = [side] + [exchange(side, 2 * mask, "side_z") for mask in (1, 2, 3)]
    line = jnp.concatenate(pieces, axis=0)
    line, _ = lax.optimization_barrier((line, side))
    again, _ = lax.optimization_barrier((own, one))
    line_y = exchange(line, 1, "side_y")
    three = shift(again, -1, "three")
    one_y = exchange(one, 1, "one_y")
    two = shift(one, 1, "two")
    three_y = exchange(three, 1, "three_y")

    width, feats = mats[0].shape
    grads = jax.ShapeDtypeStruct((feats + mats[2].shape[0], width), F32)
    weights = jax.ShapeDtypeStruct((16, 128), F32)
    sides = jax.ShapeDtypeStruct((64, side.shape[1]), F32)
    done = ahead((own, own_y, one), mats[0], mats[2])
    sum_0, sum_1, weights, sides = call(
        first_kernel, "first", slots, 3, (*done, line, line_y), mats,
        (grads, grads, weights, sides),
    )
    sum_1y, sum_3 = call(
        second_kernel, "second", slots, 2, (one_y, three, sides, weights, sum_1), mats,
        (grads, grads),
    )
    two, sum_3 = lax.optimization_barrier((two, sum_3))
    two_y = exchange(two, 1, "two_y")
    odd, sum_2 = call(
        third_kernel, "third", slots, 2, (three_y, two, sides, weights, sum_1y, sum_3), mats,
        (grads, grads),
    )
    return call(
        fourth_kernel, "fourth", slots, 1, (two_y, sides, weights, odd, sum_0, sum_2), mats,
        jax.ShapeDtypeStruct(grads.shape, BF16),
    )


def body(
    n_hst, n_cores, observations, lengths, actions, rewards, assign, actor_embed, actor_policy,
    master_embed, master_policy, master_value, embed_moment, policy_moment, value_moment, next_obs,
):
    traj, slots, feats = observations.shape
    learners = n_hst * n_cores
    rows = traj * slots
    own = observations.reshape(rows, feats)
    value_row = master_value.reshape(1, -1)
    spread, owner = select(traj, slots)
    flip = [(core, core ^ 1) for core in range(n_cores)]
    there = [lax.ppermute(array, "cores", flip) for array in (lengths, assign)]
    gather = n_hst == 8 and n_cores == 2 and rows == BLOCK
    side = side_data(
        spread, owner, own, *[array.reshape(1, -1) for array in (lengths, assign, *there)],
        actions, rewards, actor_embed, actor_policy,
    )
    late_row, _ = lax.optimization_barrier((value_row, side))
    mats = convert(master_embed, master_policy, late_row)
    if gather:
        mine = gathered_grads(slots, own, side, mats)
        theirs = lax.ppermute(mine, "cores", flip)
    else:
        named = (assign[:, None] == jnp.arange(learners)[None, :]).astype(F32)
        totals = lax.psum(jnp.sum(named * lengths[:, None].astype(F32), axis=0), AXES)
        weights = jnp.broadcast_to((1.0 / (learners * totals))[:, None], (learners, 128))
        grads = call(
            local_kernel, "local", slots, rows // BLOCK,
            (own.reshape(-1, BLOCK, feats), side, weights), mats,
            jax.ShapeDtypeStruct((feats + mats[2].shape[0], mats[0].shape[0]), F32),
        )
        mine = lax.psum(grads, AXES)
        theirs = jnp.zeros_like(mine)
    outs = update(
        mine, theirs, master_embed, master_policy, value_row, embed_moment, policy_moment,
        value_moment.reshape(1, -1), next_obs,
    )
    logits, new_embed, new_policy, new_value, new_em, new_pm, new_vm = outs
    return logits, new_embed, new_policy, new_value.reshape(-1), new_em, new_pm, new_vm.reshape(-1)


def solution(mesh):
    split = P(("group", "hst", "cores"))
    whole = P("group")
    return jax.shard_map(
        functools.partial(body, mesh.shape["hst"], mesh.shape["cores"]),
        mesh=mesh,
        in_specs=(split,) * 5 + (whole,) * 8 + (split,),
        out_specs=(split,) + (whole,) * 6,
        check_vma=False,
    )
```

```python
import functools

import jax
import jax.numpy as jnp
from jax import lax
from jax.experimental import pallas as pl
from jax.experimental.pallas import tpu as pltpu
from jax.sharding import PartitionSpec as P

GAMMA = 0.99
ENTROPY_COEF = 0.1
MOMENTUM = 0.9
LEARN_RATE = 0.05
AXES = ("hst", "cores")
F32 = jnp.float32
BF16 = jnp.bfloat16
VMEM = pl.BlockSpec(memory_space=pltpu.VMEM)
MIB = 2**20
BLOCK = 256
PAD = 16
BEHAVE, ACTION, REWARD, LENGTH, ASSIGN, LENGTH_2, ASSIGN_2 = range(7)


def iota(shape, dim):
    return lax.broadcasted_iota(jnp.int32, shape, dim)


def mm(a, b):
    return jnp.dot(a, b, preferred_element_type=F32)


def mm_nt(a, b):
    return lax.dot_general(a, b, (((1,), (1,)), ((), ())), preferred_element_type=F32)


def params(mib):
    return pltpu.CompilerParams(vmem_limit_bytes=mib * MIB)


def cost(micros):
    return pl.CostEstimate(flops=int(micros * 1.1e9), bytes_accessed=0, transcendentals=0)


def select_kernel(spread, owner):
    traj, rows = owner.shape
    slots = spread.shape[0]
    spread[...] = (lax.rem(iota((slots, rows), 1), slots) == iota((slots, rows), 0)).astype(F32)
    owner[...] = (lax.div(iota((traj, rows), 1), slots) == iota((traj, rows), 0)).astype(F32)


def select(traj, slots):
    rows = traj * slots
    return pl.pallas_call(
        select_kernel,
        out_shape=(jax.ShapeDtypeStruct((slots, rows), F32), jax.ShapeDtypeStruct((traj, rows), F32)),
        out_specs=(VMEM, VMEM),
        compiler_params=params(4),
        cost_estimate=cost(40),
        name="select",
    )()


def side_kernel(
    lengths, assign, lengths_2, assign_2, actions, rewards, actor_embed, actor_policy,
    spread, owner, obs, side,
):

    def flat(series):
        wide = jnp.dot(
            series, spread[...], precision=lax.Precision.HIGHEST, preferred_element_type=F32
        )
        return jnp.sum(wide * owner[...], axis=0, keepdims=True)

    def repeat(series):
        return jnp.dot(
            series.astype(F32), owner[...],
            precision=lax.Precision.HIGHEST, preferred_element_type=F32,
        )

    action = flat(actions[...].astype(F32))
    hidden = jnp.maximum(mm(obs[...], actor_embed[...]), 0.0).astype(BF16)
    logits = mm(hidden, actor_policy[...]).T
    top = jnp.max(logits, axis=0, keepdims=True)
    shifted = logits - top
    norm = jnp.log(jnp.sum(jnp.exp(shifted), axis=0, keepdims=True))
    onehot = iota(logits.shape, 0) == action.astype(jnp.int32)
    side[...] = jnp.zeros_like(side)
    side[BEHAVE : BEHAVE + 1, :] = (
        jnp.sum(jnp.where(onehot, shifted, 0.0), axis=0, keepdims=True) - norm
    )
    side[ACTION : ACTION + 1, :] = action
    side[REWARD : REWARD + 1, :] = flat(rewards[...])
    side[LENGTH : LENGTH + 1, :] = repeat(lengths[...])
    side[ASSIGN : ASSIGN + 1, :] = repeat(assign[...])
    side[LENGTH_2 : LENGTH_2 + 1, :] = repeat(lengths_2[...])
    side[ASSIGN_2 : ASSIGN_2 + 1, :] = repeat(assign_2[...])


def side_data(spread, owner, obs, *args):
    count = len(args) + 3
    return pl.pallas_call(
        side_kernel,
        out_shape=jax.ShapeDtypeStruct((8, spread.shape[1]), F32),
        in_specs=[VMEM] * count,
        out_specs=VMEM,
        compiler_params=params(12),
        cost_estimate=cost(1.3),
        name="side",
    )(*args, spread, owner, obs)


def convert_kernel(master_embed, master_policy, master_value, embed_t, head, head_t):
    embed_t[...] = master_embed[...].T.astype(BF16)
    nact = master_policy.shape[1]
    wide = jnp.concatenate(
        [
            master_policy[...].T,
            master_value[...],
            jnp.zeros((PAD - 1, head_t.shape[1]), F32),
        ],
        axis=0,
    )
    head_t[...] = wide.astype(BF16)
    head[:, 0:nact] = master_policy[...].astype(BF16)
    head[:, nact:] = wide[nact:, :].T.astype(BF16)


def convert(master_embed, master_policy, master_value):
    feats, width = master_embed.shape
    nact = master_policy.shape[1]
    return pl.pallas_call(
        convert_kernel,
        out_shape=(
            jax.ShapeDtypeStruct((width, feats), BF16),
            jax.ShapeDtypeStruct((width, nact + PAD), BF16),
            jax.ShapeDtypeStruct((nact + PAD, width), BF16),
        ),
        in_specs=[VMEM] * 3,
        out_specs=(VMEM,) * 3,
        compiler_params=params(12),
        cost_estimate=cost(0.6),
        name="convert",
    )(master_embed, master_policy, master_value)


def learner_weights(slots, sides, out):
    learners, rows = out.shape[0], sides.shape[1]
    total = jnp.zeros((learners, rows), F32)
    first = lax.rem(iota((1, rows), 1), slots) == 0
    for place in range(0, sides.shape[0], 8):
        for length_at, assign_at in ((LENGTH, ASSIGN), (LENGTH_2, ASSIGN_2)):
            assign = sides[place + assign_at : place + assign_at + 1, :].astype(jnp.int32)
            length = jnp.where(first, sides[place + length_at : place + length_at + 1, :], 0.0)
            total = total + jnp.where(iota((learners, rows), 0) == assign, length, 0.0)
    summed = jnp.sum(total, axis=1, keepdims=True)
    out[...] = jnp.broadcast_to(1.0 / (learners * summed), out.shape)


def vtrace(slots, nact, side, weights, logits, values):
    rows = logits.shape[1]
    learners = weights.shape[0]
    behave = side[BEHAVE : BEHAVE + 1, :]
    reward = side[REWARD : REWARD + 1, :]
    length = side[LENGTH : LENGTH + 1, :].astype(jnp.int32)
    assign = side[ASSIGN : ASSIGN + 1, :].astype(jnp.int32)
    action = side[ACTION : ACTION + 1, :].astype(jnp.int32)
    weight = jnp.sum(
        jnp.where(iota((learners, rows), 0) == assign, weights[:, 0:1], 0.0), axis=0, keepdims=True
    )
    top = jnp.max(logits, axis=0, keepdims=True)
    exps = jnp.exp(logits - top)
    norm = jnp.sum(exps, axis=0, keepdims=True)
    logprob = logits - (top + jnp.log(norm))
    probs = exps * (1.0 / norm)
    onehot = iota(logits.shape, 0) == action
    taken = jnp.sum(jnp.where(onehot, logprob, 0.0), axis=0, keepdims=True)
    entropy = -jnp.sum(probs * logprob, axis=0, keepdims=True)
    step = lax.rem(iota((1, rows), 1), slots)
    inside = (step < length).astype(F32)
    beyond = (step + 1 < length).astype(F32)
    ratios = jnp.minimum(1.0, jnp.exp(taken - behave))

    def later(series, by):
        return pltpu.roll(series, rows - by, 1)

    deltas = inside * ratios * (reward + GAMMA * later(values, 1) * beyond - values)
    decay = GAMMA * ratios * inside
    corrections = deltas
    reach = 1
    while reach < slots:
        within = step + reach < slots
        corrections = corrections + decay * jnp.where(within, later(corrections, reach), 0.0)
        decay = decay * jnp.where(within, later(decay, reach), 0.0)
        reach *= 2
    targets = values + corrections
    advantage = ratios * (reward + GAMMA * later(targets, 1) * beyond - values)
    scale = weight * inside
    grad = scale * (
        -advantage * (onehot.astype(F32) - probs) + ENTROPY_COEF * probs * (logprob + entropy)
    )
    return grad, scale * (values - targets)


def forward(frames, embed_t, head_t, frames_t, hidden_t):
    width = embed_t.shape[0]
    tile = 256
    for index, block in enumerate(frames):
        frames_t[:, index * BLOCK : (index + 1) * BLOCK] = block[...].T
    for start in range(0, width, tile):
        here = slice(start, start + tile)
        hidden_t[here, :] = jnp.maximum(mm(embed_t[here, :], frames_t[...]), 0.0).astype(BF16)
    return mm(head_t[...], hidden_t[...])


def backward(slots, logits, side, weights, head, frames_t, hidden_t, preact_t, add):
    width, feats = head.shape[0], frames_t.shape[0]
    nact = logits.shape[0] - PAD
    tile = 256
    grad, grad_values = vtrace(
        slots, nact, side, weights, logits[0:nact, :], logits[nact : nact + 1, :]
    )
    pad = jnp.zeros((PAD - 1, grad.shape[1]), F32)
    grad_t = jnp.concatenate([grad, grad_values, pad], axis=0).astype(BF16)
    for start in range(0, width, tile):
        here = slice(start, start + tile)
        back = mm(head[here, :], grad_t)
        alive = hidden_t[here, :].astype(F32) > 0.0
        preact_t[here, :] = jnp.where(alive, back, 0.0).astype(BF16)
    for index in range(frames_t.shape[1] // BLOCK):
        lanes = slice(index * BLOCK, (index + 1) * BLOCK)
        add(index, slice(0, feats), mm_nt(frames_t[:, lanes], preact_t[:, lanes]))
        add(index, slice(feats, feats + nact + PAD), mm_nt(grad_t[:, lanes], hidden_t[:, lanes]))


def work(slots, frames, side, weights, embed_t, head, head_t, frames_t, hidden_t, preact_t, add):
    logits = forward(frames, embed_t, head_t, frames_t, hidden_t)
    backward(slots, logits, side, weights, head, frames_t, hidden_t, preact_t, add)


def side_of(sides, back, flip):
    line = lax.div(lax.axis_index("hst"), 2)
    there = lax.bitwise_xor(line, lax.bitwise_and(line + 4 - back, 3))
    return sides[pl.ds(pl.multiple_of(8 * (4 * flip + there), 8), 8), :]


def ahead_kernel(*refs):
    (*frames, embed_t, head_t, frames_t, hidden_t, logits) = refs
    logits[...] = forward(frames, embed_t, head_t, frames_t, hidden_t)


def ahead(frames, embed_t, head_t):
    width, feats = embed_t.shape
    rows = len(frames) * BLOCK
    return pl.pallas_call(
        ahead_kernel,
        out_shape=(
            jax.ShapeDtypeStruct((feats, rows), BF16),
            jax.ShapeDtypeStruct((width, rows), BF16),
            jax.ShapeDtypeStruct((head_t.shape[0], rows), F32),
        ),
        in_specs=[VMEM] * (len(frames) + 2),
        out_specs=(VMEM,) * 3,
        compiler_params=params(20),
        cost_estimate=cost(1.6),
        name="ahead",
    )(*frames, embed_t, head_t)


def first_kernel(slots, *refs):
    (frames_t, hidden_t, logits, *pieces), mats, (sum_0, sum_1, weights, sides), scratch = (
        refs[0:5], refs[5:8], refs[8:12], refs[12:15])
    start = 0
    for piece in pieces:
        sides[start : start + piece.shape[0], :] = piece[...]
        start += piece.shape[0]
    learner_weights(slots, sides, weights)

    def add(index, rows, value):
        if index == 0:
            sum_0[rows, :] = value
        elif index == 1:
            sum_0[rows, :] += value
        else:
            sum_1[rows, :] = value

    side = jnp.concatenate([side_of(sides, *at) for at in ((0, 0), (0, 1), (1, 0))], axis=1)
    backward(slots, logits[...], side, weights, mats[1], frames_t, hidden_t, scratch[2], add)


def second_kernel(slots, *refs):
    frames, (sides, weights, sum_1), mats, (sum_1y, sum_3), scratch = (
        refs[0:2], refs[2:5], refs[5:8], refs[8:10], refs[10:13])

    def add(index, rows, value):
        if index == 0:
            sum_1y[rows, :] = sum_1[rows, :] + value
        else:
            sum_3[rows, :] = value

    side = jnp.concatenate([side_of(sides, 1, 1), side_of(sides, 3, 0)], axis=1)
    work(slots, frames, side, weights, *mats, *scratch, add)


def third_kernel(slots, *refs):
    frames, (sides, weights, sum_1y, sum_3), mats, (odd, sum_2), scratch = (
        refs[0:2], refs[2:6], refs[6:9], refs[9:11], refs[11:14])

    def add(index, rows, value):
        if index == 0:
            odd[rows, :] = sum_1y[rows, :] + (sum_3[rows, :] + value)
        else:
            sum_2[rows, :] = value

    side = jnp.concatenate([side_of(sides, 3, 1), side_of(sides, 2, 0)], axis=1)
    work(slots, frames, side, weights, *mats, *scratch, add)


def fourth_kernel(slots, *refs):
    frames, (sides, weights, odd, sum_0, sum_2), mats, out, scratch = (
        refs[0:1], refs[1:6], refs[6:9], refs[9], refs[10:13])

    def add(index, rows, value):
        out[rows, :] = (
            odd[rows, :] + (sum_0[rows, :] + (sum_2[rows, :] + value))
        ).astype(BF16)

    work(slots, frames, side_of(sides, 2, 1), weights, *mats, *scratch, add)


def local_kernel(slots, frames, side, weights, embed_t, head, head_t, out, *scratch):
    def add(index, rows, value):
        if index == 0:
            out[rows, :] = value
        else:
            out[rows, :] += value

    blocks = [frames.at[index] for index in range(frames.shape[0])]
    work(slots, blocks, side, weights, embed_t, head, head_t, *scratch, add)


def call(kernel, name, slots, blocks, args, mats, outs):
    width, feats = mats[0].shape
    rows = blocks * BLOCK
    return pl.pallas_call(
        functools.partial(kernel, slots),
        out_shape=outs,
        in_specs=[VMEM] * (len(args) + 3),
        out_specs=jax.tree.map(lambda leaf: VMEM, outs),
        scratch_shapes=[
            pltpu.VMEM((feats, rows), BF16),
            pltpu.VMEM((width, rows), BF16),
            pltpu.VMEM((width, rows), BF16),
        ],
        compiler_params=params(32),
        cost_estimate=cost(0.6 * blocks),
        name=name,
    )(*args, *mats)


def update_kernel(
    feats, nact, mine, theirs, master_embed, master_policy, master_value,
    embed_moment, policy_moment, value_moment, next_obs,
    next_logits, new_embed, new_policy, new_value, new_em, new_pm, new_vm,
):
    def step(grad, moment, master, new_moment, new_master):
        held = MOMENTUM * moment[...] + grad
        new_moment[...] = held
        fresh = master[...] - LEARN_RATE * held
        new_master[...] = fresh
        return fresh

    def grad(start, size):
        return mine[start : start + size, :].astype(F32) + theirs[start : start + size, :].astype(F32)

    embed = step(grad(0, feats), embed_moment, master_embed, new_em, new_embed)
    hidden = jnp.maximum(mm(next_obs[...], embed.astype(BF16)), 0.0).astype(BF16)
    policy = step(grad(feats, nact).T, policy_moment, master_policy, new_pm, new_policy)
    step(grad(feats + nact, PAD)[0:1, :], value_moment, master_value, new_vm, new_value)
    next_logits[...] = mm(hidden, policy.astype(BF16)).astype(BF16)


def update(mine, theirs, *args):
    embed, policy, value = args[0], args[1], args[2]
    next_obs = args[6]
    feats, nact = embed.shape[0], policy.shape[1]
    shapes = [jax.ShapeDtypeStruct(array.shape, F32) for array in (embed, policy, value)]
    return pl.pallas_call(
        functools.partial(update_kernel, feats, nact),
        out_shape=(jax.ShapeDtypeStruct((next_obs.shape[0], nact), BF16), *shapes, *shapes),
        in_specs=[VMEM] * 9,
        out_specs=(VMEM,) * 7,
        compiler_params=params(32),
        cost_estimate=cost(3.4),
        name="update",
    )(mine, theirs, *args)


def gathered_grads(slots, own, side, mats):
    def exchange(array, mask, name):
        with jax.named_scope(name):
            return lax.ppermute(array, "hst", [(at, at ^ mask) for at in range(8)])

    def shift(array, by, name):
        with jax.named_scope(name):
            return lax.ppermute(array, "hst", [(at, (at + 2 * by) % 8) for at in range(8)])

    one = shift(own, 1, "one")
    own_y = exchange(own, 1, "own_y")
    pieces = [side] + [exchange(side, 2 * mask, "side_z") for mask in (1, 2, 3)]
    line = jnp.concatenate(pieces, axis=0)
    line, _ = lax.optimization_barrier((line, side))
    again, _ = lax.optimization_barrier((own, side))
    line_y = exchange(line, 1, "side_y")
    three = shift(again, -1, "three")
    one_y = exchange(one, 1, "one_y")
    two = shift(one, 1, "two")
    three_y = exchange(three, 1, "three_y")

    width, feats = mats[0].shape
    grads = jax.ShapeDtypeStruct((feats + mats[2].shape[0], width), F32)
    weights = jax.ShapeDtypeStruct((16, 128), F32)
    sides = jax.ShapeDtypeStruct((64, side.shape[1]), F32)
    done = ahead((own, own_y, one), mats[0], mats[2])
    sum_0, sum_1, weights, sides = call(
        first_kernel, "first", slots, 3, (*done, line, line_y), mats,
        (grads, grads, weights, sides),
    )
    sum_1y, sum_3 = call(
        second_kernel, "second", slots, 2, (one_y, three, sides, weights, sum_1), mats,
        (grads, grads),
    )
    two, sum_3 = lax.optimization_barrier((two, sum_3))
    two_y = exchange(two, 1, "two_y")
    odd, sum_2 = call(
        third_kernel, "third", slots, 2, (three_y, two, sides, weights, sum_1y, sum_3), mats,
        (grads, grads),
    )
    return call(
        fourth_kernel, "fourth", slots, 1, (two_y, sides, weights, odd, sum_0, sum_2), mats,
        jax.ShapeDtypeStruct(grads.shape, BF16),
    )


def body(
    n_hst, n_cores, observations, lengths, actions, rewards, assign, actor_embed, actor_policy,
    master_embed, master_policy, master_value, embed_moment, policy_moment, value_moment, next_obs,
):
    traj, slots, feats = observations.shape
    learners = n_hst * n_cores
    rows = traj * slots
    own = observations.reshape(rows, feats)
    value_row = master_value.reshape(1, -1)
    spread, owner = select(traj, slots)
    flip = [(core, core ^ 1) for core in range(n_cores)]
    there = [lax.ppermute(array, "cores", flip) for array in (lengths, assign)]
    gather = n_hst == 8 and n_cores == 2 and rows == BLOCK
    side = side_data(
        spread, owner, own, *[array.reshape(1, -1) for array in (lengths, assign, *there)],
        actions, rewards, actor_embed, actor_policy,
    )
    late_row, _ = lax.optimization_barrier((value_row, side))
    mats = convert(master_embed, master_policy, late_row)
    if gather:
        mine = gathered_grads(slots, own, side, mats)
        theirs = lax.ppermute(mine, "cores", flip)
    else:
        named = (assign[:, None] == jnp.arange(learners)[None, :]).astype(F32)
        totals = lax.psum(jnp.sum(named * lengths[:, None].astype(F32), axis=0), AXES)
        weights = jnp.broadcast_to((1.0 / (learners * totals))[:, None], (learners, 128))
        grads = call(
            local_kernel, "local", slots, rows // BLOCK,
            (own.reshape(-1, BLOCK, feats), side, weights), mats,
            jax.ShapeDtypeStruct((feats + mats[2].shape[0], mats[0].shape[0]), F32),
        )
        mine = lax.psum(grads, AXES)
        theirs = jnp.zeros_like(mine)
    outs = update(
        mine, theirs, master_embed, master_policy, value_row, embed_moment, policy_moment,
        value_moment.reshape(1, -1), next_obs,
    )
    logits, new_embed, new_policy, new_value, new_em, new_pm, new_vm = outs
    return logits, new_embed, new_policy, new_value.reshape(-1), new_em, new_pm, new_vm.reshape(-1)


def solution(mesh):
    split = P(("group", "hst", "cores"))
    whole = P("group")
    return jax.shard_map(
        functools.partial(body, mesh.shape["hst"], mesh.shape["cores"]),
        mesh=mesh,
        in_specs=(split,) * 5 + (whole,) * 8 + (split,),
        out_specs=(split,) + (whole,) * 6,
        check_vma=False,
    )
```
